32 devices in a mesh: shard: 4 (over x, core), rep: 8 (over z, y).
Axes of the slice: x: 2, y: 2, z: 4, core: 2. Of those that a mesh axis runs over, the one named last changes fastest.
Arguments:
- tokens: bfloat16 [25216, 384], P(('shard', 'rep')), may hold values from -6 to 6
- routes: int32 [25216, 2], P(('shard', 'rep')), may hold values from 0 to 7, all different within a row; in each aligned block of 788 rows (0 to 787, 788 to 1575, ...) at most 264 rows name the same one
- cotangent: bfloat16 [25216, 384], P(('shard', 'rep')), may hold values from -6 to 6
- attn_weights: float32 [4, 384, 384], P(None, 'shard'), may hold values from -0.4375 to 0.4375
- attn_first: float32 [4, 384, 384], P(None, 'shard'), may hold values from -56 to 56
- attn_second: float32 [4, 384, 384], P(None, 'shard'), may hold values from 3.152 to 50.432
- router_weights: float32 [384, 8], P('shard'), may hold values from -0.3125 to 0.3125
- router_first: float32 [384, 8], P('shard'), may hold values from -40 to 40
- router_second: float32 [384, 8], P('shard'), may hold values from 1.576 to 25.216
- norm_params: float32 [4, 384], P(None, 'shard'), may hold values from -0.5 to 1.5, as said below
- norm_first: float32 [4, 384], P(None, 'shard'), may hold values from -112 to 112
- norm_second: float32 [4, 384], P(None, 'shard'), may hold values from 12.608 to 201.728
- expert_weights: float32 [8, 2, 1536, 384], P('shard', None, 'rep'), may hold values from -0.3125 to 0.3125
- expert_first: float32 [8, 2, 1536, 384], P('shard', None, 'rep'), may hold values from -16 to 16
- expert_second: float32 [8, 2, 1536, 384], P('shard', None, 'rep'), may hold values from 0.315 to 5.04
Outputs:
- output: bfloat16 [25216, 384], P(('shard', 'rep'))
- input_grad: float32 [25216, 384], P(('shard', 'rep'))
- attn_grad: float32 [4, 384, 384], P(None, 'shard')
- attn_first_new: float32 [4, 384, 384], P(None, 'shard')
- attn_second_new: float32 [4, 384, 384], P(None, 'shard')
- attn_new: float32 [4, 384, 384], P(None, 'shard')
- router_grad: float32 [384, 8], P('shard')
- router_first_new: float32 [384, 8], P('shard')
- router_second_new: float32 [384, 8], P('shard')
- router_new: float32 [384, 8], P('shard')
- norm_grad: float32 [4, 384], P(None, 'shard')
- norm_first_new: float32 [4, 384], P(None, 'shard')
- norm_second_new: float32 [4, 384], P(None, 'shard')
- norm_new: float32 [4, 384], P(None, 'shard')
- expert_grad: float32 [8, 2, 1536, 384], P('shard', None, 'rep')
- expert_first_new: float32 [8, 2, 1536, 384], P('shard', None, 'rep')
- expert_second_new: float32 [8, 2, 1536, 384], P('shard', None, 'rep')
- expert_new: float32 [8, 2, 1536, 384], P('shard', None, 'rep')
The draws below stay inside these ranges and needn't reach their ends.
Inputs may be any that keep to these rules, and one draw needn't show every extreme that they name: `routes`: a token's two experts differ; among the rows of one device no expert is named more than 264 times. `norm_params`: rows 0 and 2 are the norms' gains, rows 1 and 3 their shifts.
All inputs are finite; a program needn't handle non-finite values.
Results may differ from the reference program's by a relative error of at most 0.029.
Values may be sent and summed in bfloat16 or wider, within the bound.
No kernel may reach another device: no remote copies, remote signals or barrier semaphores. Data moves between devices by JAX's collectives and lax.ppermute only.
A program may use at most 128 MiB of HBM per device.

```python
import math
import jax
import jax.numpy as jnp
import numpy as np
from jax import lax

D = 384
HEADS = 6
HEAD_DIM = 64
FF = 1536
SEQ = 197
IMG_DEV = 4
STEP = 10
TOK_DEV = 788
TOKENS = 25216
EXPERTS = 8
CAP = 264
DEVICES = 32


def draw_norm_params(key, part):
    key = jax.random.fold_in(key, 11)
    gain_key, shift_key = jax.random.split(key)
    gains = jax.random.uniform(gain_key, (2, D), jnp.float32, 0.5, 1.5)
    shifts = jnp.clip(0.1 * jax.random.normal(shift_key, (2, D), jnp.float32), -0.5, 0.5)
    return jnp.stack([gains[0], shifts[0], gains[1], shifts[1]], axis=0)


def shard_levels(rng, dims, shards, low, largest):
    def one(axis_at, shards_of):
        draws = jax.random.uniform(jax.random.fold_in(jax.random.fold_in(rng, 6), axis_at), (shards_of,), jnp.float32, low / len(shards), largest / len(shards))
        return jnp.repeat(jnp.exp(draws), dims[axis_at] // shards_of).reshape((-1,) + (1,) * (len(dims) - axis_at - 1))

    loudness = one(*shards[0])
    for cut in shards[1:]:
        loudness = loudness * one(*cut)
    return loudness


def deal_out(stream_key, own, number, rows, count, top, reach, lean):
    ranking = jax.random.permutation(stream_key, count)
    packed, usual = load_shares(count, rows * top, reach, lean, True), load_shares(count, rows * top, reach, lean, False)
    places = jnp.arange(count)

    def named(lengths, turn):
        used = int((lengths > 0).sum())
        fixed = max(1, used // 4)
        passed = fixed + (places - fixed + turn * (used - fixed)) % max(1, count - fixed)
        return jnp.zeros((count,), jnp.int32).at[ranking[jnp.where(places < fixed, places, passed)]].set(jnp.asarray(lengths, jnp.int32))

    lengths = jnp.where(number % 4 == 0, named(packed, number // 4), named(usual, number - number // 4 - 1))
    mixed = jax.random.permutation(jax.random.fold_in(own, 3), count)
    source_of, sink = mixed[0:count // 2 * 2:2], mixed[1:count // 2 * 2:2]
    room = jnp.minimum(lengths[source_of] - 1, reach - lengths[sink]) // 2
    room = jnp.where((source_of == ranking[0]) | (sink == ranking[0]) | (lengths[sink] == 0), 0, jnp.maximum(room, 0))
    passed = jax.random.randint(jax.random.fold_in(own, 4), (count // 2,), 0, 1 << 20) % (room + 1)
    lengths = lengths.at[source_of].add(-passed).at[sink].add(passed)
    items = jnp.searchsorted(jnp.cumsum(lengths), jnp.arange(rows * top), side="right").astype(jnp.int32)
    listing = items.reshape(top, rows).T
    listing = listing[jax.random.permutation(jax.random.fold_in(own, 1), rows)]
    turn = jax.random.randint(jax.random.fold_in(own, 2), (rows, 1), 0, top)
    return jnp.take_along_axis(listing, (jnp.arange(top)[None, :] + turn) % top, axis=1)


def load_shares(amount, total, bound, skew, full):
    weights = [(1 << 20) // math.isqrt(standing ** skew) + 1 for standing in range(1, amount + 1)]
    largest = bound if full else min(bound, max(-(-total // amount), total * weights[0] // sum(weights)))
    least = 1 if total - largest >= amount - 1 else 0
    given, spare = [largest] + [least] * (amount - 1), total - largest - least * (amount - 1)
    while spare > 0:
        movable = [i for i in range(1, amount) if given[i] < largest] or [i for i in range(1, amount) if given[i] < bound]
        pool, budget = sum([weights[i] for i in movable]), spare
        for i in movable:
            addition = min(bound - given[i], max(1, budget * weights[i] // pool), spare)
            given[i] = given[i] + addition
            spare = spare - addition
    return np.array(given)


def noise(rng, shape, spread, reach, cuts=(), kind=jnp.bfloat16):
    values = jax.random.normal(rng, shape, jnp.float32) * spread
    if len(cuts) > 0:
        values = shard_levels(rng, shape, cuts, -0.22, 0.18) * values
    return jnp.clip(values, min=-reach, max=reach).astype(kind)


def setup_inputs(seed: int = 0) -> dict:
    arg_keys = jax.random.split(jax.random.key(seed), 16)
    tokens = noise(arg_keys[0], (TOKENS, D), 1.0, 6.0, ((0, 32),))
    routes_keys = jax.random.split(jax.random.fold_in(arg_keys[1], 1), TOKENS // TOK_DEV)
    routes_turns = jax.random.permutation(jax.random.fold_in(arg_keys[1], 3), TOKENS // TOK_DEV)
    routes = jax.vmap(lambda own, number: deal_out(jax.random.fold_in(arg_keys[1], 2), own, number, TOK_DEV, EXPERTS, 2, CAP, 1))(routes_keys, routes_turns).reshape((TOKENS, 2))
    cotangent = noise(arg_keys[2], (TOKENS, D), 1.0, 6.0, ((0, 32),))
    attn_weights = noise(arg_keys[3], (4, D, D), (D // 2) ** -0.5, 0.4375, ((1, 4),), jnp.float32)
    attn_first = noise(arg_keys[4], (4, D, D), (0.055 * TOKENS ** 0.5), 56.0, ((1, 4),), jnp.float32)
    attn_second = jnp.clip(jnp.exp(math.log(50.432) - 2.7725887 * jax.random.uniform(arg_keys[5], (4, D, D), jnp.float32) ** shard_levels(arg_keys[5], (4, D, D), ((1, 4),), -0.2, 0.2)), 3.152, 50.432)
    router_weights = noise(arg_keys[6], (D, EXPERTS), D ** -0.5, 0.3125, ((0, 4),), jnp.float32)
    router_first = noise(arg_keys[7], (D, EXPERTS), (0.039 * TOKENS ** 0.5), 40.0, ((0, 4),), jnp.float32)
    router_second = jnp.clip(jnp.exp(math.log(25.216) - 2.7725887 * jax.random.uniform(arg_keys[8], (D, EXPERTS), jnp.float32) ** shard_levels(arg_keys[8], (D, EXPERTS), ((0, 4),), -0.2, 0.2)), 1.576, 25.216)
    norm_params = draw_norm_params(jax.random.fold_in(arg_keys[15], 71), 0)
    norm_first = noise(arg_keys[10], (4, D), (0.11 * TOKENS ** 0.5), 112.0, ((1, 4),), jnp.float32)
    norm_second = jnp.clip(jnp.exp(math.log(201.728) - 2.7725887 * jax.random.uniform(arg_keys[11], (4, D), jnp.float32) ** shard_levels(arg_keys[11], (4, D), ((1, 4),), -0.2, 0.2)), 12.608, 201.728)
    expert_weights = noise(arg_keys[12], (EXPERTS, 2, FF, D), D ** -0.5, 0.3125, ((0, 4), (2, 8)), jnp.float32)
    expert_first = noise(arg_keys[13], (EXPERTS, 2, FF, D), (0.11 * (TOKENS // (5 * EXPERTS)) ** 0.5), 16.0, ((0, 4), (2, 8)), jnp.float32)
    expert_second = jnp.clip(jnp.exp(math.log(5.04) - 2.7725887 * jax.random.uniform(arg_keys[14], (EXPERTS, 2, FF, D), jnp.float32) ** shard_levels(arg_keys[14], (EXPERTS, 2, FF, D), ((0, 4), (2, 8)), -0.2, 0.2)), 0.315, 5.04)
    return dict(tokens=tokens, routes=routes, cotangent=cotangent, attn_weights=attn_weights, attn_first=attn_first, attn_second=attn_second, router_weights=router_weights, router_first=router_first, router_second=router_second, norm_params=norm_params, norm_first=norm_first, norm_second=norm_second, expert_weights=expert_weights, expert_first=expert_first, expert_second=expert_second)


@jax.custom_vjp
def low(v):
    return lax.optimization_barrier(v.astype(jnp.bfloat16)).astype(jnp.float32)

@jax.custom_vjp
def low_back(v):
    return v

def low_keep(v):
    return (low(v), None)

def low_pass(kept, grad):
    return (grad,)

def back_keep(v):
    return (v, None)

def back_low(kept, grad):
    return (low(grad),)
low.defvjp(low_keep, low_pass)
low_back.defvjp(back_keep, back_low)
beta_one = 0.9
beta_two = 0.999
adam_floor = 1e-08
decay_rate = 0.1
rate_matrix = 0.05
rate_vector = 0.3
norm_floor = 1e-06

def layer_norm(values, gain_row, shift_row):
    centred = values - lax.optimization_barrier(jnp.mean(values, axis=-1, keepdims=True))
    variance = lax.optimization_barrier(jnp.mean(centred * centred, axis=-1, keepdims=True))
    return centred * lax.rsqrt(variance + norm_floor) * gain_row + shift_row

def matmul(left, right):
    return jnp.dot(left, right, precision=lax.Precision.HIGHEST, preferred_element_type=jnp.float32)

def slot_positions(chosen, experts, capacity):
    flat_routes = jnp.concatenate([chosen[:, 0], chosen[:, 1]]).astype(jnp.int32)
    onehot = (flat_routes[:, None] == jnp.arange(experts, dtype=jnp.int32)[None, :]).astype(jnp.int32)
    earlier = jnp.cumsum(onehot, axis=0).astype(jnp.int32) - onehot
    return (flat_routes * capacity + lax.optimization_barrier(jnp.sum(earlier * onehot, axis=1))).astype(jnp.int32)

def adamw(weight, first, second, grad, rate, decay):
    first_new = beta_one * first + (1.0 - beta_one) * grad
    second_new = beta_two * second + (1.0 - beta_two) * grad * grad
    first_hat = first_new / (1.0 - beta_one ** STEP)
    second_hat = second_new / (1.0 - beta_two ** STEP)
    return (first_new, second_new, weight - rate * (first_hat / (jnp.sqrt(second_hat) + adam_floor) + decay * weight))

def reference(tokens, routes, cotangent, attn_weights, attn_first, attn_second, router_weights, router_first, router_second, norm_params, norm_first, norm_second, expert_weights, expert_first, expert_second):
    scale = HEAD_DIM ** (-0.5)
    highest = lax.Precision.HIGHEST

    def forward(attn_w, router_w, norm_w, expert_w, inputs):
        attn_b = low(attn_w)
        router_b = low(router_w)
        norm_b = low(norm_w)
        expert_b = low(expert_w)

        def block(pair):
            rows, chosen = pair
            attn_in = low(layer_norm(rows, norm_b[0], norm_b[1]))
            query = low(low_back(matmul(attn_in, attn_b[0]))).reshape(IMG_DEV, SEQ, HEADS, HEAD_DIM)
            keys = low(low_back(matmul(attn_in, attn_b[1]))).reshape(IMG_DEV, SEQ, HEADS, HEAD_DIM)
            values = low(low_back(matmul(attn_in, attn_b[2]))).reshape(IMG_DEV, SEQ, HEADS, HEAD_DIM)
            scores = low_back(scale * jnp.einsum('bqhd,bkhd->bhqk', query, keys, precision=highest))
            probs = low(jax.nn.softmax(scores, axis=-1))
            mixed = jnp.einsum('bhqk,bkhd->bqhd', probs, values, precision=highest).reshape(TOK_DEV, D)
            attended = low(low_back(mixed))
            middle = rows + low_back(matmul(attended, attn_b[3]))
            expert_in = low(layer_norm(middle, norm_b[2], norm_b[3]))
            logits = low_back(matmul(expert_in, router_b))
            iota_row = jnp.arange(EXPERTS, dtype=jnp.int32)[None, :]
            pick_one = (chosen[:, 0:1] == iota_row).astype(jnp.float32)
            pick_two = (chosen[:, 1:2] == iota_row).astype(jnp.float32)
            picked = jnp.stack([lax.optimization_barrier(jnp.sum(logits * pick_one, axis=1)), lax.optimization_barrier(jnp.sum(logits * pick_two, axis=1))], axis=1)
            gates = jax.nn.softmax(picked, axis=1)
            positions = slot_positions(chosen, EXPERTS, CAP)
            sent_rows = jnp.concatenate([low_back(expert_in), low_back(expert_in)], axis=0)
            buffer = jnp.zeros((EXPERTS * CAP, D), jnp.float32).at[positions].set(sent_rows).reshape(EXPERTS, CAP, D)
            pre = low_back(jnp.einsum('ecd,efd->ecf', buffer, expert_b[:, 0], precision=highest))
            hidden = low(jax.nn.gelu(pre))
            expert_out = low(low_back(jnp.einsum('ecf,efd->ecd', hidden, expert_b[:, 1], precision=highest)))
            returned = expert_out.reshape(EXPERTS * CAP, D)[positions]
            return middle + gates[:, 0:1] * returned[:TOK_DEV] + gates[:, 1:2] * returned[TOK_DEV:]
        blocks = lax.map(jax.checkpoint(block), (inputs.reshape(DEVICES, TOK_DEV, D), routes.reshape(DEVICES, TOK_DEV, 2)))
        return blocks.reshape(TOKENS, D)
    primal, pullback = jax.vjp(forward, attn_weights, router_weights, norm_params, expert_weights, tokens.astype(jnp.float32))
    attn_grad, router_grad, norm_grad, expert_grad, input_grad = pullback(cotangent.astype(jnp.float32))
    attn_first_new, attn_second_new, attn_new = adamw(attn_weights, attn_first, attn_second, attn_grad, rate_matrix, decay_rate)
    router_first_new, router_second_new, router_new = adamw(router_weights, router_first, router_second, router_grad, rate_matrix, decay_rate)
    norm_first_new, norm_second_new, norm_new = adamw(norm_params, norm_first, norm_second, norm_grad, rate_vector, 0.0)
    expert_first_new, expert_second_new, expert_new = adamw(expert_weights, expert_first, expert_second, expert_grad, rate_matrix, decay_rate)
    return (primal.astype(jnp.bfloat16), input_grad, attn_grad, attn_first_new, attn_second_new, attn_new, router_grad, router_first_new, router_second_new, router_new, norm_grad, norm_first_new, norm_second_new, norm_new, expert_grad, expert_first_new, expert_second_new, expert_new)
```

```python
import functools

import jax
import jax.numpy as jnp
from jax import lax
from jax.experimental import pallas as pl
from jax.experimental.pallas import tpu as pltpu
from jax.sharding import PartitionSpec as P

HEADS = 6
HEAD_DIM = 64
SEQ = 197
PAD = 208
STEP = 10
GROUP = 2

beta_one = 0.9
beta_two = 0.999
adam_floor = 1e-08
decay_rate = 0.1
rate_matrix = 0.05
rate_vector = 0.3
norm_floor = 1e-06

bf16 = jnp.bfloat16
f32 = jnp.float32
VMEM = pltpu.VMEM
ANY = pl.BlockSpec(memory_space=pl.ANY)
WHOLE = pl.BlockSpec(memory_space=pltpu.VMEM)
SCALAR = pl.BlockSpec(memory_space=pltpu.SMEM)
MIB = 1 << 20


def sds(shape, dtype):
    return jax.ShapeDtypeStruct(shape, dtype)


def nn(left, right):
    return lax.dot_general(left, right, (((1,), (0,)), ((), ())), preferred_element_type=f32)


def nt(left, right):
    return lax.dot_general(left, right, (((1,), (1,)), ((), ())), preferred_element_type=f32)


def iota(shape, dim):
    return lax.broadcasted_iota(jnp.int32, shape, dim)


def normalize(values):
    centred = values - jnp.mean(values, axis=-1, keepdims=True)
    inverse = lax.rsqrt(jnp.mean(centred * centred, axis=-1, keepdims=True) + norm_floor)
    return centred * inverse, inverse


def norm_back(grad_rows, normed, inverse, gain):
    scaled = grad_rows * gain
    inner = (
        scaled
        - jnp.mean(scaled, axis=-1, keepdims=True)
        - normed * jnp.mean(scaled * normed, axis=-1, keepdims=True)
    )
    return inner * inverse


def eight_rows(values):
    rows, cols = values.shape
    return jnp.sum(values.reshape(rows // 8, 8, cols), axis=0)


def adamw(weight, first, second, grad, rate, decay):
    first_new = beta_one * first + (1.0 - beta_one) * grad
    second_new = beta_two * second + (1.0 - beta_two) * grad * grad
    first_hat = first_new * (1.0 / (1.0 - beta_one**STEP))
    second_hat = second_new * (1.0 / (1.0 - beta_two**STEP))
    return (
        first_new,
        second_new,
        weight - rate * (first_hat / (jnp.sqrt(second_hat) + adam_floor) + decay * weight),
    )


def pack_kernel(attn, router, norm, expert, packed, *experts):
    width = attn.shape[2]
    for index in range(4):
        packed[:, index * width : (index + 1) * width] = attn[index].astype(bf16)
    rows, count = router.shape
    filler = jnp.zeros((128 - count - 4, rows), f32)
    block = jnp.concatenate([router[...].T, norm[...], filler], axis=0)
    packed[:, 4 * width :] = block.T.astype(bf16)
    for index, out in enumerate(experts):
        out[...] = expert[index].astype(bf16)


def pack(attn, router, norm, expert):
    _, rows, width = attn.shape
    local, _, hidden, _ = expert.shape
    return pl.pallas_call(
        pack_kernel,
        out_shape=[sds((rows, 4 * width + 128), bf16)]
        + [sds((2, hidden, width), bf16) for _ in range(local)],
        in_specs=[WHOLE] * 4,
        out_specs=[WHOLE] * (1 + local),
        name="pack",
    )(attn, router, norm, expert)


def routes_kernel(experts, local, group, stride, me_ref, routes_ref, pos_ref, meta_ref):
    images = routes_ref.shape[0]
    rows = images * PAD
    routes = routes_ref[...].reshape(rows, 2).astype(f32)
    one, two = routes[:, 0:1], routes[:, 1:2]
    lane = iota((rows, 128), 1).astype(f32)
    pick_one, pick_two = lane == one, lane == two
    mask = jnp.where(pick_one | pick_two, 1.0, 0.0).astype(bf16)
    lower = jnp.where(iota((rows, rows), 0) >= iota((rows, rows), 1), 1.0, 0.0).astype(bf16)
    count = nn(lower, mask)
    ranks = [
        jnp.sum(jnp.where(pick, count, 0.0), axis=1, keepdims=True) - 1.0
        for pick in (pick_one, pick_two)
    ]
    me = me_ref[0]
    places = []
    for route, rank in zip((one, two), ranks):
        owner = jnp.floor(route * (1.0 / local))
        inner = route - owner * local
        other = jnp.bitwise_xor(owner.astype(jnp.int32), me).astype(f32)
        place = (inner * group + other) * stride + rank
        places.append(jnp.where(route < 0.0, -1.0, place))
    pos = jnp.where(lane == 0.0, places[0], jnp.where(lane == 1.0, places[1], 0.0))
    pos = jnp.where(lane == 2.0, one, jnp.where(lane == 3.0, two, pos))
    pos_ref[...] = pos.reshape(images, PAD, 128)
    table = jnp.where(lane == 2.0, one, jnp.where(lane == 3.0, two, 0.0))
    for at, rank in enumerate(ranks):
        high = jnp.floor(rank * (1.0 / 16.0))
        table = jnp.where(lane == 4.0 + 2 * at, high, table)
        table = jnp.where(lane == 5.0 + 2 * at, rank - 16.0 * high, table)
    for image in range(images):
        turned = table[image * PAD : (image + 1) * PAD].T
        meta_ref[image] = jnp.concatenate(
            [turned[:8], jnp.zeros((8, 256 - PAD), f32)], axis=1
        )


def route_tables(me, routes, experts, local, group, stride):
    images = routes.shape[0]
    return pl.pallas_call(
        functools.partial(routes_kernel, experts, local, group, stride),
        out_shape=[sds((images, PAD, 128), f32), sds((images, 8, 256), f32)],
        in_specs=[SCALAR, WHOLE],
        out_specs=[WHOLE, WHOLE],
        name="routes",
    )(me, routes)


def load_weights(me, pieces, weights, turned, sem):
    rows = pieces[0].shape[0]
    copies = []
    for index, piece in enumerate(pieces):
        start = pl.multiple_of(jnp.bitwise_xor(me, index) * rows, 16)
        copies.append(pltpu.make_async_copy(piece, weights.at[pl.ds(start, rows)], sem.at[index]))
    for copy in copies:
        copy.start()
    for copy in copies:
        copy.wait()
    width = weights.shape[0]
    turned[...] = weights[:, 4 * width :].astype(f32).T


def front_kernel(experts, group, *refs):
    me_ref, x_ref, meta_ref = refs[:3]
    pieces = refs[3 : 3 + group]
    sent_ref, mid_ref, qkv_ref, probs_ref, turned_ref, gate_ref, weights, table, sem = refs[
        3 + group :
    ]
    width = weights.shape[0]

    @pl.when(pl.program_id(0) == 0)
    def _():
        load_weights(me_ref[0], pieces, weights, table, sem)

    inputs = x_ref[0].astype(f32)
    normed, _ = normalize(inputs)
    gains = table[experts : experts + 4]
    rows_in = (normed * gains[0:1] + gains[1:2]).astype(bf16)
    qkv = nn(rows_in, weights[:, : 3 * width]).astype(bf16)
    qkv_ref[0] = qkv
    half = iota((PAD, 128), 1) < HEAD_DIM
    real = iota((PAD, PAD), 0) < SEQ
    scale = HEAD_DIM ** (-0.5)
    joined = []
    for pair in range(HEADS // 2):
        at = pair * 128
        query = qkv[:, at : at + 128]
        keys = qkv[:, width + at : width + at + 128]
        values = qkv[:, 2 * width + at : 2 * width + at + 128].astype(f32).T.astype(bf16)
        parts = []
        for head in range(2):
            own = jnp.where(half if head == 0 else ~half, keys, jnp.zeros_like(keys))
            scores = jnp.where(real, nt(own, query) * scale, -1e30)
            expd = jnp.exp(scores - jnp.max(scores, axis=0, keepdims=True))
            probs = (expd * (1.0 / jnp.sum(expd, axis=0, keepdims=True))).astype(bf16)
            probs_ref[0, 2 * pair + head] = probs
            parts.append(nn(values[head * HEAD_DIM : (head + 1) * HEAD_DIM], probs))
        both = jnp.concatenate(parts, axis=0)
        turned_ref[0, at : at + 128, :] = both.astype(bf16)
        joined.append(both.T.astype(bf16))
    attended = jnp.concatenate(joined, axis=1)
    middle = inputs + nn(attended, weights[:, 3 * width : 4 * width])
    mid_ref[0] = middle
    normed_two, _ = normalize(middle)
    expert_in = (normed_two * gains[2:3] + gains[3:4]).astype(bf16)
    logits = nt(table[:16].astype(bf16), expert_in)
    meta = meta_ref[0][:, :PAD]
    row = iota((16, PAD), 0).astype(f32)
    picked = [
        jnp.sum(jnp.where(row == meta[2 + j : 3 + j], logits, 0.0), axis=0, keepdims=True)
        for j in range(2)
    ]
    top = jnp.maximum(picked[0], picked[1])
    exps = [jnp.exp(value - top) for value in picked]
    total = exps[0] + exps[1]
    row8 = iota((8, PAD), 0)
    gates = jnp.where(row8 == 0, exps[0] / total, jnp.where(row8 == 1, exps[1] / total, 0.0))
    gate_ref[0] = jnp.concatenate([gates, jnp.zeros((120, PAD), f32)], axis=0).T
    gap = picked[0] - picked[1]
    high = gap.astype(bf16).astype(f32)
    meta = jnp.where(row8 == 0, high, jnp.where(row8 == 1, gap - high, meta))
    meta = jnp.concatenate([meta, jnp.zeros((8, width - PAD), f32)], axis=1)
    sent_ref[0] = jnp.concatenate([expert_in.astype(f32)[: PAD - 8], meta], axis=0).astype(bf16)


def front(me, x, meta, pieces, experts, start, count):
    width = x.shape[2]
    group = len(pieces)
    columns = pieces[0].shape[1]

    def take(*tail):
        return pl.BlockSpec((1,) + tail, lambda i: (i + start,) + (0,) * len(tail))

    def give(*tail):
        return pl.BlockSpec((1,) + tail, lambda i: (i,) + (0,) * len(tail))

    return pl.pallas_call(
        functools.partial(front_kernel, experts, group),
        grid=(count,),
        out_shape=[
            sds((count, PAD, width), bf16),
            sds((count, PAD, width), f32),
            sds((count, PAD, 3 * width), bf16),
            sds((count, HEADS, PAD, PAD), bf16),
            sds((count, width, PAD), bf16),
            sds((count, PAD, 128), f32),
        ],
        in_specs=[SCALAR, take(PAD, width), take(8, 256)] + [ANY] * group,
        out_specs=[
            give(PAD, width),
            give(PAD, width),
            give(PAD, 3 * width),
            give(HEADS, PAD, PAD),
            give(width, PAD),
            give(PAD, 128),
        ],
        scratch_shapes=[
            VMEM((width, columns), bf16),
            VMEM((128, width), f32),
            pltpu.SemaphoreType.DMA((group,)),
        ],
        compiler_params=pltpu.CompilerParams(vmem_limit_bytes=40 * MIB),
        cost_estimate=pl.CostEstimate(
            flops=count * 500_000_000, bytes_accessed=count * 2_500_000, transcendentals=0
        ),
        name="front",
    )(me, x, meta, *pieces)


def expert_kernel(index, local, group, chunks, ring, stride, merged, *refs):
    refs = list(refs)
    me_ref = refs.pop(0)
    tokens = [[refs.pop(0) for _ in range(chunks)] for _ in range(group)]
    grads = [refs.pop(0) for _ in range(group)]
    shards = [refs.pop(0) for _ in range(ring)]
    if merged:
        both = [refs.pop(0) for _ in range(group)]
        back_out = [ref.at[0] for ref in both]
        out_out = [ref.at[1] for ref in both]
    else:
        back_out = [refs.pop(0) for _ in range(group)]
        out_out = [refs.pop(0) for _ in range(group)]
    grad_out = [refs.pop(0) for _ in range(ring)]
    (tok, cot, first, second, first_t, second_t, rows, outs, acc, back_acc, moment, grad_a, grad_b) = refs[:13]
    tok_sem, cot_sem, weight_sem, out_sem = refs[13:]
    width = tok.shape[2]
    per = tok.shape[1] // chunks
    images = tok.shape[1] // PAD
    hidden = shards[0].shape[1]
    slots = group * stride

    token_copies = [
        [
            pltpu.make_async_copy(
                tokens[k][i], tok.at[k, pl.ds(i * per, per)], tok_sem.at[k, i]
            )
            for i in range(chunks)
        ]
        for k in range(group)
    ]
    grad_copies = [pltpu.make_async_copy(grads[k], cot.at[k], cot_sem.at[k]) for k in range(group)]
    weight_copies = []
    for r in range(ring):
        for m, target in enumerate((first, second)):
            weight_copies.append(
                pltpu.make_async_copy(
                    shards[r].at[m], target.at[pl.ds(r * hidden, hidden)], weight_sem.at[r, m]
                )
            )
    for k in range(group):
        for copy in token_copies[k]:
            copy.start()
        grad_copies[k].start()
    for copy in weight_copies:
        copy.start()

    expert = (me_ref[0] * local + index).astype(f32)
    slot = iota((stride, PAD), 0).astype(f32)
    for k in range(group):
        for copy in token_copies[k]:
            copy.wait()
        grad_copies[k].wait()
        rows_sum = jnp.zeros((stride, width), f32)
        grad_sum = jnp.zeros((stride, width), f32)
        gate_sum = jnp.zeros((stride, PAD), f32)
        for image in range(images):
            block = tok[k, image * PAD : (image + 1) * PAD, :]
            meta = block[PAD - 16 :].astype(f32)[8:, :PAD]
            gap = meta[0:1] + meta[1:2]
            top = jnp.maximum(gap, 0.0)
            left, right = jnp.exp(gap - top), jnp.exp(-top)
            is_one = meta[2:3] == expert
            is_two = meta[3:4] == expert
            gate = jnp.where(is_one, left, right) / (left + right)
            place = jnp.where(
                is_one,
                16.0 * meta[4:5] + meta[5:6],
                jnp.where(is_two, 16.0 * meta[6:7] + meta[7:8], -1.0),
            )
            match = slot == place
            pick = jnp.where(match, 1.0, 0.0).astype(bf16)
            rows_sum += nn(pick, block)
            grad_sum += nn(pick, cot[k, image * PAD : (image + 1) * PAD, :])
            gate_sum += jnp.where(match, gate, 0.0)
        rows[k * stride : (k + 1) * stride, :] = rows_sum.astype(bf16)
        scaled = grad_sum * jnp.sum(gate_sum, axis=1, keepdims=True)
        outs[k * stride : (k + 1) * stride, :] = scaled.astype(bf16)

    for copy in weight_copies:
        copy.wait()
    step = first_t.shape[2]
    steps = first_t.shape[0]
    for i in range(steps):
        at = i * step
        first_t[i] = first[at : at + step, :].astype(f32).T.astype(bf16)
        second_t[i] = second[at : at + step, :].astype(f32).T.astype(bf16)
    acc[...] = jnp.zeros_like(acc)
    back_acc[...] = jnp.zeros_like(back_acc)
    moment[...] = jnp.zeros_like(moment)

    k0 = 0.7978845608028654
    k1 = 0.044715

    @pl.loop(0, steps)
    def _(i):
        at = pl.multiple_of(i * step, step)
        pre = nt(first[pl.ds(at, step), :], rows[...])
        back = nt(second[pl.ds(at, step), :], outs[...])
        square = pre * pre
        tanh = jnp.tanh(pre * (k0 + (k0 * k1) * square))
        half = 0.5 + 0.5 * tanh
        act = pre * half
        slope = half + (2.0 * act) * (1.0 - half) * (k0 + (3.0 * k0 * k1) * square)
        moment[...] += eight_rows(act * back)
        act = act.astype(bf16)
        down = (back * slope).astype(bf16)
        acc[...] += nn(second_t[i], act)
        back_acc[...] += nn(first_t[i], down)
        grad_a[pl.ds(at, step), :] = nn(down, rows[...]).astype(bf16)
        grad_b[pl.ds(at, step), :] = nn(act, outs[...]).astype(bf16)

    out_copies = []
    for r in range(ring):
        for m, source in enumerate((grad_a, grad_b)):
            out_copies.append(
                pltpu.make_async_copy(
                    source.at[pl.ds(r * hidden, hidden)], grad_out[r].at[m], out_sem.at[r, m]
                )
            )
    for copy in out_copies:
        copy.start()

    total = jnp.sum(moment[...], axis=0, keepdims=True)
    high = total.astype(bf16).astype(f32)
    wide = -(-slots // 128) * 128
    row8 = iota((8, slots), 0)
    table = jnp.where(row8 == 0, high, jnp.where(row8 == 1, total - high, 0.0))
    if wide > slots:
        table = jnp.concatenate([table, jnp.zeros((8, wide - slots), f32)], axis=1)
    made = acc[...].T
    gone = back_acc[...].T
    inside = iota((8, width), 1) < stride - 8
    for k in range(group):
        here = table if k == 0 else pltpu.roll(table, wide - k * stride, 1)
        here = jnp.where(inside, here[:, :width], 0.0)
        part = gone[k * stride : (k + 1) * stride - 8]
        back_out[k][...] = jnp.concatenate([part, here], axis=0).astype(bf16)
        out_out[k][...] = made[k * stride : (k + 1) * stride].astype(bf16)
    for copy in out_copies:
        copy.wait()


def run_expert(index, local, me, tokens, grads, shards, stride, merged):
    group, chunks, ring = len(tokens), len(tokens[0]), len(shards)
    rows, width = grads[0].shape
    hidden = shards[0].shape[1]
    total = ring * hidden
    slots = group * stride
    step = 384 if total % 384 == 0 else 256
    if merged:
        outs = [sds((2, stride, width), bf16)] * group
    else:
        outs = [sds((stride, width), bf16)] * (2 * group)
    return pl.pallas_call(
        functools.partial(expert_kernel, index, local, group, chunks, ring, stride, merged),
        out_shape=outs + [sds((2, hidden, width), bf16)] * ring,
        in_specs=[SCALAR] + [ANY] * (group * chunks + group + ring),
        out_specs=[WHOLE] * len(outs) + [ANY] * ring,
        scratch_shapes=[
            VMEM((group, rows, width), bf16),
            VMEM((group, rows, width), bf16),
            VMEM((total, width), bf16),
            VMEM((total, width), bf16),
            VMEM((total // step, width, step), bf16),
            VMEM((total // step, width, step), bf16),
            VMEM((slots, width), bf16),
            VMEM((slots, width), bf16),
            VMEM((width, slots), f32),
            VMEM((width, slots), f32),
            VMEM((8, slots), f32),
            VMEM((total, width), bf16),
            VMEM((total, width), bf16),
            pltpu.SemaphoreType.DMA((group, chunks)),
            pltpu.SemaphoreType.DMA((group,)),
            pltpu.SemaphoreType.DMA((ring, 2)),
            pltpu.SemaphoreType.DMA((ring, 2)),
        ],
        compiler_params=pltpu.CompilerParams(vmem_limit_bytes=56 * MIB),
        cost_estimate=pl.CostEstimate(
            flops=12 * slots * total * width, bytes_accessed=16_000_000, transcendentals=0
        ),
        name="expert" + str(index),
    )(me, *[c for chunk in tokens for c in chunk], *grads, *shards)


def load_slots(blocks, buffer, sem):
    stride = blocks[0].shape[0]
    return [
        pltpu.make_async_copy(block, buffer.at[pl.ds(i * stride, stride)], sem.at[i])
        for i, block in enumerate(blocks)
    ]


def home_kernel(experts, group, blocks, merged, *refs):
    refs = list(refs)
    me_ref, pos_ref, gate_ref, x_ref, cot_ref, mid_ref, qkv_ref, probs_ref, turned_ref = refs[:9]
    refs = refs[9:]
    pieces = refs[:group]
    slots = [ref.at[0] if merged[i] else ref for i, ref in enumerate(refs[group : group + blocks])]
    (grad_ref, keep_ref, send_ref) = refs[group + blocks : group + blocks + 3]
    (weights, table, buffer, moments, grads, router_acc, norm_acc, sem, slot_sem) = refs[
        group + blocks + 3 :
    ]
    width = weights.shape[0]
    stride = slots[0].shape[0]
    wide = buffer.shape[0]
    step = pl.program_id(0)

    @pl.when(step == 0)
    def _():
        copies = load_slots(slots, buffer, slot_sem)
        for copy in copies:
            copy.start()
        load_weights(me_ref[0], pieces, weights, table, sem)
        grads[...] = jnp.zeros_like(grads)
        router_acc[...] = jnp.zeros_like(router_acc)
        norm_acc[...] = jnp.zeros_like(norm_acc)
        for copy in copies:
            copy.wait()
        total = jnp.zeros((8, wide), f32)
        for i in range(blocks):
            tail = buffer[(i + 1) * stride - 16 : (i + 1) * stride, :].astype(f32)[8:]
            tail = jnp.concatenate([tail, jnp.zeros((8, wide - width), f32)], axis=1)
            total += tail if i == 0 else pltpu.roll(tail, i * stride, 1)
        moments[...] = total

    gains = table[experts : experts + 4]
    pos = pos_ref[0]
    gates = gate_ref[0]
    lane = iota((PAD, wide), 1).astype(f32)
    match_one = lane == pos[:, 0:1]
    match_two = lane == pos[:, 1:2]
    pick = jnp.where(match_one | match_two, 1.0, 0.0).astype(bf16)
    moment = moments[0:1] + moments[1:2]
    moment_one = jnp.sum(jnp.where(match_one, moment, 0.0), axis=1, keepdims=True)
    moment_two = jnp.sum(jnp.where(match_two, moment, 0.0), axis=1, keepdims=True)
    dz = gates[:, 1:2] * moment_one - gates[:, 0:1] * moment_two
    lane = iota((PAD, 128), 1).astype(f32)
    dl = jnp.where(lane == pos[:, 2:3], dz, jnp.where(lane == pos[:, 3:4], -dz, 0.0))
    middle = mid_ref[0]
    normed, inverse = normalize(middle)
    expert_in = (normed * gains[2:3] + gains[3:4]).astype(bf16)
    dc = nn(pick, buffer[...]) + nn(dl.astype(bf16), table[...].astype(bf16))
    router_acc[...] += nn(dl.T.astype(bf16), expert_in)
    norm_acc[2] += eight_rows(dc * normed)
    norm_acc[3] += eight_rows(dc)
    dx1 = cot_ref[0].astype(f32) + norm_back(dc, normed, inverse, gains[2:3])
    low = dx1.astype(bf16)
    turned = turned_ref[0]
    grads[:, 3 * width :] += nn(turned, low)
    out_proj = weights[:, 3 * width : 4 * width]
    d_out = nt(low, out_proj).astype(bf16)
    d_out_t = nt(out_proj, low).astype(bf16)
    shared = d_out_t.astype(f32) * turned.astype(f32)

    qkv = qkv_ref[0]
    scale = HEAD_DIM ** (-0.5)
    half = iota((PAD, 128), 1) < HEAD_DIM
    dq, dk, dv = [], [], []
    for pair in range(HEADS // 2):
        at = pair * 128
        query = qkv[:, at : at + 128]
        keys = qkv[:, width + at : width + at + 128]
        values = qkv[:, 2 * width + at : 2 * width + at + 128]
        keys_t = keys.astype(f32).T.astype(bf16)
        do = d_out[:, at : at + 128]
        do_t = d_out_t[at : at + 128]
        zero = jnp.zeros_like(query)
        dq_t = []
        dk_sum = jnp.zeros((PAD, 128), f32)
        dv_sum = jnp.zeros((PAD, 128), f32)
        for head in range(2):
            mask = half if head == 0 else ~half
            low_at = at + head * HEAD_DIM
            probs = probs_ref[0, 2 * pair + head]
            dp = nn(jnp.where(mask, values, zero), do_t)
            center = jnp.sum(shared[low_at : low_at + HEAD_DIM], axis=0, keepdims=True)
            ds = (probs.astype(f32) * (dp - center)).astype(bf16)
            dk_sum += nn(ds, jnp.where(mask, query, zero))
            dv_sum += nn(probs, jnp.where(mask, do, zero))
            dq_t.append(nn(keys_t[head * HEAD_DIM : (head + 1) * HEAD_DIM], ds))
        dq.append((jnp.concatenate(dq_t, axis=0).T * scale).astype(bf16))
        dk.append((dk_sum * scale).astype(bf16))
        dv.append(dv_sum.astype(bf16))
    dqkv = jnp.concatenate(dq + dk + dv, axis=1)
    inputs = x_ref[0].astype(f32)
    normed_one, inverse_one = normalize(inputs)
    rows_in = normed_one * gains[0:1] + gains[1:2]
    grads[:, : 3 * width] += nn(rows_in.T.astype(bf16), dqkv)
    da = nt(dqkv, weights[:, : 3 * width])
    norm_acc[0] += eight_rows(da * normed_one)
    norm_acc[1] += eight_rows(da)
    grad_ref[0] = dx1 + norm_back(da, normed_one, inverse_one, gains[0:1])

    @pl.when(step == pl.num_programs(0) - 1)
    def _():
        rows = pieces[0].shape[0]
        row = iota((128, width), 0)
        misc = router_acc[...]
        for i in range(4):
            misc = jnp.where(
                row == experts + i, jnp.sum(norm_acc[i], axis=0, keepdims=True), misc
            )
        table[...] = misc
        extra = table[...].T
        weights[:, : 4 * width] = grads[...].astype(bf16)
        weights[:, 4 * width :] = extra.astype(bf16)
        for k in range(group):
            start = pl.multiple_of(jnp.bitwise_xor(me_ref[0], k) * rows, 16)
            target = keep_ref if k % 2 == 0 else send_ref
            target[k // 2] = weights[pl.ds(start, rows), :]


def home(me, pos, gates, x, cot, mid, qkv, probs, turned, pieces, slots, merged, experts):
    group, blocks = len(pieces), len(slots)
    images, _, width = x.shape
    rows, columns = pieces[0].shape
    stride = slots[0].shape[-2]
    wide = blocks * stride

    def take(*tail):
        return pl.BlockSpec((1,) + tail, lambda i: (i,) + (0,) * len(tail))

    half = (group // 2, rows, columns)
    return pl.pallas_call(
        functools.partial(home_kernel, experts, group, blocks, merged),
        grid=(images,),
        out_shape=[sds((images, PAD, width), f32), sds(half, bf16), sds(half, bf16)],
        in_specs=[
            SCALAR,
            take(PAD, 128),
            take(PAD, 128),
            take(PAD, width),
            take(PAD, width),
            take(PAD, width),
            take(PAD, 3 * width),
            take(HEADS, PAD, PAD),
            take(width, PAD),
        ]
        + [ANY] * (group + blocks),
        out_specs=[take(PAD, width), WHOLE, WHOLE],
        scratch_shapes=[
            VMEM((width, columns), bf16),
            VMEM((128, width), f32),
            VMEM((wide, width), bf16),
            VMEM((8, wide), f32),
            VMEM((width, 4 * width), f32),
            VMEM((128, width), f32),
            VMEM((4, 8, width), f32),
            pltpu.SemaphoreType.DMA((group,)),
            pltpu.SemaphoreType.DMA((blocks,)),
        ],
        compiler_params=pltpu.CompilerParams(vmem_limit_bytes=48 * MIB),
        cost_estimate=pl.CostEstimate(
            flops=8_000_000_000, bytes_accessed=20_000_000, transcendentals=0
        ),
        name="home",
    )(me, pos, gates, x, cot, mid, qkv, probs, turned, *pieces, *slots)


def finish_kernel(blocks, merged, *refs):
    pos_ref, gate_ref, mid_ref = refs[:3]
    slots = [ref.at[1] if merged[i] else ref for i, ref in enumerate(refs[3 : 3 + blocks])]
    out_ref, buffer, slot_sem = refs[3 + blocks :]

    @pl.when(pl.program_id(0) == 0)
    def _():
        copies = load_slots(slots, buffer, slot_sem)
        for copy in copies:
            copy.start()
        for copy in copies:
            copy.wait()

    pos, gates = pos_ref[0], gate_ref[0]
    lane = iota((PAD, buffer.shape[0]), 1).astype(f32)
    total = mid_ref[0]
    for j in range(2):
        pick = jnp.where(lane == pos[:, j : j + 1], 1.0, 0.0).astype(bf16)
        total += gates[:, j : j + 1] * nn(pick, buffer[...])
    out_ref[0] = total.astype(bf16)


def finish(pos, gates, mid, slots, merged):
    images, _, width = mid.shape
    blocks = len(slots)
    stride = slots[0].shape[-2]

    def take(*tail):
        return pl.BlockSpec((1,) + tail, lambda i: (i,) + (0,) * len(tail))

    return pl.pallas_call(
        functools.partial(finish_kernel, blocks, merged),
        grid=(images,),
        out_shape=sds((images, PAD, width), bf16),
        in_specs=[take(PAD, 128), take(PAD, 128), take(PAD, width)] + [ANY] * blocks,
        out_specs=take(PAD, width),
        scratch_shapes=[
            VMEM((blocks * stride, width), bf16),
            pltpu.SemaphoreType.DMA((blocks,)),
        ],
        compiler_params=pltpu.CompilerParams(vmem_limit_bytes=32 * MIB),
        cost_estimate=pl.CostEstimate(
            flops=3_000_000_000, bytes_accessed=4_000_000, transcendentals=0
        ),
        name="finish",
    )(pos, gates, mid, *slots)


def dense_kernel(sum_ref, *refs):
    attn, router, norm = refs[:3], refs[3:6], refs[6:9]
    attn_out, router_out, norm_out = refs[9:13], refs[13:17], refs[17:21]
    width = attn[0].shape[2]
    count = router[0].shape[1]
    for index in range(4):
        grad = sum_ref[:, index * width : (index + 1) * width].astype(f32)
        new = adamw(*(ref[index] for ref in attn), grad, rate_matrix, decay_rate)
        for ref, value in zip(attn_out, (grad,) + new):
            ref[index] = value
    extra = sum_ref[:, 4 * width :].astype(f32)
    grad = extra[:, :count]
    new = adamw(*(ref[...] for ref in router), grad, rate_matrix, decay_rate)
    for ref, value in zip(router_out, (grad,) + new):
        ref[...] = value
    grad = extra.T[count : count + 4]
    new = adamw(*(ref[...] for ref in norm), grad, rate_vector, 0.0)
    for ref, value in zip(norm_out, (grad,) + new):
        ref[...] = value


def dense_update(total, attn, router, norm):
    shapes = [sds(group[0].shape, f32) for group in (attn, router, norm) for _ in range(4)]
    return pl.pallas_call(
        dense_kernel,
        out_shape=shapes,
        in_specs=[WHOLE] * 10,
        out_specs=[WHOLE] * 12,
        name="dense_update",
    )(total, *attn, *router, *norm)


def expert_update_kernel(parts, *refs):
    grad = sum(ref[0, 0].astype(f32) for ref in refs[:parts])
    weight, first, second = (ref[0, 0] for ref in refs[parts : parts + 3])
    new = adamw(weight, first, second, grad, rate_matrix, decay_rate)
    for ref, value in zip(refs[parts + 3 :], (grad,) + new):
        ref[0, 0] = value


def expert_update(parts, weight, first, second):
    local, _, hidden, width = weight.shape
    block = pl.BlockSpec((1, 1, hidden, width), lambda e, m: (e, m, 0, 0))
    return pl.pallas_call(
        functools.partial(expert_update_kernel, len(parts)),
        grid=(local, 2),
        out_shape=[sds(weight.shape, f32)] * 4,
        in_specs=[block] * (len(parts) + 3),
        out_specs=[block] * 4,
        name="expert_update",
    )(*parts, weight, first, second)


def swap(value, axis, size, bit):
    return lax.ppermute(value, axis, [(i, i ^ bit) for i in range(size)])


def ring_list(size):
    half = size // 2
    return [2 * i for i in range(half)] + [2 * i + 1 for i in reversed(range(half))]


def turn(value, size, by):
    order = ring_list(size)
    pairs = [(order[i], order[(i + by) % size]) for i in range(size)]
    return lax.ppermute(value, "rep", pairs)


def spread(value, size):
    held = {0: value}
    bit = size // 2
    while bit:
        held.update({k ^ bit: swap(v, "shard", size, bit) for k, v in list(held.items())})
        bit //= 2
    return [held[k] for k in range(size)]


def ring_gather(value, size, lean):
    held = {0: value}
    reach = {1: size // 2 - (1 - lean), -1: size // 2 - lean}
    moving = {1: value, -1: value}
    for hop in range(1, size // 2 + 1):
        for way in (1, -1):
            if hop <= reach[way]:
                moving[way] = turn(moving[way], size, way)
                held[-way * hop % size] = moving[way]
    return held


def ring_sum(grads, size, lean):
    reach = {1: size // 2 - (1 - lean), -1: size // 2 - lean}
    arrived = {}
    for way in (1, -1):
        moving = None
        for hop in range(reach[way], 0, -1):
            own = grads[way * hop % size]
            if moving is not None:
                own = (own.astype(f32) + moving.astype(f32)).astype(bf16)
            moving = turn(own, size, way)
        arrived[way] = moving
    return [arrived[1], arrived[-1]]


def add(left, right):
    return (left.astype(f32) + right.astype(f32)).astype(bf16)


def shards(
    tokens,
    routes,
    cotangent,
    attn_weights,
    attn_first,
    attn_second,
    router_weights,
    router_first,
    router_second,
    norm_params,
    norm_first,
    norm_second,
    expert_weights,
    expert_first,
    expert_second,
    *,
    group,
    ring,
):
    tok_count, width = tokens.shape
    experts = router_weights.shape[1]
    local = expert_weights.shape[0]
    capacity = min(tok_count, (tok_count * 8 // (3 * experts) + 7) // 8 * 8)
    stride = -(-(capacity + 8) // 16) * 16
    images = tok_count // SEQ
    me = lax.axis_index("shard").astype(jnp.int32).reshape(1)

    def padded(rows, value):
        return jnp.pad(
            rows.reshape(images, SEQ, rows.shape[1]),
            ((0, 0), (0, PAD - SEQ), (0, 0)),
            constant_values=value,
        )

    packed, *expert_low = pack(attn_weights, router_weights, norm_params, expert_weights)
    pieces = spread(packed, group)
    held = [ring_gather(expert_low[e], ring, e % 2) for e in range(local)]
    x = padded(tokens, 0)
    cot = padded(cotangent, 0)
    cots = spread(cot.reshape(images * PAD, width), group)
    pos, meta = route_tables(me, padded(routes, -1), experts, local, group, stride)

    saved = []
    sent = [[] for _ in range(group)]
    for start in range(0, images, GROUP):
        c, *rest = front(me, x, meta, pieces, experts, start, GROUP)
        saved.append(rest)
        for k, piece in enumerate(spread(c.reshape(GROUP * PAD, width), group)):
            sent[k].append(piece)
    mid, qkv, probs, turned, gates = [jnp.concatenate(parts, axis=0) for parts in zip(*saved)]

    back, made, flags, parts = [], [], [], []
    for e in range(local):
        merged = e + 1 < local
        order = [held[e][d] for d in range(ring)]
        out = run_expert(e, local, me, sent, cots, order, stride, merged)
        if merged:
            both = [v if k == 0 else swap(v, "shard", group, k) for k, v in enumerate(out[:group])]
            back += both
            made += both
            grads = out[group:]
        else:
            back += [v if k == 0 else swap(v, "shard", group, k) for k, v in enumerate(out[:group])]
            made += [
                v if k == 0 else swap(v, "shard", group, k)
                for k, v in enumerate(out[group : 2 * group])
            ]
            grads = out[2 * group :]
        flags += [merged] * group
        parts.append([grads[0]] + ring_sum(grads, ring, e % 2))

    grad, keep, send = home(
        me, pos, gates, x, cot, mid, qkv, probs, turned, pieces, back, flags, experts
    )
    output = finish(pos, gates, mid, made, flags)

    total = add(keep, swap(send, "shard", group, 1))
    bit = 2
    while bit < group:
        count = total.shape[0] // 2
        pairs = total.reshape(count, 2, *total.shape[1:])
        total = add(pairs[:, 0], swap(pairs[:, 1], "shard", group, bit))
        bit *= 2
    total = total[0]
    bit = 1
    while bit < ring:
        total = add(total, swap(total, "rep", ring, bit))
        bit *= 2
    dense = dense_update(
        total,
        (attn_weights, attn_first, attn_second),
        (router_weights, router_first, router_second),
        (norm_params, norm_first, norm_second),
    )
    stacked = [jnp.stack([parts[e][i] for e in range(local)]) for i in range(3)]
    updated = expert_update(stacked, expert_weights, expert_first, expert_second)

    def unpadded(rows):
        return rows[:, :SEQ].reshape(tok_count, width)

    return (unpadded(output), unpadded(grad), *dense, *updated)


def solution(mesh):
    rows = P(("shard", "rep"), None)
    attn = P(None, "shard", None)
    router = P("shard", None)
    norm = P(None, "shard")
    expert = P("shard", None, "rep", None)
    return jax.shard_map(
        functools.partial(shards, group=mesh.shape["shard"], ring=mesh.shape["rep"]),
        mesh=mesh,
        in_specs=(rows,) * 3 + (attn,) * 3 + (router,) * 3 + (norm,) * 3 + (expert,) * 3,
        out_specs=(rows,) * 2 + (attn,) * 4 + (router,) * 4 + (norm,) * 4 + (expert,) * 4,
        check_vma=False,
    )
```

```python
import functools

import jax
import jax.numpy as jnp
from jax import lax
from jax.experimental import pallas as pl
from jax.experimental.pallas import tpu as pltpu
from jax.sharding import PartitionSpec as P

HEADS = 6
HEAD_DIM = 64
SEQ = 197
PAD = 208
STEP = 10
GROUP = 2

beta_one = 0.9
beta_two = 0.999
adam_floor = 1e-08
decay_rate = 0.1
rate_matrix = 0.05
rate_vector = 0.3
norm_floor = 1e-06

bf16 = jnp.bfloat16
f32 = jnp.float32
VMEM = pltpu.VMEM
ANY = pl.BlockSpec(memory_space=pl.ANY)
WHOLE = pl.BlockSpec(memory_space=pltpu.VMEM)
SCALAR = pl.BlockSpec(memory_space=pltpu.SMEM)


def params(mebibytes):
    return pltpu.CompilerParams(vmem_limit_bytes=mebibytes << 20)


def sds(shape, dtype):
    return jax.ShapeDtypeStruct(shape, dtype)


def cost(time_us):
    return pl.CostEstimate(
        flops=time_us * 1_150_000_000, bytes_accessed=time_us * 1_000_000, transcendentals=0
    )


def nn(left, right):
    return lax.dot_general(left, right, (((1,), (0,)), ((), ())), preferred_element_type=f32)


def nt(left, right):
    return lax.dot_general(left, right, (((1,), (1,)), ((), ())), preferred_element_type=f32)


def iota(shape, dim):
    return lax.broadcasted_iota(jnp.int32, shape, dim)


def normalize(values):
    centred = values - jnp.mean(values, axis=-1, keepdims=True)
    inverse = lax.rsqrt(jnp.mean(centred * centred, axis=-1, keepdims=True) + norm_floor)
    return centred * inverse, inverse


def norm_back(grad_rows, normed, inverse, gain):
    scaled = grad_rows * gain
    inner = (
        scaled
        - jnp.mean(scaled, axis=-1, keepdims=True)
        - normed * jnp.mean(scaled * normed, axis=-1, keepdims=True)
    )
    return inner * inverse


def eight_rows(values):
    rows, cols = values.shape
    return jnp.sum(values.reshape(rows // 8, 8, cols), axis=0)


def adamw(weight, first, second, grad, rate, decay):
    first_new = beta_one * first + (1.0 - beta_one) * grad
    second_new = beta_two * second + (1.0 - beta_two) * grad * grad
    first_hat = first_new * (1.0 / (1.0 - beta_one**STEP))
    second_hat = second_new * (1.0 / (1.0 - beta_two**STEP))
    return (
        first_new,
        second_new,
        weight - rate * (first_hat / (jnp.sqrt(second_hat) + adam_floor) + decay * weight),
    )


def pack_kernel(attn, router_t, norm, expert, packed, low):
    for e in range(expert.shape[0]):
        for m in range(2):
            low[m, e] = expert[e, m].astype(bf16)
    width = attn.shape[2]
    for index in range(4):
        packed[:, index * width : (index + 1) * width] = attn[index].astype(bf16)
    count, rows = router_t.shape
    filler = jnp.zeros((128 - count - 4, rows), f32)
    block = jnp.concatenate([router_t[...], norm[...], filler], axis=0)
    packed[:, 4 * width :] = block.T.astype(bf16)


def pack(attn, router_t, norm, expert):
    _, rows, width = attn.shape
    local, _, hidden, _ = expert.shape
    return pl.pallas_call(
        pack_kernel,
        out_shape=[sds((rows, 4 * width + 128), bf16), sds((2, local, hidden, width), bf16)],
        in_specs=[WHOLE] * 4,
        out_specs=[WHOLE] * 2,
        compiler_params=params(60),
        cost_estimate=cost(2),
        name="pack",
    )(attn, router_t, norm, expert)


def stage_kernel(local, group, stride, me_ref, tok_ref, cot_ref, routes_ref, _, *refs):
    x_ref, sent_ref, pos_ref, wide_ref, route_ref = refs
    images, _, width = x_ref.shape
    count = tok_ref.shape[0]
    rows = images * PAD

    def cut(image):
        tail = jnp.zeros((PAD - SEQ, width), f32)
        return jnp.concatenate([wide_ref[image * SEQ : (image + 1) * SEQ, :], tail], axis=0)

    wide_ref[:count, :] = tok_ref[...].astype(f32)
    for image in range(images):
        x_ref[image] = cut(image).astype(bf16)

    route_ref[:count, :] = routes_ref[...].astype(f32)
    gap = jnp.full((PAD - SEQ, 2), -1.0, f32)
    parts = []
    for image in range(images):
        parts += [route_ref[image * SEQ : (image + 1) * SEQ, :], gap]
    routes = jnp.concatenate(parts, axis=0)
    one, two = routes[:, 0:1], routes[:, 1:2]
    lane = iota((rows, 128), 1).astype(f32)
    pick_one, pick_two = lane == one, lane == two
    mask = jnp.where(pick_one | pick_two, 1.0, 0.0).astype(bf16)
    lower = jnp.where(iota((rows, rows), 0) >= iota((rows, rows), 1), 1.0, 0.0).astype(bf16)
    seen = nn(lower, mask)
    ranks = [
        jnp.sum(jnp.where(pick, seen, 0.0), axis=1, keepdims=True) - 1.0
        for pick in (pick_one, pick_two)
    ]
    places = []
    for route, rank in zip((one, two), ranks):
        owner = jnp.floor(route * (1.0 / local))
        inner = route - owner * local
        other = jnp.bitwise_xor(owner.astype(jnp.int32), me_ref[0]).astype(f32)
        places.append(
            jnp.where(route < 0.0, -1.0, (other * local + inner) * stride + rank)
        )
    table = jnp.where(lane == 0.0, places[0], jnp.where(lane == 1.0, places[1], 0.0))
    table = jnp.where(lane == 2.0, one, jnp.where(lane == 3.0, two, table))
    pos_ref[...] = table.reshape(images, PAD, 128)
    for at, rank in enumerate(ranks):
        high = jnp.floor(rank * (1.0 / 16.0))
        table = jnp.where(lane == 4.0 + 2 * at, high, table)
        table = jnp.where(lane == 5.0 + 2 * at, rank - 16.0 * high, table)
    wide_ref[:count, :] = cot_ref[...].astype(f32)
    for image in range(images):
        turned = table[image * PAD : (image + 1) * PAD].T[:8]
        turned = jnp.where(iota((8, PAD), 0) < 2, 0.0, turned)
        meta = jnp.concatenate([turned, jnp.zeros((8, width - PAD), f32)], axis=1)
        body = cut(image)[: PAD - 8]
        sent_ref[image] = jnp.concatenate([body, meta], axis=0).astype(bf16)


def stage(me, tokens, cotangent, routes, after, images, local, group, stride):
    count, width = tokens.shape
    padded = -(-count // 8) * 8
    return pl.pallas_call(
        functools.partial(stage_kernel, local, group, stride),
        out_shape=[sds((images, PAD, width), bf16)] * 2 + [sds((images, PAD, 128), f32)],
        in_specs=[SCALAR, WHOLE, WHOLE, WHOLE, ANY],
        out_specs=[WHOLE] * 3,
        scratch_shapes=[VMEM((padded, width), f32), VMEM((padded, 2), f32)],
        compiler_params=params(24),
        cost_estimate=cost(5),
        name="stage",
    )(me, tokens, cotangent, routes, after)


def load_weights(me, pieces, weights, turned, sem):
    rows = pieces[0].shape[0]
    copies = []
    for index, piece in enumerate(pieces):
        start = pl.multiple_of(jnp.bitwise_xor(me, index) * rows, 16)
        copies.append(pltpu.make_async_copy(piece, weights.at[pl.ds(start, rows)], sem.at[index]))
    for copy in copies:
        copy.start()
    for copy in copies:
        copy.wait()
    width = weights.shape[0]
    turned[...] = weights[:, 4 * width :].astype(f32).T


def front_kernel(experts, group, *refs):
    me_ref, x_ref, meta_ref = refs[:3]
    pieces = refs[3 : 3 + group]
    sent_ref, mid_ref, qkv_ref, probs_ref, turned_ref, gate_ref, weights, table, sem = refs[-9:]
    width = weights.shape[0]

    @pl.when(pl.program_id(0) == 0)
    def _():
        load_weights(me_ref[0], pieces, weights, table, sem)

    inputs = x_ref[0].astype(f32)
    normed, _ = normalize(inputs)
    gains = table[experts : experts + 4]
    rows_in = (normed * gains[0:1] + gains[1:2]).astype(bf16)
    qkv = nn(rows_in, weights[:, : 3 * width]).astype(bf16)
    qkv_ref[0] = qkv
    half = iota((PAD, 128), 1) < HEAD_DIM
    real = iota((PAD, PAD), 0) < SEQ
    scale = HEAD_DIM ** (-0.5)
    joined = []
    for pair in range(HEADS // 2):
        at = pair * 128
        query = qkv[:, at : at + 128]
        keys = qkv[:, width + at : width + at + 128]
        values = qkv[:, 2 * width + at : 2 * width + at + 128].astype(f32).T.astype(bf16)
        parts = []
        for head in range(2):
            own = jnp.where(half if head == 0 else ~half, keys, jnp.zeros_like(keys))
            scores = jnp.where(real, nt(own, query) * scale, -1e30)
            expd = jnp.exp(scores - jnp.max(scores, axis=0, keepdims=True))
            probs = (expd * (1.0 / jnp.sum(expd, axis=0, keepdims=True))).astype(bf16)
            probs_ref[0, 2 * pair + head] = probs
            parts.append(nn(values[head * HEAD_DIM : (head + 1) * HEAD_DIM], probs))
        both = jnp.concatenate(parts, axis=0)
        turned_ref[0, at : at + 128, :] = both.astype(bf16)
        joined.append(both.T.astype(bf16))
    attended = jnp.concatenate(joined, axis=1)
    middle = inputs + nn(attended, weights[:, 3 * width : 4 * width])
    mid_ref[0] = middle
    normed_two, _ = normalize(middle)
    expert_in = (normed_two * gains[2:3] + gains[3:4]).astype(bf16)
    logits = nt(table[:16].astype(bf16), expert_in)
    meta = meta_ref[0][PAD - 16 :].astype(f32)[8:, :PAD]
    row = iota((16, PAD), 0).astype(f32)
    picked = [
        jnp.sum(jnp.where(row == meta[2 + j : 3 + j], logits, 0.0), axis=0, keepdims=True)
        for j in range(2)
    ]
    top = jnp.maximum(picked[0], picked[1])
    exps = [jnp.exp(value - top) for value in picked]
    total = exps[0] + exps[1]
    row8 = iota((8, PAD), 0)
    gates = jnp.where(row8 == 0, exps[0] / total, jnp.where(row8 == 1, exps[1] / total, 0.0))
    gate_ref[0] = jnp.concatenate([gates, jnp.zeros((120, PAD), f32)], axis=0).T
    gap = picked[0] - picked[1]
    high = gap.astype(bf16).astype(f32)
    meta = jnp.where(row8 == 0, high, jnp.where(row8 == 1, gap - high, 0.0))
    meta = jnp.concatenate([meta, jnp.zeros((8, width - PAD), f32)], axis=1)
    sent_ref[0] = jnp.concatenate([expert_in.astype(f32)[: PAD - 8], meta], axis=0).astype(bf16)


def front(me, x, cot, pieces, experts, after):
    width = x.shape[2]
    count = x.shape[0]
    group = len(pieces)
    columns = pieces[0].shape[1]

    def take(*tail):
        return pl.BlockSpec((1,) + tail, lambda i: (i,) + (0,) * len(tail))

    give = take

    return pl.pallas_call(
        functools.partial(front_kernel, experts, group),
        grid=(count,),
        out_shape=[
            sds((count, PAD, width), bf16),
            sds((count, PAD, width), f32),
            sds((count, PAD, 3 * width), bf16),
            sds((count, HEADS, PAD, PAD), bf16),
            sds((count, width, PAD), bf16),
            sds((count, PAD, 128), f32),
        ],
        in_specs=[SCALAR, take(PAD, width), take(PAD, width)] + [ANY] * (group + len(after)),
        out_specs=[
            give(PAD, width),
            give(PAD, width),
            give(PAD, 3 * width),
            give(HEADS, PAD, PAD),
            give(width, PAD),
            give(PAD, 128),
        ],
        scratch_shapes=[
            VMEM((width, columns), bf16),
            VMEM((128, width), f32),
            pltpu.SemaphoreType.DMA((group,)),
        ],
        compiler_params=params(28),
        cost_estimate=cost(3 * count),
        name="front",
    )(me, x, cot, *pieces, *after)


def gather_grads_kernel(local, stride, *refs):
    refs = list(refs)
    me_ref, *grads = refs[: len(refs) - 4]
    out_ref, place_ref, cot, sem = refs[len(refs) - 4 :]
    group = len(grads)
    copies = [pltpu.make_async_copy(grads[k], cot.at[k], sem.at[k]) for k in range(group)]
    for copy in copies:
        copy.start()
    images = cot.shape[1]
    width = cot.shape[3]
    first = me_ref[0] * local
    slot = iota((stride, PAD), 0).astype(f32)
    row8 = iota((8, PAD), 0)
    for k in range(group):
        copies[k].wait()
        sums = jnp.zeros((local * stride, width), f32)
        for image in range(images):
            block = cot[k, image]
            meta = block[PAD - 16 :].astype(f32)[8:, :PAD]
            ranks = [16.0 * meta[4 + 2 * j : 5 + 2 * j] + meta[5 + 2 * j : 6 + 2 * j] for j in range(2)]
            picks = []
            table = jnp.zeros((8, PAD), f32)
            for e in range(local):
                expert = (first + e).astype(f32)
                is_one, is_two = meta[2:3] == expert, meta[3:4] == expert
                place = jnp.where(is_one, ranks[0], jnp.where(is_two, ranks[1], -1.0))
                picks.append(jnp.where(slot == place, 1.0, 0.0).astype(bf16))
                table = jnp.where(row8 == e, place, table)
                table = jnp.where(row8 == 4 + e, jnp.where(is_one, 1.0, 0.0), table)
            place_ref[k, image] = jnp.concatenate([table, jnp.zeros((8, 256 - PAD), f32)], axis=1)
            sums += nn(jnp.concatenate(picks, axis=0), block)
        for e in range(local):
            out_ref[e, k * stride : (k + 1) * stride, :] = sums[
                e * stride : (e + 1) * stride
            ].astype(bf16)


def gather_grads(me, grads, local, stride):
    group = len(grads)
    images, _, width = grads[0].shape
    return pl.pallas_call(
        functools.partial(gather_grads_kernel, local, stride),
        out_shape=[
            sds((local, group * stride, width), bf16),
            sds((group, images, 8, 256), f32),
        ],
        in_specs=[SCALAR] + [ANY] * group,
        out_specs=[WHOLE] * 2,
        scratch_shapes=[
            VMEM((group, images, PAD, width), bf16),
            pltpu.SemaphoreType.DMA((group,)),
        ],
        compiler_params=params(22),
        cost_estimate=cost(6),
        name="gather_grads",
    )(me, *grads)


def gather_rows_kernel(local, stride, *refs):
    refs = list(refs)
    place_ref, grad_ref, *tokens = refs[: len(refs) - 4]
    rows_ref, outs_ref, tok, sem = refs[len(refs) - 4 :]
    group = len(tokens)
    copies = [pltpu.make_async_copy(tokens[k], tok.at[k], sem.at[k]) for k in range(group)]
    for copy in copies:
        copy.start()
    images = tok.shape[1]
    width = tok.shape[3]
    slot = iota((stride, PAD), 0).astype(f32)
    for k in range(group):
        copies[k].wait()
        sums = jnp.zeros((local * stride, width), f32)
        gate_sum = jnp.zeros((local * stride, PAD), f32)
        for image in range(images):
            block = tok[k, image]
            meta = block[PAD - 16 :].astype(f32)[8:, :PAD]
            gap = meta[0:1] + meta[1:2]
            top = jnp.maximum(gap, 0.0)
            left, right = jnp.exp(gap - top), jnp.exp(-top)
            inverse = 1.0 / (left + right)
            table = place_ref[k, image][:, :PAD]
            picks, weighted = [], []
            for e in range(local):
                match = slot == table[e : e + 1]
                gate = jnp.where(table[4 + e : 5 + e] > 0.0, left, right) * inverse
                picks.append(jnp.where(match, 1.0, 0.0).astype(bf16))
                weighted.append(jnp.where(match, gate, 0.0))
            sums += nn(jnp.concatenate(picks, axis=0), block)
            gate_sum += jnp.concatenate(weighted, axis=0)
        gate = jnp.sum(gate_sum, axis=1, keepdims=True)
        part = slice(k * stride, (k + 1) * stride)
        for e in range(local):
            mine = slice(e * stride, (e + 1) * stride)
            rows_ref[e, part, :] = sums[mine].astype(bf16)
            outs_ref[e, part, :] = (grad_ref[e, part, :].astype(f32) * gate[mine]).astype(bf16)


def gather_rows(places, grads, tokens):
    local, slots, width = grads.shape
    group = len(tokens)
    images = tokens[0].shape[0]
    return pl.pallas_call(
        functools.partial(gather_rows_kernel, local, slots // group),
        out_shape=[sds((local, slots, width), bf16)] * 2,
        in_specs=[WHOLE] * 2 + [ANY] * group,
        out_specs=[WHOLE] * 2,
        scratch_shapes=[
            VMEM((group, images, PAD, width), bf16),
            pltpu.SemaphoreType.DMA((group,)),
        ],
        compiler_params=params(22),
        cost_estimate=cost(6),
        name="gather_rows",
    )(places, grads, *tokens)


def shard_views(shards):
    half = (len(shards) - 1) // 2
    views = [[ref.at[0], ref.at[1]] for ref in shards[:half]]
    views.append([shards[half], shards[half + 1]])
    return views + [[ref.at[0], ref.at[1]] for ref in shards[half + 2 :]]


def experts_kernel(group, count, *refs):
    refs = list(refs)
    rows_h, outs_h = refs[:2]
    shards, refs = shard_views(refs[2 : 2 + count]), refs[2 + count :]
    back_out, refs = refs[:group], refs[group:]
    act_h, down_h = refs[:2]
    rows, outs, mats, gone, moment, act_s, down_s, held_sem, weight_sem, out_sem = refs[2:]
    ring = len(shards)
    local, _, total, width = mats.shape
    hidden = total // ring
    _, steps, slots, step = act_s.shape
    stride = slots // group

    held_copies = [
        [
            pltpu.make_async_copy(rows_h.at[e], rows.at[e], held_sem.at[e, 0]),
            pltpu.make_async_copy(outs_h.at[e], outs.at[e], held_sem.at[e, 1]),
        ]
        for e in range(local)
    ]
    weight_copies = [
        [
            [
                pltpu.make_async_copy(
                    shards[r][m].at[e],
                    mats.at[e, m, pl.ds(r * hidden, hidden)],
                    weight_sem.at[e, r, m],
                )
                for m in range(2)
            ]
            for r in range(ring)
        ]
        for e in range(local)
    ]
    out_copies = [
        [
            [
                pltpu.make_async_copy(act_s.at[e, i], act_h.at[e, i], out_sem.at[e, i, 0]),
                pltpu.make_async_copy(down_s.at[e, i], down_h.at[e, i], out_sem.at[e, i, 1]),
            ]
            for i in range(steps)
        ]
        for e in range(local)
    ]
    for e in range(local):
        for copy in held_copies[e]:
            copy.start()
        for pair in weight_copies[e]:
            for copy in pair:
                copy.start()

    k0 = 0.7978845608028654
    k1 = 0.044715
    wide = -(-slots // 128) * 128
    row8 = iota((8, slots), 0)
    inside = iota((8, width), 1) < stride - 8
    for e in range(local):
        for copy in held_copies[e]:
            copy.wait()
        loaded = 0
        for i in range(steps):
            at = i * step
            while loaded * hidden < at + step:
                for copy in weight_copies[e][loaded]:
                    copy.wait()
                loaded += 1
            one, two = mats[e, 0, at : at + step, :], mats[e, 1, at : at + step, :]
            for k in range(group):
                part = slice(k * stride, (k + 1) * stride)
                pre = nt(rows[e, part, :], one)
                back = nt(outs[e, part, :], two)
                square = pre * pre
                tanh = jnp.tanh(pre * (k0 + (k0 * k1) * square))
                half = 0.5 + 0.5 * tanh
                act = pre * half
                slope = half + (2.0 * act) * (1.0 - half) * (k0 + (3.0 * k0 * k1) * square)
                both = act * back
                both = sum(both[:, lane : lane + 128] for lane in range(0, step, 128))
                down = (back * slope).astype(bf16)
                act_s[e, i, part, :] = act.astype(bf16)
                down_s[e, i, part, :] = down
                if i == 0:
                    moment[part, :] = both
                    gone[part, :] = nn(down, one)
                else:
                    moment[part, :] += both
                    gone[part, :] += nn(down, one)
            for copy in out_copies[e][i]:
                copy.start()
        sums = jnp.sum(moment[...].T, axis=0, keepdims=True)
        high = sums.astype(bf16).astype(f32)
        table = jnp.where(row8 == 0, high, jnp.where(row8 == 1, sums - high, 0.0))
        if wide > slots:
            table = jnp.concatenate([table, jnp.zeros((8, wide - slots), f32)], axis=1)
        for k in range(group):
            here = table if k == 0 else pltpu.roll(table, wide - k * stride, 1)
            here = jnp.where(inside, here[:, :width], 0.0)
            part = gone[k * stride : (k + 1) * stride - 8, :]
            back_out[k][e * stride : (e + 1) * stride, :] = jnp.concatenate(
                [part, here], axis=0
            ).astype(bf16)
    for e in range(local):
        for pair in out_copies[e]:
            for copy in pair:
                copy.wait()


def run_experts(rows, outs, shards, group):
    ring = len(shards) - 1
    local, slots, width = rows.shape
    stride = slots // group
    hidden = shards[0].shape[2]
    total = ring * hidden
    step = 512 if total % 512 == 0 else 256
    kept = (local, total // step, slots, step)
    return pl.pallas_call(
        functools.partial(experts_kernel, group, len(shards)),
        out_shape=[sds((local * stride, width), bf16)] * group + [sds(kept, bf16)] * 2,
        in_specs=[ANY] * (2 + len(shards)),
        out_specs=[WHOLE] * group + [ANY] * 2,
        scratch_shapes=[
            VMEM(rows.shape, bf16),
            VMEM(rows.shape, bf16),
            VMEM((local, 2, total, width), bf16),
            VMEM((slots, width), f32),
            VMEM((slots, 128), f32),
            VMEM(kept, bf16),
            VMEM(kept, bf16),
            pltpu.SemaphoreType.DMA((local, 2)),
            pltpu.SemaphoreType.DMA((local, ring, 2)),
            pltpu.SemaphoreType.DMA((local, total // step, 2)),
        ],
        compiler_params=params(56),
        cost_estimate=cost(24),
        name="experts",
    )(rows, outs, *shards)


def expert_grads_kernel(group, count, *refs):
    refs = list(refs)
    rows_h, outs_h, act_h, down_h = refs[:4]
    shards, refs = shard_views(refs[4 : 4 + count]), refs[4 + count :]
    made_out, refs = refs[:group], refs[group:]
    grad_out, refs = shard_views(refs[:count]), refs[count:]
    rows, outs, act, down, second, made, grads, held_sem, kept_sem, weight_sem, out_sem = refs
    ring = len(shards)
    local, total, width = second.shape
    hidden = total // ring
    _, steps, slots, step = act.shape
    stride = slots // group

    held_copies = [
        [
            pltpu.make_async_copy(rows_h.at[e], rows.at[e], held_sem.at[e, 0]),
            pltpu.make_async_copy(outs_h.at[e], outs.at[e], held_sem.at[e, 1]),
        ]
        for e in range(local)
    ]
    kept_copies = [
        [
            [
                pltpu.make_async_copy(act_h.at[e, i], act.at[e, i], kept_sem.at[e, i, 0]),
                pltpu.make_async_copy(down_h.at[e, i], down.at[e, i], kept_sem.at[e, i, 1]),
            ]
            for i in range(steps)
        ]
        for e in range(local)
    ]
    weight_copies = [
        [
            pltpu.make_async_copy(
                shards[r][1].at[e], second.at[e, pl.ds(r * hidden, hidden)], weight_sem.at[e, r]
            )
            for r in range(ring)
        ]
        for e in range(local)
    ]
    out_copies = [
        [
            [
                pltpu.make_async_copy(
                    grads.at[e, m, pl.ds(r * hidden, hidden)],
                    grad_out[r][m].at[e],
                    out_sem.at[e, r, m],
                )
                for m in range(2)
            ]
            for r in range(ring)
        ]
        for e in range(local)
    ]
    for e in range(local):
        for copy in held_copies[e] + kept_copies[e][0] + weight_copies[e]:
            copy.start()
        for pair in kept_copies[e][1:]:
            for copy in pair:
                copy.start()
    for e in range(local):
        for copy in held_copies[e]:
            copy.wait()
        rows_t = rows[e].astype(f32).T.astype(bf16)
        outs_t = outs[e].astype(f32).T.astype(bf16)
        loaded = sent = 0
        for i in range(steps):
            at = i * step
            while loaded * hidden < at + step:
                weight_copies[e][loaded].wait()
                loaded += 1
            for copy in kept_copies[e][i]:
                copy.wait()
            grads[e, 0, at : at + step, :] = nn(rows_t, down[e, i]).T.astype(bf16)
            grads[e, 1, at : at + step, :] = nn(outs_t, act[e, i]).T.astype(bf16)
            while (sent + 1) * hidden <= at + step:
                for copy in out_copies[e][sent]:
                    copy.start()
                sent += 1
            if i == 0:
                made[...] = nn(act[e, i], second[e, at : at + step, :])
            else:
                made[...] += nn(act[e, i], second[e, at : at + step, :])
        for k in range(group):
            made_out[k][e * stride : (e + 1) * stride, :] = made[
                k * stride : (k + 1) * stride, :
            ].astype(bf16)
    for e in range(local):
        for pair in out_copies[e]:
            for copy in pair:
                copy.wait()


def expert_grads(rows, outs, act, down, shards, group):
    ring = len(shards) - 1
    local, slots, width = rows.shape
    stride = slots // group
    hidden = shards[0].shape[2]
    total = ring * hidden
    return pl.pallas_call(
        functools.partial(expert_grads_kernel, group, len(shards)),
        out_shape=[sds((local * stride, width), bf16)] * group
        + [sds(value.shape, bf16) for value in shards],
        in_specs=[ANY] * (4 + len(shards)),
        out_specs=[WHOLE] * group + [ANY] * len(shards),
        scratch_shapes=[
            VMEM(rows.shape, bf16),
            VMEM(rows.shape, bf16),
            VMEM(act.shape, bf16),
            VMEM(act.shape, bf16),
            VMEM((local, total, width), bf16),
            VMEM((slots, width), f32),
            VMEM((local, 2, total, width), bf16),
            pltpu.SemaphoreType.DMA((local, 2)),
            pltpu.SemaphoreType.DMA((local, act.shape[1], 2)),
            pltpu.SemaphoreType.DMA((local, ring)),
            pltpu.SemaphoreType.DMA((local, ring, 2)),
        ],
        compiler_params=params(56),
        cost_estimate=cost(22),
        name="expert_grads",
    )(rows, outs, act, down, *shards)


def load_slots(blocks, buffer, sem):
    stride = blocks[0].shape[0]
    return [
        pltpu.make_async_copy(block, buffer.at[pl.ds(i * stride, stride)], sem.at[i])
        for i, block in enumerate(blocks)
    ]


def home_kernel(experts, local, group, blocks, extra, opening, closing, *refs):
    refs = list(refs)
    me_ref, pos_ref, gate_ref, x_ref, cot_ref, mid_ref, qkv_ref, probs_ref, turned_ref = refs[:9]
    refs = refs[9:]
    pieces, refs = refs[:group], refs[group:]
    slots, refs = refs[:blocks], refs[blocks:]
    refs = refs[extra:]
    if not opening:
        carried, refs = refs[:3], refs[3:]
    grad_ref, refs = refs[0], refs[1:]
    if closing:
        keep_ref, send_ref = refs[:2]
        refs = refs[2:]
    else:
        carry, refs = refs[:3], refs[3:]
    weights, table, buffer, moments, grads, router_acc, norm_acc, sem, slot_sem, carry_sem = refs
    sums = (grads, router_acc, norm_acc)
    width = weights.shape[0]
    stride = slots[0].shape[0] // local
    wide = buffer.shape[0]
    step = pl.program_id(0)

    @pl.when(step == 0)
    def _():
        copies = load_slots(slots, buffer, slot_sem)
        if not opening:
            copies += [
                pltpu.make_async_copy(carried[i], sums[i], carry_sem.at[i]) for i in range(3)
            ]
        for copy in copies:
            copy.start()
        load_weights(me_ref[0], pieces, weights, table, sem)
        if opening:
            for ref in sums:
                ref[...] = jnp.zeros_like(ref)
        for copy in copies:
            copy.wait()
        total = jnp.zeros((8, wide), f32)
        for i in range(blocks * local):
            tail = buffer[(i + 1) * stride - 16 : (i + 1) * stride, :].astype(f32)[8:]
            tail = jnp.concatenate([tail, jnp.zeros((8, wide - width), f32)], axis=1)
            total += tail if i == 0 else pltpu.roll(tail, i * stride, 1)
        moments[...] = total

    real = iota((PAD, 1), 0) < SEQ
    gains = table[experts : experts + 4]
    pos = pos_ref[0]
    gates = gate_ref[0]
    lane = iota((PAD, wide), 1).astype(f32)
    match_one = lane == pos[:, 0:1]
    match_two = lane == pos[:, 1:2]
    pick = jnp.where(match_one | match_two, 1.0, 0.0).astype(bf16)
    moment = moments[0:1] + moments[1:2]
    moment_one = jnp.sum(jnp.where(match_one, moment, 0.0), axis=1, keepdims=True)
    moment_two = jnp.sum(jnp.where(match_two, moment, 0.0), axis=1, keepdims=True)
    dz = gates[:, 1:2] * moment_one - gates[:, 0:1] * moment_two
    lane = iota((PAD, 128), 1).astype(f32)
    dl = jnp.where(lane == pos[:, 2:3], dz, jnp.where(lane == pos[:, 3:4], -dz, 0.0))
    middle = mid_ref[0]
    normed, inverse = normalize(middle)
    expert_in = (normed * gains[2:3] + gains[3:4]).astype(bf16)
    dc = nn(pick, buffer[...]) + nn(dl.astype(bf16), table[...].astype(bf16))
    router_acc[...] += nn(dl.T.astype(bf16), expert_in)
    norm_acc[2] += eight_rows(dc * normed)
    norm_acc[3] += eight_rows(dc)
    dx1 = jnp.where(real, cot_ref[0].astype(f32), 0.0) + norm_back(dc, normed, inverse, gains[2:3])
    low = dx1.astype(bf16)
    turned = turned_ref[0]
    grads[:, 3 * width :] += nn(turned, low)
    out_proj = weights[:, 3 * width : 4 * width]
    d_out = nt(low, out_proj).astype(bf16)
    d_out_t = nt(out_proj, low).astype(bf16)
    shared = d_out_t.astype(f32) * turned.astype(f32)

    qkv = qkv_ref[0]
    scale = HEAD_DIM ** (-0.5)
    half = iota((PAD, 128), 1) < HEAD_DIM
    dq, dk, dv = [], [], []
    for pair in range(HEADS // 2):
        at = pair * 128
        query = qkv[:, at : at + 128]
        keys = qkv[:, width + at : width + at + 128]
        values = qkv[:, 2 * width + at : 2 * width + at + 128]
        keys_t = keys.astype(f32).T.astype(bf16)
        do = d_out[:, at : at + 128]
        do_t = d_out_t[at : at + 128]
        zero = jnp.zeros_like(query)
        dq_t = []
        dk_sum = jnp.zeros((PAD, 128), f32)
        dv_sum = jnp.zeros((PAD, 128), f32)
        for head in range(2):
            mask = half if head == 0 else ~half
            low_at = at + head * HEAD_DIM
            probs = probs_ref[0, 2 * pair + head]
            dp = nn(jnp.where(mask, values, zero), do_t)
            center = jnp.sum(shared[low_at : low_at + HEAD_DIM], axis=0, keepdims=True)
            ds = (probs.astype(f32) * (dp - center)).astype(bf16)
            dk_sum += nn(ds, jnp.where(mask, query, zero))
            dv_sum += nn(probs, jnp.where(mask, do, zero))
            dq_t.append(nn(keys_t[head * HEAD_DIM : (head + 1) * HEAD_DIM], ds))
        dq.append((jnp.concatenate(dq_t, axis=0).T * scale).astype(bf16))
        dk.append((dk_sum * scale).astype(bf16))
        dv.append(dv_sum.astype(bf16))
    dqkv = jnp.concatenate(dq + dk + dv, axis=1)
    inputs = x_ref[0].astype(f32)
    normed_one, inverse_one = normalize(inputs)
    rows_in = normed_one * gains[0:1] + gains[1:2]
    grads[:, : 3 * width] += nn(rows_in.T.astype(bf16), dqkv)
    da = nt(dqkv, weights[:, : 3 * width])
    norm_acc[0] += eight_rows(da * normed_one)
    norm_acc[1] += eight_rows(da)
    grad_ref[0] = dx1 + norm_back(da, normed_one, inverse_one, gains[0:1])

    @pl.when(step == pl.num_programs(0) - 1)
    def _():
        if not closing:
            copies = [pltpu.make_async_copy(sums[i], carry[i], carry_sem.at[i]) for i in range(3)]
            for copy in copies:
                copy.start()
            for copy in copies:
                copy.wait()
            return
        rows = pieces[0].shape[0]
        row = iota((128, width), 0)
        misc = router_acc[...]
        for i in range(4):
            misc = jnp.where(
                row == experts + i, jnp.sum(norm_acc[i], axis=0, keepdims=True), misc
            )
        table[...] = misc
        extra = table[...].T
        weights[:, : 4 * width] = grads[...].astype(bf16)
        weights[:, 4 * width :] = extra.astype(bf16)
        for k in range(group):
            start = pl.multiple_of(jnp.bitwise_xor(me_ref[0], k) * rows, 16)
            target = keep_ref if k % 2 == 0 else send_ref
            target[k // 2] = weights[pl.ds(start, rows), :]


def home(me, pos, cot, x, saved, pieces, slots, after, carried, start, closing, experts, local):
    mid, qkv, probs, turned, gates = saved
    group, blocks = len(pieces), len(slots)
    count = GROUP
    width = x.shape[2]
    rows, columns = pieces[0].shape
    stride = slots[0].shape[0]
    wide = blocks * stride

    def take(*tail):
        return pl.BlockSpec((1,) + tail, lambda i: (i + start,) + (0,) * len(tail))

    sums = [sds((width, 4 * width), f32), sds((128, width), f32), sds((4, 8, width), f32)]
    if closing:
        last = [sds((group // 2, rows, columns), bf16)] * 2
    else:
        last = sums
    return pl.pallas_call(
        functools.partial(
            home_kernel, experts, local, group, blocks, len(after), carried is None, closing
        ),
        grid=(count,),
        out_shape=[sds((count, PAD, width), f32)] + last,
        in_specs=[
            SCALAR,
            take(PAD, 128),
            take(PAD, 128),
            take(PAD, width),
            take(PAD, width),
            take(PAD, width),
            take(PAD, 3 * width),
            take(HEADS, PAD, PAD),
            take(width, PAD),
        ]
        + [ANY] * (group + blocks + len(after) + (0 if carried is None else 3)),
        out_specs=[pl.BlockSpec((1, PAD, width), lambda i: (i, 0, 0))]
        + [WHOLE if closing else ANY] * len(last),
        scratch_shapes=[
            VMEM((width, columns), bf16),
            VMEM((128, width), f32),
            VMEM((wide, width), bf16),
            VMEM((8, wide), f32),
        ]
        + [VMEM(value.shape, f32) for value in sums]
        + [
            pltpu.SemaphoreType.DMA((group,)),
            pltpu.SemaphoreType.DMA((blocks,)),
            pltpu.SemaphoreType.DMA((3,)),
        ],
        compiler_params=params(32),
        cost_estimate=cost(6 * count),
        name="home",
    )(me, pos, gates, x, cot, mid, qkv, probs, turned, *pieces, *slots, *after, *(carried or ()))


def finish_kernel(blocks, *refs):
    pos_ref, gate_ref, mid_ref = refs[:3]
    slots = refs[3 : 3 + blocks]
    out_ref, buffer, slot_sem = refs[-3:]

    @pl.when(pl.program_id(0) == 0)
    def _():
        copies = load_slots(slots, buffer, slot_sem)
        for copy in copies:
            copy.start()
        for copy in copies:
            copy.wait()

    pos, gates = pos_ref[0], gate_ref[0]
    lane = iota((PAD, buffer.shape[0]), 1).astype(f32)
    total = mid_ref[0]
    for j in range(2):
        pick = jnp.where(lane == pos[:, j : j + 1], 1.0, 0.0).astype(bf16)
        total += gates[:, j : j + 1] * nn(pick, buffer[...])
    out_ref[0] = total.astype(bf16)


def finish(pos, saved, slots, after):
    mid, gates = saved[0], saved[4]
    count, _, width = mid.shape
    blocks = len(slots)
    stride = slots[0].shape[0]

    def take(*tail):
        return pl.BlockSpec((1,) + tail, lambda i: (i,) + (0,) * len(tail))

    return pl.pallas_call(
        functools.partial(finish_kernel, blocks),
        grid=(count,),
        out_shape=sds((count, PAD, width), bf16),
        in_specs=[
            take(PAD, 128),
            take(PAD, 128),
            take(PAD, width),
        ]
        + [ANY] * (blocks + len(after)),
        out_specs=take(PAD, width),
        scratch_shapes=[
            VMEM((blocks * stride, width), bf16),
            pltpu.SemaphoreType.DMA((blocks,)),
        ],
        compiler_params=params(24),
        cost_estimate=cost(2 * count),
        name="finish",
    )(pos, gates, mid, *slots, *after)


def dense_kernel(sum_ref, *refs):
    attn, router, norm = refs[:3], refs[3:6], refs[6:9]
    attn_out, router_out, norm_out = refs[9:13], refs[13:17], refs[17:21]
    width = attn[0].shape[2]
    count = router[0].shape[0]
    for index in range(4):
        grad = sum_ref[:, index * width : (index + 1) * width].astype(f32)
        new = adamw(*(ref[index] for ref in attn), grad, rate_matrix, decay_rate)
        for ref, value in zip(attn_out, (grad,) + new):
            ref[index] = value
    extra = sum_ref[:, 4 * width :].astype(f32).T
    grad = extra[:count]
    new = adamw(*(ref[...] for ref in router), grad, rate_matrix, decay_rate)
    for ref, value in zip(router_out, (grad,) + new):
        ref[...] = value
    grad = extra[count : count + 4]
    new = adamw(*(ref[...] for ref in norm), grad, rate_vector, 0.0)
    for ref, value in zip(norm_out, (grad,) + new):
        ref[...] = value


def dense_update(total, attn, router, norm):
    shapes = [sds(group[0].shape, f32) for group in (attn, router, norm) for _ in range(4)]
    return pl.pallas_call(
        dense_kernel,
        out_shape=shapes,
        in_specs=[WHOLE] * 10,
        out_specs=[WHOLE] * 12,
        compiler_params=params(16),
        cost_estimate=cost(3),
        name="dense_update",
    )(total, *attn, *router, *norm)


def expert_update_kernel(parts, *refs):
    state, sources, outs = refs[:3], refs[3 : 3 + parts], refs[-4:]
    for e in range(state[0].shape[0]):
        grad = sum(ref[0, e].astype(f32) for ref in sources)
        new = adamw(*(ref[e, 0] for ref in state), grad, rate_matrix, decay_rate)
        for ref, value in zip(outs, (grad,) + new):
            ref[e, 0] = value


def expert_update(parts, weight, first, second, after):
    local, _, hidden, width = weight.shape
    block = pl.BlockSpec((local, 1, hidden, width), lambda m: (0, m, 0, 0))
    part = pl.BlockSpec((1, local, hidden, width), lambda m: (m, 0, 0, 0))
    return pl.pallas_call(
        functools.partial(expert_update_kernel, len(parts)),
        grid=(2,),
        out_shape=[sds(weight.shape, f32)] * 4,
        in_specs=[block] * 3 + [part] * len(parts) + [ANY] * len(after),
        out_specs=[block] * 4,
        compiler_params=params(24),
        cost_estimate=cost(4),
        name="expert_update",
    )(weight, first, second, *parts, *after)


def swap(value, axis, size, bit):
    return lax.ppermute(value, axis, [(i, i ^ bit) for i in range(size)])


def ring_list(size):
    half = size // 2
    return [2 * i for i in range(half)] + [2 * i + 1 for i in reversed(range(half))]


def turn(value, size, by):
    order = ring_list(size)
    pairs = [(order[i], order[(i + by) % size]) for i in range(size)]
    return lax.ppermute(value, "rep", pairs)


def relay_kernel(*refs):
    pass


def tie(values, *others):
    values = list(values)
    return pl.pallas_call(
        relay_kernel,
        out_shape=[sds(value.shape, value.dtype) for value in values],
        in_specs=[ANY] * (len(values) + len(others)),
        out_specs=[ANY] * len(values),
        input_output_aliases={i: i for i in range(len(values))},
        compiler_params=params(1),
        cost_estimate=cost(0),
        name="relay",
    )(*values, *others)


def spread_far(value, size):
    held = {0: value}
    bit = size // 2
    while bit > 1:
        for k in list(held):
            held[k ^ bit] = swap(held[k], "shard", size, bit)
        bit //= 2
    return [held[k] for k in range(0, size, 2)]


def spread_near(values, size):
    both = [(value, swap(value, "shard", size, 1)) for value in values]
    return [value for pair in both for value in pair]


def ring_gather(value, size):
    half = size // 2
    held = [None] * size
    held[0] = value
    others = []
    ahead = behind = value
    for hop in range(1, half + 1):
        if others:
            ahead, behind = tie([ahead, behind], *others)
            held[size - hop + 1], held[hop - 1] = ahead, behind
        if hop == half:
            ahead, behind = ahead[0], behind[1]
        ahead, behind = turn(ahead, size, 1), turn(behind, size, -1)
        if hop < half:
            held[size - hop], held[hop] = ahead, behind
            others = (yield [ahead, behind]) or []
    yield held[:half] + [ahead, behind] + held[half + 1 :]


def ring_add_kernel(ahead, first, behind, second, *refs):
    out_a, out_b = refs[-2:]
    if len(first.shape) == len(ahead.shape):
        out_a[...] = (ahead[...].astype(f32) + first[...].astype(f32)).astype(bf16)
        out_b[...] = (behind[...].astype(f32) + second[...].astype(f32)).astype(bf16)
    else:
        out_a[0] = (ahead[0].astype(f32) + first[...].astype(f32)).astype(bf16)
        out_a[1] = ahead[1]
        out_b[0] = behind[0]
        out_b[1] = (behind[1].astype(f32) + second[...].astype(f32)).astype(bf16)


def ring_add(ahead, first, behind, second, after):
    return pl.pallas_call(
        ring_add_kernel,
        out_shape=[sds(ahead.shape, bf16)] * 2,
        in_specs=[WHOLE] * 4 + [ANY] * len(after),
        out_specs=[WHOLE] * 2,
        compiler_params=params(16),
        cost_estimate=cost(2),
        name="ring_add",
    )(ahead, first, behind, second, *after)


def ring_sum(grads, size):
    half = size // 2
    full = grads[:half] + [None] + grads[half + 2 :]
    sums = grads[half : half + 2]
    for hop in range(half, 0, -1):
        moving = [turn(sums[0], size, 1), turn(sums[1], size, -1)]
        if hop > 1:
            others = (yield moving) or []
            sums = ring_add(full[hop - 1], moving[0], full[size - hop + 1], moving[1], others)
    yield [full[0]] + moving


def add(left, right):
    return (left.astype(f32) + right.astype(f32)).astype(bf16)


def shards(
    tokens,
    routes,
    cotangent,
    attn_weights,
    attn_first,
    attn_second,
    router_weights,
    router_first,
    router_second,
    norm_params,
    norm_first,
    norm_second,
    expert_weights,
    expert_first,
    expert_second,
    *,
    group,
    ring,
):
    tok_count, width = tokens.shape
    experts = router_weights.shape[1]
    local = expert_weights.shape[0]
    capacity = min(tok_count, (tok_count * 8 // (3 * experts) + 7) // 8 * 8)
    stride = -(-(capacity + 8) // 16) * 16
    images = tok_count // SEQ
    me = lax.axis_index("shard").astype(jnp.int32).reshape(1)

    packed, low = pack(attn_weights, router_weights.T, norm_params, expert_weights)
    gathering = ring_gather(low, ring)
    hop = next(gathering)
    pieces = spread_far(packed, group)
    x, cot, pos = stage(me, tokens, cotangent, routes, packed, images, local, group, stride)

    second = next(gathering)
    cots = spread_far(cot, group)
    pieces = spread_near(tie(pieces, pos), group)
    c, *saved = front(me, x, cot, pieces, experts, hop)
    c = tie([c], *second)[0]

    cs = spread_far(c, group)
    gathering.send([c])
    cots = tie(cots, c)
    cot = cots[0]
    cot_slots, places = gather_grads(me, spread_near(cots, group), local, stride)
    cs = spread_near(tie(cs, places), group)
    shards = list(gathering)[-1]
    rows, outs = gather_rows(places, cot_slots, cs)

    out = run_experts(rows, outs, shards, group)
    back = [v if k == 0 else swap(v, "shard", group, k) for k, v in enumerate(out[:group])]
    act, down = out[group:]
    out = expert_grads(rows, outs, act, down, shards, group)
    made, grads = out[:group], out[group:]
    summing = ring_sum(list(grads), ring)
    moving = next(summing)
    after = grads[:1]
    made = [v if k == 0 else swap(v, "shard", group, k) for k, v in enumerate(made)]

    grad, carried = [], None
    for start in range(0, images, GROUP):
        closing = start + GROUP >= images
        value, *carried = home(
            me, pos, cot, x, saved, pieces, back, after, carried, start, closing, experts, local
        )
        grad.append(value)
        if start == 0:
            after = grad[:1] + moving
            moving = summing.send(after)
    keep, send = carried
    send = tie([send], *made, *moving)[0]

    total = add(keep, swap(send, "shard", group, 1))
    summing.send([total])
    bit = 2
    while bit < group:
        count = total.shape[0] // 2
        pairs = total.reshape(count, 2, *total.shape[1:])
        total = add(pairs[:, 0], swap(pairs[:, 1], "shard", group, bit))
        bit *= 2
    total = total[0]
    output = finish(pos, saved, made, [total])
    bit = 1
    while bit < ring:
        total = add(total, swap(total, "rep", ring, bit))
        if bit == 1:
            parts = summing.send([total])
        if bit == 2:
            after = [total]
        bit *= 2
    for parts in summing:
        pass
    dense = dense_update(
        total,
        (attn_weights, attn_first, attn_second),
        (router_weights.T, router_first.T, router_second.T),
        (norm_params, norm_first, norm_second),
    )
    dense = [value.T if 4 <= i < 8 else value for i, value in enumerate(dense)]
    updated = expert_update(parts, expert_weights, expert_first, expert_second, after)

    def unpadded(*chunks):
        return jnp.concatenate([rows[:, :SEQ] for rows in chunks], axis=0).reshape(tok_count, width)

    return (unpadded(output), unpadded(*grad), *dense, *updated)


def solution(mesh):
    rows = P(("shard", "rep"), None)
    attn = P(None, "shard", None)
    router = P("shard", None)
    norm = P(None, "shard")
    expert = P("shard", None, "rep", None)
    return jax.shard_map(
        functools.partial(shards, group=mesh.shape["shard"], ring=mesh.shape["rep"]),
        mesh=mesh,
        in_specs=(rows,) * 3 + (attn,) * 3 + (router,) * 3 + (norm,) * 3 + (expert,) * 3,
        out_specs=(rows,) * 2 + (attn,) * 4 + (router,) * 4 + (norm,) * 4 + (expert,) * 4,
        check_vma=False,
    )
```

```python
import functools

import jax
import jax.numpy as jnp
from jax import lax
from jax.experimental import pallas as pl
from jax.experimental.pallas import tpu as pltpu
from jax.sharding import PartitionSpec as P

HEADS = 6
HEAD_DIM = 64
SEQ = 197
PAD = 208
STEP = 10
GROUP = 2
CHUNK = 272
STEP_HIDDEN = 256

beta_one = 0.9
beta_two = 0.999
adam_floor = 1e-08
decay_rate = 0.1
rate_matrix = 0.05
rate_vector = 0.3
norm_floor = 1e-06

bf16 = jnp.bfloat16
f32 = jnp.float32
VMEM = pltpu.VMEM
ANY = pl.BlockSpec(memory_space=pl.ANY)
FAR = pl.BlockSpec(memory_space=pltpu.HBM)
WHOLE = pl.BlockSpec(memory_space=pltpu.VMEM)
SCALAR = pl.BlockSpec(memory_space=pltpu.SMEM)


def params(mebibytes):
    return pltpu.CompilerParams(vmem_limit_bytes=mebibytes << 20)


def sds(shape, dtype):
    return jax.ShapeDtypeStruct(shape, dtype)


def cost(time_us):
    return pl.CostEstimate(
        flops=time_us * 1_150_000_000, bytes_accessed=time_us * 1_000_000, transcendentals=0
    )


def nn(left, right):
    return lax.dot_general(left, right, (((1,), (0,)), ((), ())), preferred_element_type=f32)


def nt(left, right):
    return lax.dot_general(left, right, (((1,), (1,)), ((), ())), preferred_element_type=f32)


def iota(shape, dim):
    return lax.broadcasted_iota(jnp.int32, shape, dim)


def normalize(values):
    centred = values - jnp.mean(values, axis=-1, keepdims=True)
    inverse = lax.rsqrt(jnp.mean(centred * centred, axis=-1, keepdims=True) + norm_floor)
    return centred * inverse, inverse


def norm_back(grad_rows, normed, inverse, gain):
    scaled = grad_rows * gain
    inner = (
        scaled
        - jnp.mean(scaled, axis=-1, keepdims=True)
        - normed * jnp.mean(scaled * normed, axis=-1, keepdims=True)
    )
    return inner * inverse


def eight_rows(values):
    rows, cols = values.shape
    return jnp.sum(values.reshape(rows // 8, 8, cols), axis=0)


def adamw(weight, first, second, grad, rate, decay):
    first_new = beta_one * first + (1.0 - beta_one) * grad
    second_new = beta_two * second + (1.0 - beta_two) * grad * grad
    first_hat = first_new * (1.0 / (1.0 - beta_one**STEP))
    second_hat = second_new * (1.0 / (1.0 - beta_two**STEP))
    return (
        first_new,
        second_new,
        weight - rate * (first_hat / (jnp.sqrt(second_hat) + adam_floor) + decay * weight),
    )


def pack_kernel(attn, router_t, norm, expert, packed, low):
    for e in range(expert.shape[0]):
        for m in range(2):
            low[m, e] = expert[e, m].astype(bf16)
    width = attn.shape[2]
    for index in range(4):
        packed[:, index * width : (index + 1) * width] = attn[index].astype(bf16)
    count, rows = router_t.shape
    filler = jnp.zeros((128 - count - 4, rows), f32)
    block = jnp.concatenate([router_t[...], norm[...], filler], axis=0)
    packed[:, 4 * width :] = block.T.astype(bf16)


def pack(attn, router_t, norm, expert):
    _, rows, width = attn.shape
    local, _, hidden, _ = expert.shape
    return pl.pallas_call(
        pack_kernel,
        out_shape=[sds((rows, 4 * width + 128), bf16), sds((2, local, hidden, width), bf16)],
        in_specs=[WHOLE] * 4,
        out_specs=[WHOLE] * 2,
        compiler_params=params(60),
        cost_estimate=cost(2),
        name="pack",
    )(attn, router_t, norm, expert)


def stage_kernel(local, group, stride, me_ref, tok_ref, cot_ref, routes_ref, _, *refs):
    x_ref, sent_ref, pos_ref, wide_ref, route_ref = refs
    images, _, width = x_ref.shape
    count = tok_ref.shape[0]
    rows = images * PAD

    def cut(image):
        tail = jnp.zeros((PAD - SEQ, width), f32)
        return jnp.concatenate([wide_ref[image * SEQ : (image + 1) * SEQ, :], tail], axis=0)

    wide_ref[:count, :] = tok_ref[...].astype(f32)
    for image in range(images):
        x_ref[image] = cut(image).astype(bf16)

    route_ref[:count, :] = routes_ref[...].astype(f32)
    gap = jnp.full((PAD - SEQ, 2), -1.0, f32)
    parts = []
    for image in range(images):
        parts += [route_ref[image * SEQ : (image + 1) * SEQ, :], gap]
    routes = jnp.concatenate(parts, axis=0)
    one, two = routes[:, 0:1], routes[:, 1:2]
    lane = iota((rows, 128), 1).astype(f32)
    pick_one, pick_two = lane == one, lane == two
    mask = jnp.where(pick_one | pick_two, 1.0, 0.0).astype(bf16)
    lower = jnp.where(iota((rows, rows), 0) >= iota((rows, rows), 1), 1.0, 0.0).astype(bf16)
    seen = nn(lower, mask)
    ranks = [
        jnp.sum(jnp.where(pick, seen, 0.0), axis=1, keepdims=True) - 1.0
        for pick in (pick_one, pick_two)
    ]
    places = []
    for route, rank in zip((one, two), ranks):
        owner = jnp.floor(route * (1.0 / local))
        inner = route - owner * local
        other = jnp.bitwise_xor(owner.astype(jnp.int32), me_ref[0]).astype(f32)
        places.append(
            jnp.where(route < 0.0, -1.0, (inner * group + other) * stride + rank)
        )
    table = jnp.where(lane == 0.0, places[0], jnp.where(lane == 1.0, places[1], 0.0))
    table = jnp.where(lane == 2.0, one, jnp.where(lane == 3.0, two, table))
    pos_ref[...] = table.reshape(images, PAD, 128)
    for at, rank in enumerate(ranks):
        high = jnp.floor(rank * (1.0 / 16.0))
        table = jnp.where(lane == 4.0 + 2 * at, high, table)
        table = jnp.where(lane == 5.0 + 2 * at, rank - 16.0 * high, table)
    wide_ref[:count, :] = cot_ref[...].astype(f32)
    for image in range(images):
        turned = table[image * PAD : (image + 1) * PAD].T[:8]
        turned = jnp.where(iota((8, PAD), 0) < 2, 0.0, turned)
        meta = jnp.concatenate([turned, jnp.zeros((8, width - PAD), f32)], axis=1)
        body = cut(image)[: PAD - 8]
        sent_ref[image] = jnp.concatenate([body, meta], axis=0).astype(bf16)


def stage(me, tokens, cotangent, routes, after, images, local, group, stride):
    count, width = tokens.shape
    padded = -(-count // 8) * 8
    return pl.pallas_call(
        functools.partial(stage_kernel, local, group, stride),
        out_shape=[sds((images, PAD, width), bf16)] * 2 + [sds((images, PAD, 128), f32)],
        in_specs=[SCALAR, WHOLE, WHOLE, WHOLE, ANY],
        out_specs=[WHOLE] * 3,
        scratch_shapes=[VMEM((padded, width), f32), VMEM((padded, 2), f32)],
        compiler_params=params(24),
        cost_estimate=cost(5),
        name="stage",
    )(me, tokens, cotangent, routes, after)


def load_weights(me, pieces, weights, turned, sem):
    rows = pieces[0].shape[0]
    copies = []
    for index, piece in enumerate(pieces):
        start = pl.multiple_of(jnp.bitwise_xor(me, index) * rows, 16)
        copies.append(pltpu.make_async_copy(piece, weights.at[pl.ds(start, rows)], sem.at[index]))
    for copy in copies:
        copy.start()
    for copy in copies:
        copy.wait()
    width = weights.shape[0]
    turned[...] = weights[:, 4 * width :].astype(f32).T


def front_kernel(experts, group, *refs):
    me_ref, x_ref, meta_ref = refs[:3]
    pieces = refs[3 : 3 + group]
    sent_ref, mid_ref, qkv_ref, probs_ref, turned_ref, gate_ref, weights, table, sem = refs[-9:]
    width = weights.shape[0]

    @pl.when(pl.program_id(0) == 0)
    def _():
        load_weights(me_ref[0], pieces, weights, table, sem)

    inputs = x_ref[0].astype(f32)
    normed, _ = normalize(inputs)
    gains = table[experts : experts + 4]
    rows_in = (normed * gains[0:1] + gains[1:2]).astype(bf16)
    qkv = nn(rows_in, weights[:, : 3 * width]).astype(bf16)
    qkv_ref[0] = qkv
    half = iota((PAD, 128), 1) < HEAD_DIM
    real = iota((PAD, PAD), 0) < SEQ
    scale = HEAD_DIM ** (-0.5)
    joined = []
    for pair in range(HEADS // 2):
        at = pair * 128
        query = qkv[:, at : at + 128]
        keys = qkv[:, width + at : width + at + 128]
        values = qkv[:, 2 * width + at : 2 * width + at + 128].astype(f32).T.astype(bf16)
        parts = []
        for head in range(2):
            own = jnp.where(half if head == 0 else ~half, keys, jnp.zeros_like(keys))
            scores = jnp.where(real, nt(own, query) * scale, -1e30)
            expd = jnp.exp(scores - jnp.max(scores, axis=0, keepdims=True))
            probs = (expd * (1.0 / jnp.sum(expd, axis=0, keepdims=True))).astype(bf16)
            probs_ref[0, 2 * pair + head] = probs
            parts.append(nn(values[head * HEAD_DIM : (head + 1) * HEAD_DIM], probs))
        both = jnp.concatenate(parts, axis=0)
        turned_ref[0, at : at + 128, :] = both.astype(bf16)
        joined.append(both.T.astype(bf16))
    attended = jnp.concatenate(joined, axis=1)
    middle = inputs + nn(attended, weights[:, 3 * width : 4 * width])
    mid_ref[0] = middle
    normed_two, _ = normalize(middle)
    expert_in = (normed_two * gains[2:3] + gains[3:4]).astype(bf16)
    logits = nt(table[:16].astype(bf16), expert_in)
    meta = meta_ref[0][PAD - 16 :].astype(f32)[8:, :PAD]
    row = iota((16, PAD), 0).astype(f32)
    picked = [
        jnp.sum(jnp.where(row == meta[2 + j : 3 + j], logits, 0.0), axis=0, keepdims=True)
        for j in range(2)
    ]
    top = jnp.maximum(picked[0], picked[1])
    exps = [jnp.exp(value - top) for value in picked]
    total = exps[0] + exps[1]
    row8 = iota((8, PAD), 0)
    gates = jnp.where(row8 == 0, exps[0] / total, jnp.where(row8 == 1, exps[1] / total, 0.0))
    gate_ref[0] = jnp.concatenate([gates, jnp.zeros((120, PAD), f32)], axis=0).T
    gap = picked[0] - picked[1]
    high = gap.astype(bf16).astype(f32)
    meta = jnp.where(row8 == 0, high, jnp.where(row8 == 1, gap - high, 0.0))
    meta = jnp.concatenate([meta, jnp.zeros((8, width - PAD), f32)], axis=1)
    sent_ref[0] = jnp.concatenate([expert_in.astype(f32)[: PAD - 8], meta], axis=0).astype(bf16)


def front(me, x, cot, pieces, experts, after):
    width = x.shape[2]
    count = x.shape[0]
    group = len(pieces)
    columns = pieces[0].shape[1]

    def take(*tail):
        return pl.BlockSpec((1,) + tail, lambda i: (i,) + (0,) * len(tail))

    give = take

    return pl.pallas_call(
        functools.partial(front_kernel, experts, group),
        grid=(count,),
        out_shape=[
            sds((count, PAD, width), bf16),
            sds((count, PAD, width), f32),
            sds((count, PAD, 3 * width), bf16),
            sds((count, HEADS, PAD, PAD), bf16),
            sds((count, width, PAD), bf16),
            sds((count, PAD, 128), f32),
        ],
        in_specs=[SCALAR, take(PAD, width), take(PAD, width)] + [ANY] * (group + len(after)),
        out_specs=[
            give(PAD, width),
            give(PAD, width),
            give(PAD, 3 * width),
            give(HEADS, PAD, PAD),
            give(width, PAD),
            give(PAD, 128),
        ],
        scratch_shapes=[
            VMEM((width, columns), bf16),
            VMEM((128, width), f32),
            pltpu.SemaphoreType.DMA((group,)),
        ],
        compiler_params=params(28),
        cost_estimate=cost(3 * count),
        name="front",
    )(me, x, cot, *pieces, *after)


def gather_grads_kernel(local, stride, *refs):
    refs = list(refs)
    me_ref, *grads = refs[: len(refs) - 4]
    out_ref, place_ref, cot, sem = refs[len(refs) - 4 :]
    group = len(grads)
    copies = [pltpu.make_async_copy(grads[k], cot.at[k], sem.at[k]) for k in range(group)]
    for copy in copies:
        copy.start()
    images = cot.shape[1]
    width = cot.shape[3]
    first = me_ref[0] * local
    slot = iota((stride, PAD), 0).astype(f32)
    row8 = iota((8, PAD), 0)
    for k in range(group):
        copies[k].wait()
        sums = jnp.zeros((local * stride, width), f32)
        for image in range(images):
            block = cot[k, image]
            meta = block[PAD - 16 :].astype(f32)[8:, :PAD]
            ranks = [16.0 * meta[4 + 2 * j : 5 + 2 * j] + meta[5 + 2 * j : 6 + 2 * j] for j in range(2)]
            picks = []
            table = jnp.zeros((8, PAD), f32)
            for e in range(local):
                expert = (first + e).astype(f32)
                is_one, is_two = meta[2:3] == expert, meta[3:4] == expert
                place = jnp.where(is_one, ranks[0], jnp.where(is_two, ranks[1], -1.0))
                picks.append(jnp.where(slot == place, 1.0, 0.0).astype(bf16))
                table = jnp.where(row8 == e, place, table)
                table = jnp.where(row8 == 4 + e, jnp.where(is_one, 1.0, 0.0), table)
            place_ref[k, image] = jnp.concatenate([table, jnp.zeros((8, 256 - PAD), f32)], axis=1)
            sums += nn(jnp.concatenate(picks, axis=0), block)
        for e in range(local):
            out_ref[e, k * stride : (k + 1) * stride, :] = sums[
                e * stride : (e + 1) * stride
            ].astype(bf16)


def gather_grads(me, grads, local, stride):
    group = len(grads)
    images, _, width = grads[0].shape
    return pl.pallas_call(
        functools.partial(gather_grads_kernel, local, stride),
        out_shape=[
            sds((local, group * stride, width), bf16),
            sds((group, images, 8, 256), f32),
        ],
        in_specs=[SCALAR] + [ANY] * group,
        out_specs=[WHOLE] * 2,
        scratch_shapes=[
            VMEM((group, images, PAD, width), bf16),
            pltpu.SemaphoreType.DMA((group,)),
        ],
        compiler_params=params(22),
        cost_estimate=cost(6),
        name="gather_grads",
    )(me, *grads)


def gather_rows_kernel(local, stride, *refs):
    refs = list(refs)
    place_ref, grad_ref, *tokens = refs[: len(refs) - 4]
    rows_ref, outs_ref, tok, sem = refs[len(refs) - 4 :]
    group = len(tokens)
    copies = [pltpu.make_async_copy(tokens[k], tok.at[k], sem.at[k]) for k in range(group)]
    for copy in copies:
        copy.start()
    images = tok.shape[1]
    width = tok.shape[3]
    slot = iota((stride, PAD), 0).astype(f32)
    for k in range(group):
        copies[k].wait()
        sums = jnp.zeros((local * stride, width), f32)
        gate_sum = jnp.zeros((local * stride, PAD), f32)
        for image in range(images):
            block = tok[k, image]
            meta = block[PAD - 16 :].astype(f32)[8:, :PAD]
            gap = meta[0:1] + meta[1:2]
            top = jnp.maximum(gap, 0.0)
            left, right = jnp.exp(gap - top), jnp.exp(-top)
            inverse = 1.0 / (left + right)
            table = place_ref[k, image][:, :PAD]
            picks, weighted = [], []
            for e in range(local):
                match = slot == table[e : e + 1]
                gate = jnp.where(table[4 + e : 5 + e] > 0.0, left, right) * inverse
                picks.append(jnp.where(match, 1.0, 0.0).astype(bf16))
                weighted.append(jnp.where(match, gate, 0.0))
            sums += nn(jnp.concatenate(picks, axis=0), block)
            gate_sum += jnp.concatenate(weighted, axis=0)
        gate = jnp.sum(gate_sum, axis=1, keepdims=True)
        part = slice(k * stride, (k + 1) * stride)
        for e in range(local):
            mine = slice(e * stride, (e + 1) * stride)
            rows_ref[e, part, :] = sums[mine].astype(bf16)
            outs_ref[e, part, :] = (grad_ref[e, part, :].astype(f32) * gate[mine]).astype(bf16)


def gather_rows(places, grads, tokens):
    local, slots, width = grads.shape
    group = len(tokens)
    images = tokens[0].shape[0]
    return pl.pallas_call(
        functools.partial(gather_rows_kernel, local, slots // group),
        out_shape=[sds((local, slots, width), bf16)] * 2,
        in_specs=[WHOLE] * 2 + [ANY] * group,
        out_specs=[WHOLE] * 2,
        scratch_shapes=[
            VMEM((group, images, PAD, width), bf16),
            pltpu.SemaphoreType.DMA((group,)),
        ],
        compiler_params=params(22),
        cost_estimate=cost(6),
        name="gather_rows",
    )(places, grads, *tokens)


def shard_views(shards):
    half = (len(shards) - 1) // 2
    views = [[ref.at[0], ref.at[1]] for ref in shards[:half]]
    views.append([shards[half], shards[half + 1]])
    return views + [[ref.at[0], ref.at[1]] for ref in shards[half + 2 :]]


def assemble(shards, index, mats, first):
    hidden = mats.shape[1] // len(shards)
    for r, shard in enumerate(shards):
        for m in range(first, 2):
            mats[m - first, r * hidden : (r + 1) * hidden, :] = shard[m][index]


def expert_back(index, rows, outs, mats, moment, act_s, down_s, back_out, finished):
    steps, slots, step = act_s.shape
    stride = slots // len(back_out)
    width = mats.shape[2]
    k0 = 0.7978845608028654
    k1 = 0.044715
    for i in range(steps):
        for k in range(len(back_out)):
            part = slice(k * stride, (k + 1) * stride)
            partial = None
            for at in range(0, step, 256):
                own = slice(i * step + at, i * step + at + 256)
                pre = nt(rows[index, part, :], mats[0, own, :])
                back = nt(outs[index, part, :], mats[1, own, :])
                square = pre * pre
                tanh = jnp.tanh(pre * (k0 + (k0 * k1) * square))
                half = 0.5 + 0.5 * tanh
                act = pre * half
                slope = half + (2.0 * act) * (1.0 - half) * (k0 + (3.0 * k0 * k1) * square)
                both = act * back
                both = both[:, :128] + both[:, 128:]
                act_s[i, part, at : at + 256] = act.astype(bf16)
                down_s[i, part, at : at + 256] = (back * slope).astype(bf16)
                partial = both if partial is None else partial + both
            if i == 0:
                moment[part, :] = partial
            else:
                moment[part, :] += partial
        finished(i)

    wide = -(-slots // 128) * 128
    row8 = iota((8, slots), 0)
    inside = iota((8, width), 1) < stride - 8
    sums = jnp.sum(moment[...].T, axis=0, keepdims=True)
    high = sums.astype(bf16).astype(f32)
    table = jnp.where(row8 == 0, high, jnp.where(row8 == 1, sums - high, 0.0))
    if wide > slots:
        table = jnp.concatenate([table, jnp.zeros((8, wide - slots), f32)], axis=1)
    for k, out in enumerate(back_out):
        part = slice(k * stride, (k + 1) * stride)
        gone = sum(
            nn(down_s[i, part, :], mats[0, i * step : (i + 1) * step, :]) for i in range(steps)
        )
        here = table if k == 0 else pltpu.roll(table, wide - k * stride, 1)
        here = jnp.where(inside, here[:, :width], 0.0)
        out[...] = jnp.concatenate([gone[: stride - 8], here], axis=0).astype(bf16)


def expert_ends(index, rows, outs, second, act, down, grads, made_out, grad_out, sem, before):
    steps, slots, step = act.shape
    stride = slots // len(made_out)
    hidden = steps * step // len(grad_out)
    copies = [
        [
            pltpu.make_async_copy(
                grads.at[m, pl.ds(r * hidden, hidden)], grad_out[r][m], sem.at[r, m]
            )
            for m in range(2)
        ]
        for r in range(len(grad_out))
    ]
    rows_t = rows[index].astype(f32).T.astype(bf16)
    outs_t = outs[index].astype(f32).T.astype(bf16)
    sent = 0
    for i in range(steps):
        at = i * step
        before(i)
        grads[0, at : at + step, :] = nn(rows_t, down[i]).T.astype(bf16)
        grads[1, at : at + step, :] = nn(outs_t, act[i]).T.astype(bf16)
        while (sent + 1) * hidden <= at + step:
            for copy in copies[sent]:
                copy.start()
            sent += 1
    for k, out in enumerate(made_out):
        part = slice(k * stride, (k + 1) * stride)
        made = sum(
            nn(act[i, part, :], second[i * step : (i + 1) * step, :]) for i in range(steps)
        )
        out[...] = made.astype(bf16)
    for pair in copies:
        for copy in pair:
            copy.wait()


def expert_all_kernel(index, group, count, *refs):
    refs = list(refs)
    rows, outs = refs[:2]
    shards, refs = shard_views(refs[2 : 2 + count]), refs[2 + count :]
    back_out, made_out, refs = refs[:group], refs[group : 2 * group], refs[2 * group :]
    grad_out, refs = shard_views(refs[:count]), refs[count:]
    mats, moment, act_s, down_s, grads, sem = refs
    assemble(shards, index, mats, 0)
    expert_back(index, rows, outs, mats, moment, act_s, down_s, back_out, lambda i: None)
    expert_ends(
        index, rows, outs, mats.at[1], act_s, down_s, grads, made_out, grad_out, sem, lambda i: None
    )


def expert_back_kernel(index, group, count, *refs):
    refs = list(refs)
    rows, outs = refs[:2]
    shards, refs = shard_views(refs[2 : 2 + count]), refs[2 + count :]
    back_out, act_s, down_s, mats, moment = (refs[-4 - group : -4], *refs[-4:])
    assemble(shards, index, mats, 0)
    expert_back(index, rows, outs, mats, moment, act_s, down_s, back_out, lambda i: None)


def expert_ends_kernel(index, group, count, *refs):
    refs = list(refs)
    rows, outs, act, down = refs[:4]
    shards, refs = shard_views(refs[4 : 4 + count]), refs[4 + count :]
    second, grads, sem = refs[-3:]
    grad_out = shard_views(refs[-3 - count : -3])
    made_out = refs[-3 - count - group : -3 - count]
    assemble(shards, index, second, 1)
    expert_ends(
        index, rows, outs, second.at[0], act, down, grads, made_out, grad_out, sem, lambda i: None
    )


def expert_shapes(rows, shards, group):
    _, slots, width = rows.shape
    hidden = shards[0].shape[2]
    total = (len(shards) - 1) * hidden
    step = 512 if total % 512 == 0 else 256
    half = (len(shards) - 1) // 2
    grads = [sds(((2, hidden, width)), bf16)] * half + [sds((hidden, width), bf16)] * 2
    grads += [sds(((2, hidden, width)), bf16)] * (half - 1)
    grads = [pltpu.HBM(value.shape, bf16) for value in grads]
    return slots // group, total, (total // step, slots, step), grads


def run_whole(index, rows, outs, shards, group):
    stride, total, kept, grads = expert_shapes(rows, shards, group)
    _, slots, width = rows.shape
    count = len(shards)
    return pl.pallas_call(
        functools.partial(expert_all_kernel, index, group, count),
        out_shape=[sds((stride, width), bf16)] * (2 * group) + grads,
        in_specs=[WHOLE] * (2 + count),
        out_specs=[WHOLE] * (2 * group) + [ANY] * count,
        scratch_shapes=[
            VMEM((2, total, width), bf16),
            VMEM((slots, 128), f32),
            VMEM(kept, bf16),
            VMEM(kept, bf16),
            VMEM((2, total, width), bf16),
            pltpu.SemaphoreType.DMA((count - 1, 2)),
        ],
        compiler_params=params(32),
        cost_estimate=cost(14),
        name="expert_all",
    )(rows, outs, *shards)


def run_first(index, rows, outs, shards, group, after):
    stride, total, kept, _ = expert_shapes(rows, shards, group)
    _, slots, width = rows.shape
    count = len(shards)
    return pl.pallas_call(
        functools.partial(expert_back_kernel, index, group, count),
        out_shape=[sds((stride, width), bf16)] * group + [sds(kept, bf16)] * 2,
        in_specs=[WHOLE] * (2 + count) + [ANY] * len(after),
        out_specs=[WHOLE] * (group + 2),
        scratch_shapes=[VMEM((2, total, width), bf16), VMEM((slots, 128), f32)],
        compiler_params=params(24),
        cost_estimate=cost(9),
        name="expert_first",
    )(rows, outs, *shards, *after)


def run_last(index, rows, outs, kept, shards, after, group):
    stride, total, shape, grads = expert_shapes(rows, shards, group)
    width = rows.shape[2]
    count = len(shards)
    return pl.pallas_call(
        functools.partial(expert_ends_kernel, index, group, count),
        out_shape=[sds((stride, width), bf16)] * group + grads,
        in_specs=[WHOLE] * (4 + count) + [ANY] * len(after),
        out_specs=[WHOLE] * group + [ANY] * count,
        scratch_shapes=[
            VMEM((1, total, width), bf16),
            VMEM((2, total, width), bf16),
            pltpu.SemaphoreType.DMA((count - 1, 2)),
        ],
        compiler_params=params(24),
        cost_estimate=cost(8),
        name="expert_last",
    )(rows, outs, *kept, *shards, *after)


def load_slots(blocks, buffer, sem):
    stride = blocks[0].shape[0]
    return [
        pltpu.make_async_copy(block, buffer.at[pl.ds(i * stride, stride)], sem.at[i])
        for i, block in enumerate(blocks)
    ]


def home_kernel(experts, group, blocks, extra, opening, closing, *refs):
    refs = list(refs)
    me_ref, pos_ref, gate_ref, x_ref, cot_ref, mid_ref, qkv_ref, probs_ref, turned_ref = refs[:9]
    refs = refs[9:]
    pieces, refs = refs[:group], refs[group:]
    slots, refs = refs[:blocks], refs[blocks:]
    refs = refs[extra:]
    if not opening:
        carried, refs = refs[:3], refs[4:]
    grad_ref, refs = refs[0], refs[1:]
    if closing:
        keep_ref, send_ref = refs[:2]
        refs = refs[2:]
    else:
        carry, refs = refs[:3], refs[3:]
    weights, table, buffer, moments, grads, router_acc, norm_acc, sem, slot_sem, carry_sem = refs
    sums = (grads, router_acc, norm_acc)
    width = weights.shape[0]
    stride = slots[0].shape[0]
    wide = buffer.shape[0]
    step = pl.program_id(0)

    @pl.when(step == 0)
    def _():
        copies = load_slots(slots, buffer, slot_sem)
        if not opening:
            copies += [
                pltpu.make_async_copy(carried[i], sums[i], carry_sem.at[i]) for i in range(3)
            ]
        for copy in copies:
            copy.start()
        load_weights(me_ref[0], pieces, weights, table, sem)
        if opening:
            for ref in sums:
                ref[...] = jnp.zeros_like(ref)
        for copy in copies:
            copy.wait()
        total = jnp.zeros((8, wide), f32)
        for i in range(blocks):
            tail = buffer[(i + 1) * stride - 16 : (i + 1) * stride, :].astype(f32)[8:]
            tail = jnp.concatenate([tail, jnp.zeros((8, wide - width), f32)], axis=1)
            total += tail if i == 0 else pltpu.roll(tail, i * stride, 1)
        moments[...] = total

    real = iota((PAD, 1), 0) < SEQ
    gains = table[experts : experts + 4]
    pos = pos_ref[0]
    gates = gate_ref[0]
    lane = iota((PAD, wide), 1).astype(f32)
    match_one = lane == pos[:, 0:1]
    match_two = lane == pos[:, 1:2]
    pick = jnp.where(match_one | match_two, 1.0, 0.0).astype(bf16)
    moment = moments[0:1] + moments[1:2]
    moment_one = jnp.sum(jnp.where(match_one, moment, 0.0), axis=1, keepdims=True)
    moment_two = jnp.sum(jnp.where(match_two, moment, 0.0), axis=1, keepdims=True)
    dz = gates[:, 1:2] * moment_one - gates[:, 0:1] * moment_two
    lane = iota((PAD, 128), 1).astype(f32)
    dl = jnp.where(lane == pos[:, 2:3], dz, jnp.where(lane == pos[:, 3:4], -dz, 0.0))
    middle = mid_ref[0]
    normed, inverse = normalize(middle)
    expert_in = (normed * gains[2:3] + gains[3:4]).astype(bf16)
    dc = nn(pick, buffer[...]) + nn(dl.astype(bf16), table[...].astype(bf16))
    router_acc[...] += nn(dl.T.astype(bf16), expert_in)
    norm_acc[2] += eight_rows(dc * normed)
    norm_acc[3] += eight_rows(dc)
    dx1 = jnp.where(real, cot_ref[0].astype(f32), 0.0) + norm_back(dc, normed, inverse, gains[2:3])
    low = dx1.astype(bf16)
    turned = turned_ref[0]
    grads[:, 3 * width :] += nn(turned, low)
    out_proj = weights[:, 3 * width : 4 * width]
    d_out = nt(low, out_proj).astype(bf16)
    d_out_t = nt(out_proj, low).astype(bf16)
    shared = d_out_t.astype(f32) * turned.astype(f32)

    qkv = qkv_ref[0]
    scale = HEAD_DIM ** (-0.5)
    half = iota((PAD, 128), 1) < HEAD_DIM
    dq, dk, dv = [], [], []
    for pair in range(HEADS // 2):
        at = pair * 128
        query = qkv[:, at : at + 128]
        keys = qkv[:, width + at : width + at + 128]
        values = qkv[:, 2 * width + at : 2 * width + at + 128]
        keys_t = keys.astype(f32).T.astype(bf16)
        do = d_out[:, at : at + 128]
        do_t = d_out_t[at : at + 128]
        zero = jnp.zeros_like(query)
        dq_t = []
        dk_sum = jnp.zeros((PAD, 128), f32)
        dv_sum = jnp.zeros((PAD, 128), f32)
        for head in range(2):
            mask = half if head == 0 else ~half
            low_at = at + head * HEAD_DIM
            probs = probs_ref[0, 2 * pair + head]
            dp = nn(jnp.where(mask, values, zero), do_t)
            center = jnp.sum(shared[low_at : low_at + HEAD_DIM], axis=0, keepdims=True)
            ds = (probs.astype(f32) * (dp - center)).astype(bf16)
            dk_sum += nn(ds, jnp.where(mask, query, zero))
            dv_sum += nn(probs, jnp.where(mask, do, zero))
            dq_t.append(nn(keys_t[head * HEAD_DIM : (head + 1) * HEAD_DIM], ds))
        dq.append((jnp.concatenate(dq_t, axis=0).T * scale).astype(bf16))
        dk.append((dk_sum * scale).astype(bf16))
        dv.append(dv_sum.astype(bf16))
    dqkv = jnp.concatenate(dq + dk + dv, axis=1)
    inputs = x_ref[0].astype(f32)
    normed_one, inverse_one = normalize(inputs)
    rows_in = normed_one * gains[0:1] + gains[1:2]
    grads[:, : 3 * width] += nn(rows_in.T.astype(bf16), dqkv)
    da = nt(dqkv, weights[:, : 3 * width])
    norm_acc[0] += eight_rows(da * normed_one)
    norm_acc[1] += eight_rows(da)
    grad_ref[0] = dx1 + norm_back(da, normed_one, inverse_one, gains[0:1])

    @pl.when(step == pl.num_programs(0) - 1)
    def _():
        if not closing:
            copies = [pltpu.make_async_copy(sums[i], carry[i], carry_sem.at[i]) for i in range(3)]
            for copy in copies:
                copy.start()
            for copy in copies:
                copy.wait()
            return
        rows = pieces[0].shape[0]
        row = iota((128, width), 0)
        misc = router_acc[...]
        for i in range(4):
            misc = jnp.where(
                row == experts + i, jnp.sum(norm_acc[i], axis=0, keepdims=True), misc
            )
        table[...] = misc
        extra = table[...].T
        weights[:, : 4 * width] = grads[...].astype(bf16)
        weights[:, 4 * width :] = extra.astype(bf16)
        for k in range(group):
            start = pl.multiple_of(jnp.bitwise_xor(me_ref[0], k) * rows, 16)
            target = keep_ref if k % 2 == 0 else send_ref
            target[k // 2] = weights[pl.ds(start, rows), :]


def home(me, pos, cot, x, saved, pieces, slots, after, carried, start, closing, experts):
    mid, qkv, probs, turned, gates = saved
    group, blocks = len(pieces), len(slots)
    count = GROUP
    width = x.shape[2]
    rows, columns = pieces[0].shape
    stride = slots[0].shape[0]
    wide = blocks * stride

    def take(*tail):
        return pl.BlockSpec((1,) + tail, lambda i: (i + start,) + (0,) * len(tail))

    sums = [sds((width, 4 * width), f32), sds((128, width), f32), sds((4, 8, width), f32)]
    if closing:
        last = [sds((group // 2, rows, columns), bf16)] * 2
    else:
        last = sums
    return pl.pallas_call(
        functools.partial(
            home_kernel, experts, group, blocks, len(after), carried is None, closing
        ),
        grid=(count,),
        out_shape=[sds(x.shape[:2] + (width,), f32)] + last,
        in_specs=[
            SCALAR,
            take(PAD, 128),
            take(PAD, 128),
            take(PAD, width),
            take(PAD, width),
            take(PAD, width),
            take(PAD, 3 * width),
            take(HEADS, PAD, PAD),
            take(width, PAD),
        ]
        + [ANY] * (group + blocks + len(after) + (0 if carried is None else 4)),
        out_specs=[take(PAD, width)] + [WHOLE if closing else ANY] * len(last),
        input_output_aliases={} if carried is None else {12 + group + blocks + len(after): 0},
        scratch_shapes=[
            VMEM((width, columns), bf16),
            VMEM((128, width), f32),
            VMEM((wide, width), bf16),
            VMEM((8, wide), f32),
        ]
        + [VMEM(value.shape, f32) for value in sums]
        + [
            pltpu.SemaphoreType.DMA((group,)),
            pltpu.SemaphoreType.DMA((blocks,)),
            pltpu.SemaphoreType.DMA((3,)),
        ],
        compiler_params=params(32),
        cost_estimate=cost(6 * count),
        name="home",
    )(me, pos, gates, x, cot, mid, qkv, probs, turned, *pieces, *slots, *after, *(carried or ()))


def finish_kernel(blocks, *refs):
    pos_ref, gate_ref, mid_ref = refs[:3]
    slots = refs[3 : 3 + blocks]
    out_ref, buffer, slot_sem = refs[-3:]

    @pl.when(pl.program_id(0) == 0)
    def _():
        copies = load_slots(slots, buffer, slot_sem)
        for copy in copies:
            copy.start()
        for copy in copies:
            copy.wait()

    pos, gates = pos_ref[0], gate_ref[0]
    lane = iota((PAD, buffer.shape[0]), 1).astype(f32)
    total = mid_ref[0]
    for j in range(2):
        pick = jnp.where(lane == pos[:, j : j + 1], 1.0, 0.0).astype(bf16)
        total += gates[:, j : j + 1] * nn(pick, buffer[...])
    out_ref[0] = total.astype(bf16)


def finish(pos, saved, slots, after):
    mid, gates = saved[0], saved[4]
    count, _, width = mid.shape
    blocks = len(slots)
    stride = slots[0].shape[0]

    def take(*tail):
        return pl.BlockSpec((1,) + tail, lambda i: (i,) + (0,) * len(tail))

    return pl.pallas_call(
        functools.partial(finish_kernel, blocks),
        grid=(count,),
        out_shape=sds((count, PAD, width), bf16),
        in_specs=[
            take(PAD, 128),
            take(PAD, 128),
            take(PAD, width),
        ]
        + [ANY] * (blocks + len(after)),
        out_specs=take(PAD, width),
        scratch_shapes=[
            VMEM((blocks * stride, width), bf16),
            pltpu.SemaphoreType.DMA((blocks,)),
        ],
        compiler_params=params(24),
        cost_estimate=cost(2 * count),
        name="finish",
    )(pos, gates, mid, *slots, *after)


def dense_kernel(side_ref, own_ref, other_ref, *refs):
    attn, router, norm = refs[:3], refs[3:6], refs[6:9]
    attn_out, router_out, norm_out, sum_ref = refs[9:13], refs[13:17], refs[17:21], refs[21]
    count = own_ref.shape[0]
    for half, ref in enumerate((own_ref, other_ref)):
        at = pl.multiple_of(jnp.bitwise_xor(side_ref[0], half) * count, 8)
        sum_ref[pl.ds(at, count), :] = ref[...].astype(f32)
    width = attn[0].shape[2]
    count = router[0].shape[0]
    for index in range(4):
        grad = sum_ref[:, index * width : (index + 1) * width]
        new = adamw(*(ref[index] for ref in attn), grad, rate_matrix, decay_rate)
        for ref, value in zip(attn_out, (grad,) + new):
            ref[index] = value
    extra = sum_ref[:, 4 * width :].T
    grad = extra[:count]
    new = adamw(*(ref[...] for ref in router), grad, rate_matrix, decay_rate)
    for ref, value in zip(router_out, (grad,) + new):
        ref[...] = value
    grad = extra[count : count + 4]
    new = adamw(*(ref[...] for ref in norm), grad, rate_vector, 0.0)
    for ref, value in zip(norm_out, (grad,) + new):
        ref[...] = value


def dense_update(side, halves, attn, router, norm):
    shapes = [sds(group[0].shape, f32) for group in (attn, router, norm) for _ in range(4)]
    return pl.pallas_call(
        dense_kernel,
        out_shape=shapes,
        in_specs=[SCALAR] + [WHOLE] * 11,
        out_specs=[WHOLE] * 12,
        scratch_shapes=[VMEM((2 * halves[0].shape[0], halves[0].shape[1]), f32)],
        compiler_params=params(16),
        cost_estimate=cost(3),
        name="dense_update",
    )(side, *halves, *attn, *router, *norm)


def expert_update_kernel(parts, *refs):
    state, sources, outs = refs[:3], refs[3:-4], refs[-4:]
    for e in range(state[0].shape[0]):
        grad = sum(ref[0].astype(f32) for ref in sources[e * parts : (e + 1) * parts])
        new = adamw(*(ref[e, 0] for ref in state), grad, rate_matrix, decay_rate)
        for ref, value in zip(outs, (grad,) + new):
            ref[e, 0] = value


def expert_update(parts, weight, first, second):
    local, _, hidden, width = weight.shape
    block = pl.BlockSpec((local, 1, hidden, width), lambda m: (0, m, 0, 0))
    part = pl.BlockSpec((1, hidden, width), lambda m: (m, 0, 0))
    flat = [value for own in parts for value in own]
    return pl.pallas_call(
        functools.partial(expert_update_kernel, len(parts[0])),
        grid=(2,),
        out_shape=[sds(weight.shape, f32)] * 4,
        in_specs=[block] * 3 + [part] * len(flat),
        out_specs=[block] * 4,
        compiler_params=params(24),
        cost_estimate=cost(4),
        name="expert_update",
    )(weight, first, second, *flat)


def swap(value, axis, size, bit):
    return lax.ppermute(value, axis, [(i, i ^ bit) for i in range(size)])


def ring_list(size):
    half = size // 2
    return [2 * i for i in range(half)] + [2 * i + 1 for i in reversed(range(half))]


def turn(value, size, by):
    order = ring_list(size)
    pairs = [(order[i], order[(i + by) % size]) for i in range(size)]
    return lax.ppermute(value, "rep", pairs)


def relay_kernel(*refs):
    pass


def tie(values, *others):
    values = list(values)
    return pl.pallas_call(
        relay_kernel,
        out_shape=[sds(value.shape, value.dtype) for value in values],
        in_specs=[ANY] * (len(values) + len(others)),
        out_specs=[ANY] * len(values),
        input_output_aliases={i: i for i in range(len(values))},
        compiler_params=params(1),
        cost_estimate=cost(0),
        name="relay",
    )(*values, *others)


def spread_far(value, size):
    held = {0: value}
    bit = size // 2
    while bit > 1:
        for k in list(held):
            held[k ^ bit] = swap(held[k], "shard", size, bit)
        bit //= 2
    return [held[k] for k in range(0, size, 2)]


def spread_near(values, size):
    both = [(value, swap(value, "shard", size, 1)) for value in values]
    return [value for pair in both for value in pair]


def ring_gather(value, size):
    half = size // 2
    held = [None] * size
    held[0] = value
    others = []
    ahead = behind = value
    for hop in range(1, half + 1):
        if others:
            ahead, behind = tie([ahead, behind], *others)
            held[size - hop + 1], held[hop - 1] = ahead, behind
        if hop == half:
            ahead, behind = ahead[0], behind[1]
        ahead, behind = turn(ahead, size, 1), turn(behind, size, -1)
        if hop < half:
            held[size - hop], held[hop] = ahead, behind
            others = (yield [ahead, behind]) or []
    yield held[:half] + [ahead, behind] + held[half + 1 :]


def ring_add_kernel(ahead, first, behind, second, *refs):
    out_a, out_b = refs[-2:]
    if len(first.shape) == len(ahead.shape):
        out_a[...] = (ahead[...].astype(f32) + first[...].astype(f32)).astype(bf16)
        out_b[...] = (behind[...].astype(f32) + second[...].astype(f32)).astype(bf16)
    else:
        out_a[0] = (ahead[0].astype(f32) + first[...].astype(f32)).astype(bf16)
        out_a[1] = ahead[1]
        out_b[0] = behind[0]
        out_b[1] = (behind[1].astype(f32) + second[...].astype(f32)).astype(bf16)


def ring_add(ahead, first, behind, second, after):
    return pl.pallas_call(
        ring_add_kernel,
        out_shape=[sds(ahead.shape, bf16)] * 2,
        in_specs=[WHOLE] * 4 + [ANY] * len(after),
        out_specs=[WHOLE] * 2,
        compiler_params=params(16),
        cost_estimate=cost(0),
        name="ring_add",
    )(ahead, first, behind, second, *after)


def ring_sum(grads, size, formed):
    half = size // 2
    full = grads[:half] + [None] + grads[half + 2 :]
    sums = grads[half : half + 2]
    for hop in range(half, 0, -1):
        moving = [turn(sums[0], size, 1), turn(sums[1], size, -1)]
        if hop > 1:
            others = (yield moving) or []
            sums = ring_add(full[hop - 1], moving[0], full[size - hop + 1], moving[1], others)
            formed.extend(sums)
    yield [full[0]] + moving


def add(left, right):
    return (left.astype(f32) + right.astype(f32)).astype(bf16)


def shards(
    tokens,
    routes,
    cotangent,
    attn_weights,
    attn_first,
    attn_second,
    router_weights,
    router_first,
    router_second,
    norm_params,
    norm_first,
    norm_second,
    expert_weights,
    expert_first,
    expert_second,
    *,
    group,
    ring,
):
    tok_count, width = tokens.shape
    experts = router_weights.shape[1]
    local = expert_weights.shape[0]
    capacity = min(tok_count, (tok_count * 8 // (3 * experts) + 7) // 8 * 8)
    stride = -(-(capacity + 8) // 16) * 16
    images = tok_count // SEQ
    me = lax.axis_index("shard").astype(jnp.int32).reshape(1)

    packed, low = pack(attn_weights, router_weights.T, norm_params, expert_weights)
    gathering = ring_gather(low, ring)
    hop = next(gathering)
    pieces = spread_far(packed, group)
    x, cot, pos = stage(me, tokens, cotangent, routes, packed, images, local, group, stride)

    second = next(gathering)
    cots = spread_far(cot, group)
    pieces = spread_near(tie(pieces, pos), group)
    c, *saved = front(me, x, cot, pieces, experts, hop)
    c = tie([c], *second)[0]

    cs = spread_far(c, group)
    gathering.send([c])
    cots = tie(cots, c)
    cot = cots[0]
    cot_slots, places = gather_grads(me, spread_near(cots, group), local, stride)
    cs = spread_near(tie(cs, places), group)
    shards = list(gathering)[-1]
    rows, outs = gather_rows(places, cot_slots, cs)

    back, made, summing, formed = [], [], [], []
    after, latest = [], []

    def send_back(blocks):
        return [v if k == 0 else swap(v, "shard", group, k) for k, v in enumerate(blocks)]

    def start_sum(grads):
        formed.append([])
        summing.append(ring_sum(list(grads), ring, formed[-1]))
        latest.append(next(summing[-1]))

    def next_hop(at, others):
        latest[at] = summing[at].send(others)

    for e in range(local - 1):
        out = run_whole(e, rows, outs, shards, group)
        back += send_back(out[:group])
        made += out[group : 2 * group]
        start_sum(out[2 * group :])
        after = [out[2 * group]]
    early = list(back)
    out = run_first(local - 1, rows, outs, shards, group, after)
    back += send_back(out[:group])
    kept = out[group:]
    for at in range(len(summing)):
        next_hop(at, [out[0]])
    after = early + [value for own in formed for value in own[-2:]]
    out = run_last(local - 1, rows, outs, kept, shards, after, group)
    grads = out[group:]
    made = [v for at in range(0, len(made), group) for v in send_back(made[at : at + group])]
    for at in range(len(summing)):
        next_hop(at, [grads[0]])
    start_sum(grads)
    after = [grads[0]] + [value for own in formed for value in own[-2:]]

    grad, carried = None, None
    for start in range(0, images, GROUP):
        closing = start + GROUP >= images
        grad, *carried = home(
            me, pos, cot, x, saved, pieces, back, after, carried, start, closing, experts
        )
        if start == 0:
            gate = carried[1]
            carried.append(grad)
            for at in range(local):
                next_hop(at, [gate])
            after = [part for own in formed for part in own[-2:]] + made
            made = made + send_back(tie(out[:group], gate))
    keep, send = carried
    send = tie([send], *made, *latest[-1][-2:])[0]

    total = add(keep, swap(send, "shard", group, 1))
    next_hop(-1, [total])
    total = tie([total], *formed[-1][-2:])[0]
    bit = 2
    while bit < group:
        count = total.shape[0] // 2
        pairs = total.reshape(count, 2, *total.shape[1:])
        total = add(pairs[:, 0], swap(pairs[:, 1], "shard", group, bit))
        bit *= 2
    total = total[0]

    total = tie([total], *latest[-1][-2:])[0]
    side = lax.axis_index("rep") % 2
    count = total.shape[0] // 2
    own = lax.dynamic_slice_in_dim(total, side * count, count)
    other = lax.dynamic_slice_in_dim(total, (1 - side) * count, count)
    total = add(own, swap(other, "rep", ring, 1))
    bit = 2
    while bit < ring:
        total = add(total, swap(total, "rep", ring, bit))
        if bit == 2:
            next_hop(-1, [total])
            output = finish(pos, saved, made, [total])
        bit *= 2
    total = tie([total], *latest[-1][-2:])[0]
    for at in range(local):
        for latest[at] in summing[at]:
            pass
    halves = [total, swap(total, "rep", ring, 1)]
    dense = dense_update(
        side.astype(jnp.int32).reshape(1),
        halves,
        (attn_weights, attn_first, attn_second),
        (router_weights.T, router_first.T, router_second.T),
        (norm_params, norm_first, norm_second),
    )
    dense = [value.T if 4 <= i < 8 else value for i, value in enumerate(dense)]
    updated = expert_update(latest, expert_weights, expert_first, expert_second)

    def unpadded(rows):
        return rows[:, :SEQ].reshape(tok_count, width)

    return (unpadded(output), unpadded(grad), *dense, *updated)


def solution(mesh):
    rows = P(("shard", "rep"), None)
    attn = P(None, "shard", None)
    router = P("shard", None)
    norm = P(None, "shard")
    expert = P("shard", None, "rep", None)
    return jax.shard_map(
        functools.partial(shards, group=mesh.shape["shard"], ring=mesh.shape["rep"]),
        mesh=mesh,
        in_specs=(rows,) * 3 + (attn,) * 3 + (router,) * 3 + (norm,) * 3 + (expert,) * 3,
        out_specs=(rows,) * 2 + (attn,) * 4 + (router,) * 4 + (norm,) * 4 + (expert,) * 4,
        check_vma=False,
    )
```

```python
import functools

import jax
import jax.numpy as jnp
from jax import lax
from jax.experimental import pallas as pl
from jax.experimental.pallas import tpu as pltpu
from jax.sharding import PartitionSpec as P

HEADS = 6
HEAD_DIM = 64
SEQ = 197
PAD = 208
STEP = 10
GROUP = 2
CHUNK = 272
STEP_HIDDEN = 256

beta_one = 0.9
beta_two = 0.999
adam_floor = 1e-08
decay_rate = 0.1
rate_matrix = 0.05
rate_vector = 0.3
norm_floor = 1e-06

bf16 = jnp.bfloat16
f32 = jnp.float32
VMEM = pltpu.VMEM
ANY = pl.BlockSpec(memory_space=pl.ANY)
FAR = pl.BlockSpec(memory_space=pltpu.HBM)
WHOLE = pl.BlockSpec(memory_space=pltpu.VMEM)
SCALAR = pl.BlockSpec(memory_space=pltpu.SMEM)


def params(mebibytes):
    return pltpu.CompilerParams(vmem_limit_bytes=mebibytes << 20)


def sds(shape, dtype):
    return jax.ShapeDtypeStruct(shape, dtype)


def cost(time_us):
    return pl.CostEstimate(
        flops=time_us * 1_150_000_000, bytes_accessed=time_us * 1_000_000, transcendentals=0
    )


def nn(left, right):
    return lax.dot_general(left, right, (((1,), (0,)), ((), ())), preferred_element_type=f32)


def nt(left, right):
    return lax.dot_general(left, right, (((1,), (1,)), ((), ())), preferred_element_type=f32)


def iota(shape, dim):
    return lax.broadcasted_iota(jnp.int32, shape, dim)


def normalize(values):
    centred = values - jnp.mean(values, axis=-1, keepdims=True)
    inverse = lax.rsqrt(jnp.mean(centred * centred, axis=-1, keepdims=True) + norm_floor)
    return centred * inverse, inverse


def norm_back(grad_rows, normed, inverse, gain):
    scaled = grad_rows * gain
    inner = (
        scaled
        - jnp.mean(scaled, axis=-1, keepdims=True)
        - normed * jnp.mean(scaled * normed, axis=-1, keepdims=True)
    )
    return inner * inverse


def eight_rows(values):
    rows, cols = values.shape
    return jnp.sum(values.reshape(rows // 8, 8, cols), axis=0)


def adamw(weight, first, second, grad, rate, decay):
    first_new = beta_one * first + (1.0 - beta_one) * grad
    second_new = beta_two * second + (1.0 - beta_two) * grad * grad
    first_hat = first_new * (1.0 / (1.0 - beta_one**STEP))
    second_hat = second_new * (1.0 / (1.0 - beta_two**STEP))
    return (
        first_new,
        second_new,
        weight - rate * (first_hat / (jnp.sqrt(second_hat) + adam_floor) + decay * weight),
    )


def pack_kernel(attn, router_t, norm, expert, packed, low):
    for e in range(expert.shape[0]):
        for m in range(2):
            low[m, e] = expert[e, m].astype(bf16)
    width = attn.shape[2]
    for index in range(4):
        packed[:, index * width : (index + 1) * width] = attn[index].astype(bf16)
    count, rows = router_t.shape
    filler = jnp.zeros((128 - count - 4, rows), f32)
    block = jnp.concatenate([router_t[...], norm[...], filler], axis=0)
    packed[:, 4 * width :] = block.T.astype(bf16)


def pack(attn, router_t, norm, expert):
    _, rows, width = attn.shape
    local, _, hidden, _ = expert.shape
    return pl.pallas_call(
        pack_kernel,
        out_shape=[sds((rows, 4 * width + 128), bf16), sds((2, local, hidden, width), bf16)],
        in_specs=[WHOLE] * 4,
        out_specs=[WHOLE] * 2,
        compiler_params=params(60),
        cost_estimate=cost(2),
        name="pack",
    )(attn, router_t, norm, expert)


def stage_kernel(local, group, stride, me_ref, tok_ref, cot_ref, routes_ref, _, *refs):
    x_ref, sent_ref, pos_ref, wide_ref, route_ref = refs
    images, _, width = x_ref.shape
    count = tok_ref.shape[0]
    rows = images * PAD

    def cut(image):
        tail = jnp.zeros((PAD - SEQ, width), f32)
        return jnp.concatenate([wide_ref[image * SEQ : (image + 1) * SEQ, :], tail], axis=0)

    wide_ref[:count, :] = tok_ref[...].astype(f32)
    for image in range(images):
        x_ref[image] = cut(image).astype(bf16)

    route_ref[:count, :] = routes_ref[...].astype(f32)
    gap = jnp.full((PAD - SEQ, 2), -1.0, f32)
    parts = []
    for image in range(images):
        parts += [route_ref[image * SEQ : (image + 1) * SEQ, :], gap]
    routes = jnp.concatenate(parts, axis=0)
    one, two = routes[:, 0:1], routes[:, 1:2]
    lane = iota((rows, 128), 1).astype(f32)
    pick_one, pick_two = lane == one, lane == two
    mask = jnp.where(pick_one | pick_two, 1.0, 0.0).astype(bf16)
    lower = jnp.where(iota((rows, rows), 0) >= iota((rows, rows), 1), 1.0, 0.0).astype(bf16)
    seen = nn(lower, mask)
    ranks = [
        jnp.sum(jnp.where(pick, seen, 0.0), axis=1, keepdims=True) - 1.0
        for pick in (pick_one, pick_two)
    ]
    places = []
    for route, rank in zip((one, two), ranks):
        owner = jnp.floor(route * (1.0 / local))
        inner = route - owner * local
        other = jnp.bitwise_xor(owner.astype(jnp.int32), me_ref[0]).astype(f32)
        places.append(
            jnp.where(route < 0.0, -1.0, (inner * group + other) * stride + rank)
        )
    table = jnp.where(lane == 0.0, places[0], jnp.where(lane == 1.0, places[1], 0.0))
    table = jnp.where(lane == 2.0, one, jnp.where(lane == 3.0, two, table))
    pos_ref[...] = table.reshape(images, PAD, 128)
    for at, rank in enumerate(ranks):
        high = jnp.floor(rank * (1.0 / 16.0))
        table = jnp.where(lane == 4.0 + 2 * at, high, table)
        table = jnp.where(lane == 5.0 + 2 * at, rank - 16.0 * high, table)
    wide_ref[:count, :] = cot_ref[...].astype(f32)
    for image in range(images):
        turned = table[image * PAD : (image + 1) * PAD].T[:8]
        turned = jnp.where(iota((8, PAD), 0) < 2, 0.0, turned)
        meta = jnp.concatenate([turned, jnp.zeros((8, width - PAD), f32)], axis=1)
        body = cut(image)[: PAD - 8]
        sent_ref[image] = jnp.concatenate([body, meta], axis=0).astype(bf16)


def stage(me, tokens, cotangent, routes, after, images, local, group, stride):
    count, width = tokens.shape
    padded = -(-count // 8) * 8
    return pl.pallas_call(
        functools.partial(stage_kernel, local, group, stride),
        out_shape=[sds((images, PAD, width), bf16)] * 2 + [sds((images, PAD, 128), f32)],
        in_specs=[SCALAR, WHOLE, WHOLE, WHOLE, ANY],
        out_specs=[WHOLE] * 3,
        scratch_shapes=[VMEM((padded, width), f32), VMEM((padded, 2), f32)],
        compiler_params=params(24),
        cost_estimate=cost(5),
        name="stage",
    )(me, tokens, cotangent, routes, after)


def load_weights(me, pieces, weights, turned):
    rows = pieces[0].shape[0]
    for index, piece in enumerate(pieces):
        start = pl.multiple_of(jnp.bitwise_xor(me, index) * rows, 16)
        weights[pl.ds(start, rows), :] = piece[...]
    width = weights.shape[0]
    turned[...] = weights[:, 4 * width :].astype(f32).T


def front_kernel(experts, group, *refs):
    me_ref, x_ref, meta_ref = refs[:3]
    pieces = refs[3 : 3 + group]
    sent_ref, mid_ref, qkv_ref, probs_ref, turned_ref, gate_ref, weights, table = refs[-8:]
    width = weights.shape[0]

    @pl.when(pl.program_id(0) == 0)
    def _():
        load_weights(me_ref[0], pieces, weights, table)

    inputs = x_ref[0].astype(f32)
    normed, _ = normalize(inputs)
    gains = table[experts : experts + 4]
    rows_in = (normed * gains[0:1] + gains[1:2]).astype(bf16)
    qkv = nn(rows_in, weights[:, : 3 * width]).astype(bf16)
    qkv_ref[0] = qkv
    half = iota((PAD, 128), 1) < HEAD_DIM
    real = iota((PAD, PAD), 0) < SEQ
    scale = HEAD_DIM ** (-0.5)
    joined = []
    for pair in range(HEADS // 2):
        at = pair * 128
        query = qkv[:, at : at + 128]
        keys = qkv[:, width + at : width + at + 128]
        values = qkv[:, 2 * width + at : 2 * width + at + 128].astype(f32).T.astype(bf16)
        parts = []
        for head in range(2):
            own = jnp.where(half if head == 0 else ~half, keys, jnp.zeros_like(keys))
            scores = jnp.where(real, nt(own, query) * scale, -1e30)
            expd = jnp.exp(scores - jnp.max(scores, axis=0, keepdims=True))
            probs = (expd * (1.0 / jnp.sum(expd, axis=0, keepdims=True))).astype(bf16)
            probs_ref[0, 2 * pair + head] = probs
            parts.append(nn(values[head * HEAD_DIM : (head + 1) * HEAD_DIM], probs))
        both = jnp.concatenate(parts, axis=0)
        turned_ref[0, at : at + 128, :] = both.astype(bf16)
        joined.append(both.T.astype(bf16))
    attended = jnp.concatenate(joined, axis=1)
    middle = inputs + nn(attended, weights[:, 3 * width : 4 * width])
    mid_ref[0] = middle
    normed_two, _ = normalize(middle)
    expert_in = (normed_two * gains[2:3] + gains[3:4]).astype(bf16)
    logits = nt(table[:16].astype(bf16), expert_in)
    meta = meta_ref[0][PAD - 16 :].astype(f32)[8:, :PAD]
    row = iota((16, PAD), 0).astype(f32)
    picked = [
        jnp.sum(jnp.where(row == meta[2 + j : 3 + j], logits, 0.0), axis=0, keepdims=True)
        for j in range(2)
    ]
    top = jnp.maximum(picked[0], picked[1])
    exps = [jnp.exp(value - top) for value in picked]
    total = exps[0] + exps[1]
    row8 = iota((8, PAD), 0)
    gates = jnp.where(row8 == 0, exps[0] / total, jnp.where(row8 == 1, exps[1] / total, 0.0))
    gate_ref[0] = jnp.concatenate([gates, jnp.zeros((120, PAD), f32)], axis=0).T
    gap = picked[0] - picked[1]
    high = gap.astype(bf16).astype(f32)
    meta = jnp.where(row8 == 0, high, jnp.where(row8 == 1, gap - high, 0.0))
    meta = jnp.concatenate([meta, jnp.zeros((8, width - PAD), f32)], axis=1)
    sent_ref[0] = jnp.concatenate([expert_in.astype(f32)[: PAD - 8], meta], axis=0).astype(bf16)


def front(me, x, cot, pieces, experts, after):
    width = x.shape[2]
    count = x.shape[0]
    group = len(pieces)
    columns = pieces[0].shape[1]

    def take(*tail):
        return pl.BlockSpec((1,) + tail, lambda i: (i,) + (0,) * len(tail))

    give = take

    return pl.pallas_call(
        functools.partial(front_kernel, experts, group),
        grid=(count,),
        out_shape=[
            sds((count, PAD, width), bf16),
            sds((count, PAD, width), f32),
            sds((count, PAD, 3 * width), bf16),
            sds((count, HEADS, PAD, PAD), bf16),
            sds((count, width, PAD), bf16),
            sds((count, PAD, 128), f32),
        ],
        in_specs=[SCALAR, take(PAD, width), take(PAD, width)]
        + [WHOLE] * group
        + [ANY] * len(after),
        out_specs=[
            give(PAD, width),
            give(PAD, width),
            give(PAD, 3 * width),
            give(HEADS, PAD, PAD),
            give(width, PAD),
            give(PAD, 128),
        ],
        scratch_shapes=[
            VMEM((width, columns), bf16),
            VMEM((128, width), f32),
        ],
        compiler_params=params(28),
        cost_estimate=cost(3 * count),
        name="front",
    )(me, x, cot, *pieces, *after)


def gather_grads_kernel(local, stride, *refs):
    refs = list(refs)
    me_ref, *grads = refs[:-2]
    out_ref, place_ref = refs[-2:]
    group = len(grads)
    images, _, width = grads[0].shape
    first = me_ref[0] * local
    slot = iota((stride, PAD), 0).astype(f32)
    row8 = iota((8, PAD), 0)
    for k in range(group):
        sums = jnp.zeros((local * stride, width), f32)
        for image in range(images):
            block = grads[k][image]
            meta = block[PAD - 16 :].astype(f32)[8:, :PAD]
            ranks = [16.0 * meta[4 + 2 * j : 5 + 2 * j] + meta[5 + 2 * j : 6 + 2 * j] for j in range(2)]
            picks = []
            table = jnp.zeros((8, PAD), f32)
            for e in range(local):
                expert = (first + e).astype(f32)
                is_one, is_two = meta[2:3] == expert, meta[3:4] == expert
                place = jnp.where(is_one, ranks[0], jnp.where(is_two, ranks[1], -1.0))
                picks.append(jnp.where(slot == place, 1.0, 0.0).astype(bf16))
                table = jnp.where(row8 == e, place, table)
                table = jnp.where(row8 == 4 + e, jnp.where(is_one, 1.0, 0.0), table)
            place_ref[k, image] = jnp.concatenate([table, jnp.zeros((8, 256 - PAD), f32)], axis=1)
            sums += nn(jnp.concatenate(picks, axis=0), block)
        for e in range(local):
            out_ref[e, k * stride : (k + 1) * stride, :] = sums[
                e * stride : (e + 1) * stride
            ].astype(bf16)


def gather_grads(me, grads, local, stride):
    group = len(grads)
    images, _, width = grads[0].shape
    return pl.pallas_call(
        functools.partial(gather_grads_kernel, local, stride),
        out_shape=[
            sds((local, group * stride, width), bf16),
            sds((group, images, 8, 256), f32),
        ],
        in_specs=[SCALAR] + [WHOLE] * group,
        out_specs=[WHOLE] * 2,
        compiler_params=params(22),
        cost_estimate=cost(6),
        name="gather_grads",
    )(me, *grads)


def gather_rows_kernel(local, stride, *refs):
    refs = list(refs)
    place_ref, grad_ref, *tokens = refs[:-2]
    rows_ref, outs_ref = refs[-2:]
    group = len(tokens)
    images, _, width = tokens[0].shape
    slot = iota((stride, PAD), 0).astype(f32)
    for k in range(group):
        sums = jnp.zeros((local * stride, width), f32)
        gate_sum = jnp.zeros((local * stride, PAD), f32)
        for image in range(images):
            block = tokens[k][image]
            meta = block[PAD - 16 :].astype(f32)[8:, :PAD]
            gap = meta[0:1] + meta[1:2]
            top = jnp.maximum(gap, 0.0)
            left, right = jnp.exp(gap - top), jnp.exp(-top)
            inverse = 1.0 / (left + right)
            table = place_ref[k, image][:, :PAD]
            picks, weighted = [], []
            for e in range(local):
                match = slot == table[e : e + 1]
                gate = jnp.where(table[4 + e : 5 + e] > 0.0, left, right) * inverse
                picks.append(jnp.where(match, 1.0, 0.0).astype(bf16))
                weighted.append(jnp.where(match, gate, 0.0))
            sums += nn(jnp.concatenate(picks, axis=0), block)
            gate_sum += jnp.concatenate(weighted, axis=0)
        gate = jnp.sum(gate_sum, axis=1, keepdims=True)
        part = slice(k * stride, (k + 1) * stride)
        for e in range(local):
            mine = slice(e * stride, (e + 1) * stride)
            rows_ref[e, part, :] = sums[mine].astype(bf16)
            outs_ref[e, part, :] = (grad_ref[e, part, :].astype(f32) * gate[mine]).astype(bf16)


def gather_rows(places, grads, tokens):
    local, slots, width = grads.shape
    group = len(tokens)
    images = tokens[0].shape[0]
    return pl.pallas_call(
        functools.partial(gather_rows_kernel, local, slots // group),
        out_shape=[sds((local, slots, width), bf16)] * 2,
        in_specs=[WHOLE] * (2 + group),
        out_specs=[WHOLE] * 2,
        compiler_params=params(22),
        cost_estimate=cost(6),
        name="gather_rows",
    )(places, grads, *tokens)


def shard_views(shards):
    half = (len(shards) - 1) // 2
    views = [[ref.at[0], ref.at[1]] for ref in shards[:half]]
    views.append([shards[half], shards[half + 1]])
    return views + [[ref.at[0], ref.at[1]] for ref in shards[half + 2 :]]


def assemble(shards, index, mats, first):
    hidden = mats.shape[1] // len(shards)
    for r, shard in enumerate(shards):
        for m in range(first, 2):
            whole = len(shard[m].shape) == 2
            mats[m - first, r * hidden : (r + 1) * hidden, :] = (
                shard[m][...] if whole else shard[m][index]
            )


def expert_back(index, rows, outs, mats, moment, act_s, down_s, back_out, finished):
    steps, slots, step = act_s.shape
    stride = slots // len(back_out)
    width = mats.shape[2]
    k0 = 0.7978845608028654
    k1 = 0.044715
    for i in range(steps):
        for k in range(len(back_out)):
            part = slice(k * stride, (k + 1) * stride)
            partial = None
            for at in range(0, step, 256):
                own = slice(i * step + at, i * step + at + 256)
                pre = nt(rows[index, part, :], mats[0, own, :])
                back = nt(outs[index, part, :], mats[1, own, :])
                square = pre * pre
                tanh = jnp.tanh(pre * (k0 + (k0 * k1) * square))
                half = 0.5 + 0.5 * tanh
                act = pre * half
                slope = half + (2.0 * act) * (1.0 - half) * (k0 + (3.0 * k0 * k1) * square)
                both = act * back
                both = both[:, :128] + both[:, 128:]
                act_s[i, part, at : at + 256] = act.astype(bf16)
                down_s[i, part, at : at + 256] = (back * slope).astype(bf16)
                partial = both if partial is None else partial + both
            if i == 0:
                moment[part, :] = partial
            else:
                moment[part, :] += partial
        finished(i)

    wide = -(-slots // 128) * 128
    row8 = iota((8, slots), 0)
    inside = iota((8, width), 1) < stride - 8
    sums = jnp.sum(moment[...].T, axis=0, keepdims=True)
    high = sums.astype(bf16).astype(f32)
    table = jnp.where(row8 == 0, high, jnp.where(row8 == 1, sums - high, 0.0))
    if wide > slots:
        table = jnp.concatenate([table, jnp.zeros((8, wide - slots), f32)], axis=1)
    for k, out in enumerate(back_out):
        part = slice(k * stride, (k + 1) * stride)
        gone = sum(
            nn(down_s[i, part, :], mats[0, i * step : (i + 1) * step, :]) for i in range(steps)
        )
        here = table if k == 0 else pltpu.roll(table, wide - k * stride, 1)
        here = jnp.where(inside, here[:, :width], 0.0)
        out[...] = jnp.concatenate([gone[: stride - 8], here], axis=0).astype(bf16)


def expert_ends(index, rows, outs, second, act, down, grads, made_out, grad_out, sem, before):
    steps, slots, step = act.shape
    stride = slots // len(made_out)
    hidden = steps * step // len(grad_out)
    copies = [
        [
            pltpu.make_async_copy(
                grads.at[m, pl.ds(r * hidden, hidden)], grad_out[r][m], sem.at[r, m]
            )
            for m in range(2)
        ]
        for r in range(len(grad_out))
    ]
    rows_t = rows[index].astype(f32).T.astype(bf16)
    outs_t = outs[index].astype(f32).T.astype(bf16)
    sent = 0
    for i in range(steps):
        at = i * step
        before(i)
        grads[0, at : at + step, :] = nn(rows_t, down[i]).T.astype(bf16)
        grads[1, at : at + step, :] = nn(outs_t, act[i]).T.astype(bf16)
        while (sent + 1) * hidden <= at + step:
            for copy in copies[sent]:
                copy.start()
            sent += 1
    for k, out in enumerate(made_out):
        part = slice(k * stride, (k + 1) * stride)
        made = sum(
            nn(act[i, part, :], second[i * step : (i + 1) * step, :]) for i in range(steps)
        )
        out[...] = made.astype(bf16)
    for pair in copies:
        for copy in pair:
            copy.wait()


def expert_all_kernel(index, group, count, *refs):
    refs = list(refs)
    rows, outs = refs[:2]
    shards, refs = shard_views(refs[2 : 2 + count]), refs[2 + count :]
    back_out, made_out, refs = refs[:group], refs[group : 2 * group], refs[2 * group :]
    grad_out, refs = shard_views(refs[:count]), refs[count:]
    mats, moment, act_s, down_s, grads, sem = refs
    assemble(shards, index, mats, 0)
    expert_back(index, rows, outs, mats, moment, act_s, down_s, back_out, lambda i: None)
    expert_ends(
        index, rows, outs, mats.at[1], act_s, down_s, grads, made_out, grad_out, sem, lambda i: None
    )


def expert_back_kernel(index, group, count, *refs):
    refs = list(refs)
    rows, outs = refs[:2]
    shards, refs = shard_views(refs[2 : 2 + count]), refs[2 + count :]
    back_out, act_s, down_s, mats, moment = (refs[-4 - group : -4], *refs[-4:])
    assemble(shards, index, mats, 0)
    expert_back(index, rows, outs, mats, moment, act_s, down_s, back_out, lambda i: None)


def expert_ends_kernel(index, group, count, *refs):
    refs = list(refs)
    rows, outs, act, down = refs[:4]
    shards, refs = shard_views(refs[4 : 4 + count]), refs[4 + count :]
    second, grads, sem = refs[-3:]
    grad_out = shard_views(refs[-3 - count : -3])
    made_out = refs[-3 - count - group : -3 - count]
    assemble(shards, index, second, 1)
    expert_ends(
        index, rows, outs, second.at[0], act, down, grads, made_out, grad_out, sem, lambda i: None
    )


def expert_shapes(rows, shards, group):
    _, slots, width = rows.shape
    hidden = shards[0].shape[2]
    total = (len(shards) - 1) * hidden
    step = 512 if total % 512 == 0 else 256
    half = (len(shards) - 1) // 2
    grads = [sds(((2, hidden, width)), bf16)] * half + [sds((hidden, width), bf16)] * 2
    grads += [sds(((2, hidden, width)), bf16)] * (half - 1)
    grads = [pltpu.HBM(value.shape, bf16) for value in grads]
    return slots // group, total, (total // step, slots, step), grads


def run_whole(index, rows, outs, shards, group):
    stride, total, kept, grads = expert_shapes(rows, shards, group)
    _, slots, width = rows.shape
    count = len(shards)
    return pl.pallas_call(
        functools.partial(expert_all_kernel, index, group, count),
        out_shape=[sds((stride, width), bf16)] * (2 * group) + grads,
        in_specs=[WHOLE] * (2 + count),
        out_specs=[WHOLE] * (2 * group) + [ANY] * count,
        scratch_shapes=[
            VMEM((2, total, width), bf16),
            VMEM((slots, 128), f32),
            VMEM(kept, bf16),
            VMEM(kept, bf16),
            VMEM((2, total, width), bf16),
            pltpu.SemaphoreType.DMA((count - 1, 2)),
        ],
        compiler_params=params(32),
        cost_estimate=cost(14),
        name="expert_all",
    )(rows, outs, *shards)


def run_first(index, rows, outs, shards, group, after):
    stride, total, kept, _ = expert_shapes(rows, shards, group)
    _, slots, width = rows.shape
    count = len(shards)
    return pl.pallas_call(
        functools.partial(expert_back_kernel, index, group, count),
        out_shape=[sds((stride, width), bf16)] * group + [sds(kept, bf16)] * 2,
        in_specs=[WHOLE] * (2 + count) + [ANY] * len(after),
        out_specs=[WHOLE] * (group + 2),
        scratch_shapes=[VMEM((2, total, width), bf16), VMEM((slots, 128), f32)],
        compiler_params=params(24),
        cost_estimate=cost(9),
        name="expert_first",
    )(rows, outs, *shards, *after)


def run_last(index, rows, outs, kept, shards, after, group):
    stride, total, shape, grads = expert_shapes(rows, shards, group)
    width = rows.shape[2]
    count = len(shards)
    return pl.pallas_call(
        functools.partial(expert_ends_kernel, index, group, count),
        out_shape=[sds((stride, width), bf16)] * group + grads,
        in_specs=[WHOLE] * (4 + count) + [ANY] * len(after),
        out_specs=[WHOLE] * group + [ANY] * count,
        scratch_shapes=[
            VMEM((1, total, width), bf16),
            VMEM((2, total, width), bf16),
            pltpu.SemaphoreType.DMA((count - 1, 2)),
        ],
        compiler_params=params(24),
        cost_estimate=cost(8),
        name="expert_last",
    )(rows, outs, *kept, *shards, *after)


def load_slots(blocks, buffer):
    stride = blocks[0].shape[0]
    for i, block in enumerate(blocks):
        buffer[i * stride : (i + 1) * stride, :] = block[...]


def home_kernel(experts, group, blocks, extra, opening, closing, *refs):
    refs = list(refs)
    me_ref, pos_ref, gate_ref, x_ref, cot_ref, mid_ref, qkv_ref, probs_ref, turned_ref = refs[:9]
    refs = refs[9:]
    pieces, refs = refs[:group], refs[group:]
    slots, refs = refs[:blocks], refs[blocks:]
    refs = refs[extra:]
    if not opening:
        carried, refs = refs[:3], refs[4:]
    grad_ref, refs = refs[0], refs[1:]
    if closing:
        keep_ref, send_ref = refs[:2]
        refs = refs[2:]
    else:
        carry, refs = refs[:3], refs[3:]
    weights, table, buffer, moments = refs[:4]
    sums = refs[4:] if closing else carry
    grads, router_acc, norm_acc = sums
    width = weights.shape[0]
    stride = slots[0].shape[0]
    wide = buffer.shape[0]
    step = pl.program_id(0)

    @pl.when(step == 0)
    def _():
        load_slots(slots, buffer)
        load_weights(me_ref[0], pieces, weights, table)
        for i, ref in enumerate(sums):
            ref[...] = jnp.zeros_like(ref) if opening else carried[i][...]
        total = jnp.zeros((8, wide), f32)
        for i in range(blocks):
            tail = buffer[(i + 1) * stride - 16 : (i + 1) * stride, :].astype(f32)[8:]
            tail = jnp.concatenate([tail, jnp.zeros((8, wide - width), f32)], axis=1)
            total += tail if i == 0 else pltpu.roll(tail, i * stride, 1)
        moments[...] = total

    real = iota((PAD, 1), 0) < SEQ
    gains = table[experts : experts + 4]
    pos = pos_ref[0]
    gates = gate_ref[0]
    lane = iota((PAD, wide), 1).astype(f32)
    match_one = lane == pos[:, 0:1]
    match_two = lane == pos[:, 1:2]
    pick = jnp.where(match_one | match_two, 1.0, 0.0).astype(bf16)
    moment = moments[0:1] + moments[1:2]
    moment_one = jnp.sum(jnp.where(match_one, moment, 0.0), axis=1, keepdims=True)
    moment_two = jnp.sum(jnp.where(match_two, moment, 0.0), axis=1, keepdims=True)
    dz = gates[:, 1:2] * moment_one - gates[:, 0:1] * moment_two
    lane = iota((PAD, 128), 1).astype(f32)
    dl = jnp.where(lane == pos[:, 2:3], dz, jnp.where(lane == pos[:, 3:4], -dz, 0.0))
    middle = mid_ref[0]
    normed, inverse = normalize(middle)
    expert_in = (normed * gains[2:3] + gains[3:4]).astype(bf16)
    dc = nn(pick, buffer[...]) + nn(dl.astype(bf16), table[...].astype(bf16))
    router_acc[...] += nn(dl.T.astype(bf16), expert_in)
    norm_acc[2] += eight_rows(dc * normed)
    norm_acc[3] += eight_rows(dc)
    dx1 = jnp.where(real, cot_ref[0].astype(f32), 0.0) + norm_back(dc, normed, inverse, gains[2:3])
    low = dx1.astype(bf16)
    turned = turned_ref[0]
    grads[:, 3 * width :] += nn(turned, low)
    out_proj = weights[:, 3 * width : 4 * width]
    d_out = nt(low, out_proj).astype(bf16)
    d_out_t = nt(out_proj, low).astype(bf16)
    shared = d_out_t.astype(f32) * turned.astype(f32)

    qkv = qkv_ref[0]
    scale = HEAD_DIM ** (-0.5)
    half = iota((PAD, 128), 1) < HEAD_DIM
    dq, dk, dv = [], [], []
    for pair in range(HEADS // 2):
        at = pair * 128
        query = qkv[:, at : at + 128]
        keys = qkv[:, width + at : width + at + 128]
        values = qkv[:, 2 * width + at : 2 * width + at + 128]
        keys_t = keys.astype(f32).T.astype(bf16)
        do = d_out[:, at : at + 128]
        do_t = d_out_t[at : at + 128]
        zero = jnp.zeros_like(query)
        dq_t = []
        dk_sum = jnp.zeros((PAD, 128), f32)
        dv_sum = jnp.zeros((PAD, 128), f32)
        for head in range(2):
            mask = half if head == 0 else ~half
            low_at = at + head * HEAD_DIM
            probs = probs_ref[0, 2 * pair + head]
            dp = nn(jnp.where(mask, values, zero), do_t)
            center = jnp.sum(shared[low_at : low_at + HEAD_DIM], axis=0, keepdims=True)
            ds = (probs.astype(f32) * (dp - center)).astype(bf16)
            dk_sum += nn(ds, jnp.where(mask, query, zero))
            dv_sum += nn(probs, jnp.where(mask, do, zero))
            dq_t.append(nn(keys_t[head * HEAD_DIM : (head + 1) * HEAD_DIM], ds))
        dq.append((jnp.concatenate(dq_t, axis=0).T * scale).astype(bf16))
        dk.append((dk_sum * scale).astype(bf16))
        dv.append(dv_sum.astype(bf16))
    dqkv = jnp.concatenate(dq + dk + dv, axis=1)
    inputs = x_ref[0].astype(f32)
    normed_one, inverse_one = normalize(inputs)
    rows_in = normed_one * gains[0:1] + gains[1:2]
    grads[:, : 3 * width] += nn(rows_in.T.astype(bf16), dqkv)
    da = nt(dqkv, weights[:, : 3 * width])
    norm_acc[0] += eight_rows(da * normed_one)
    norm_acc[1] += eight_rows(da)
    grad_ref[0] = dx1 + norm_back(da, normed_one, inverse_one, gains[0:1])

    @pl.when(step == pl.num_programs(0) - 1)
    def _():
        if not closing:
            return
        rows = pieces[0].shape[0]
        row = iota((128, width), 0)
        misc = router_acc[...]
        for i in range(4):
            misc = jnp.where(
                row == experts + i, jnp.sum(norm_acc[i], axis=0, keepdims=True), misc
            )
        table[...] = misc
        extra = table[...].T
        weights[:, : 4 * width] = grads[...].astype(bf16)
        weights[:, 4 * width :] = extra.astype(bf16)
        for k in range(group):
            start = pl.multiple_of(jnp.bitwise_xor(me_ref[0], k) * rows, 16)
            target = keep_ref if k % 2 == 0 else send_ref
            target[k // 2] = weights[pl.ds(start, rows), :]


def home(me, pos, cot, x, saved, pieces, slots, after, carried, start, closing, experts):
    mid, qkv, probs, turned, gates = saved
    group, blocks = len(pieces), len(slots)
    count = GROUP
    width = x.shape[2]
    rows, columns = pieces[0].shape
    stride = slots[0].shape[0]
    wide = blocks * stride

    def take(*tail):
        return pl.BlockSpec((1,) + tail, lambda i: (i + start,) + (0,) * len(tail))

    sums = [sds((width, 4 * width), f32), sds((128, width), f32), sds((4, 8, width), f32)]
    if closing:
        last = [sds((group // 2, rows, columns), bf16)] * 2
    else:
        last = sums
    return pl.pallas_call(
        functools.partial(
            home_kernel, experts, group, blocks, len(after), carried is None, closing
        ),
        grid=(count,),
        out_shape=[sds(x.shape[:2] + (width,), f32)] + last,
        in_specs=[
            SCALAR,
            take(PAD, 128),
            take(PAD, 128),
            take(PAD, width),
            take(PAD, width),
            take(PAD, width),
            take(PAD, 3 * width),
            take(HEADS, PAD, PAD),
            take(width, PAD),
        ]
        + [WHOLE] * (group + blocks)
        + [ANY] * len(after)
        + ([] if carried is None else [WHOLE] * 3 + [ANY]),
        out_specs=[take(PAD, width)] + [WHOLE] * len(last),
        input_output_aliases={} if carried is None else {12 + group + blocks + len(after): 0},
        scratch_shapes=[
            VMEM((width, columns), bf16),
            VMEM((128, width), f32),
            VMEM((wide, width), bf16),
            VMEM((8, wide), f32),
        ]
        + ([VMEM(value.shape, f32) for value in sums] if closing else []),
        compiler_params=params(32),
        cost_estimate=cost(6 * count),
        name="home",
    )(me, pos, gates, x, cot, mid, qkv, probs, turned, *pieces, *slots, *after, *(carried or ()))


def finish_kernel(blocks, *refs):
    pos_ref, gate_ref, mid_ref = refs[:3]
    slots = refs[3 : 3 + blocks]
    out_ref, buffer = refs[-2:]

    @pl.when(pl.program_id(0) == 0)
    def _():
        load_slots(slots, buffer)

    pos, gates = pos_ref[0], gate_ref[0]
    lane = iota((PAD, buffer.shape[0]), 1).astype(f32)
    total = mid_ref[0]
    for j in range(2):
        pick = jnp.where(lane == pos[:, j : j + 1], 1.0, 0.0).astype(bf16)
        total += gates[:, j : j + 1] * nn(pick, buffer[...])
    out_ref[0] = total.astype(bf16)


def finish(pos, saved, slots, after):
    mid, gates = saved[0], saved[4]
    count, _, width = mid.shape
    blocks = len(slots)
    stride = slots[0].shape[0]

    def take(*tail):
        return pl.BlockSpec((1,) + tail, lambda i: (i,) + (0,) * len(tail))

    return pl.pallas_call(
        functools.partial(finish_kernel, blocks),
        grid=(count,),
        out_shape=sds((count, PAD, width), bf16),
        in_specs=[
            take(PAD, 128),
            take(PAD, 128),
            take(PAD, width),
        ]
        + [WHOLE] * blocks
        + [ANY] * len(after),
        out_specs=take(PAD, width),
        scratch_shapes=[VMEM((blocks * stride, width), bf16)],
        compiler_params=params(24),
        cost_estimate=cost(2 * count),
        name="finish",
    )(pos, gates, mid, *slots, *after)


def dense_kernel(side_ref, own_ref, other_ref, *refs):
    attn, router, norm = refs[:3], refs[3:6], refs[6:9]
    attn_out, router_out, norm_out, sum_ref = refs[9:13], refs[13:17], refs[17:21], refs[21]
    count = own_ref.shape[0]
    for half, ref in enumerate((own_ref, other_ref)):
        at = pl.multiple_of(jnp.bitwise_xor(side_ref[0], half) * count, 8)
        sum_ref[pl.ds(at, count), :] = ref[...].astype(f32)
    width = attn[0].shape[2]
    count = router[0].shape[0]
    for index in range(4):
        grad = sum_ref[:, index * width : (index + 1) * width]
        new = adamw(*(ref[index] for ref in attn), grad, rate_matrix, decay_rate)
        for ref, value in zip(attn_out, (grad,) + new):
            ref[index] = value
    extra = sum_ref[:, 4 * width :].T
    grad = extra[:count]
    new = adamw(*(ref[...] for ref in router), grad, rate_matrix, decay_rate)
    for ref, value in zip(router_out, (grad,) + new):
        ref[...] = value
    grad = extra[count : count + 4]
    new = adamw(*(ref[...] for ref in norm), grad, rate_vector, 0.0)
    for ref, value in zip(norm_out, (grad,) + new):
        ref[...] = value


def dense_update(side, halves, attn, router, norm):
    shapes = [sds(group[0].shape, f32) for group in (attn, router, norm) for _ in range(4)]
    return pl.pallas_call(
        dense_kernel,
        out_shape=shapes,
        in_specs=[SCALAR] + [WHOLE] * 11,
        out_specs=[WHOLE] * 12,
        scratch_shapes=[VMEM((2 * halves[0].shape[0], halves[0].shape[1]), f32)],
        compiler_params=params(16),
        cost_estimate=cost(3),
        name="dense_update",
    )(side, *halves, *attn, *router, *norm)


def expert_update_kernel(parts, *refs):
    state, sources, outs = refs[:3], refs[3:-4], refs[-4:]
    for e in range(state[0].shape[0]):
        grad = sum(ref[0].astype(f32) for ref in sources[e * parts : (e + 1) * parts])
        new = adamw(*(ref[e, 0] for ref in state), grad, rate_matrix, decay_rate)
        for ref, value in zip(outs, (grad,) + new):
            ref[e, 0] = value


def expert_update(parts, weight, first, second):
    local, _, hidden, width = weight.shape
    block = pl.BlockSpec((local, 1, hidden, width), lambda m: (0, m, 0, 0))
    part = pl.BlockSpec((1, hidden, width), lambda m: (m, 0, 0))
    flat = [value for own in parts for value in own]
    return pl.pallas_call(
        functools.partial(expert_update_kernel, len(parts[0])),
        grid=(2,),
        out_shape=[sds(weight.shape, f32)] * 4,
        in_specs=[block] * 3 + [part] * len(flat),
        out_specs=[block] * 4,
        compiler_params=params(60),
        cost_estimate=cost(4),
        name="expert_update",
    )(weight, first, second, *flat)


def swap(value, axis, size, bit):
    return lax.ppermute(value, axis, [(i, i ^ bit) for i in range(size)])


def ring_list(size):
    half = size // 2
    return [2 * i for i in range(half)] + [2 * i + 1 for i in reversed(range(half))]


def turn(value, size, by):
    order = ring_list(size)
    pairs = [(order[i], order[(i + by) % size]) for i in range(size)]
    return lax.ppermute(value, "rep", pairs)


def relay_kernel(*refs):
    pass


def tie(values, *others):
    values = list(values)
    return pl.pallas_call(
        relay_kernel,
        out_shape=[sds(value.shape, value.dtype) for value in values],
        in_specs=[ANY] * (len(values) + len(others)),
        out_specs=[ANY] * len(values),
        input_output_aliases={i: i for i in range(len(values))},
        compiler_params=params(1),
        cost_estimate=cost(0),
        name="relay",
    )(*values, *others)


def spread_far(value, size):
    held = {0: value}
    bit = size // 2
    while bit > 1:
        for k in list(held):
            held[k ^ bit] = swap(held[k], "shard", size, bit)
        bit //= 2
    return [held[k] for k in range(0, size, 2)]


def spread_near(values, size):
    both = [(value, swap(value, "shard", size, 1)) for value in values]
    return [value for pair in both for value in pair]


def ring_gather(value, size):
    half = size // 2
    held = [None] * size
    held[0] = value
    others = []
    ahead = behind = value
    for hop in range(1, half):
        if others:
            ahead, behind = tie([ahead, behind], *others)
            held[size - hop + 1], held[hop - 1] = ahead, behind
        ahead, behind = turn(ahead, size, 1), turn(behind, size, -1)
        held[size - hop], held[hop] = ahead, behind
        others = (yield [ahead, behind]) or []
    yield held


def ring_opposite(held, size, rows):
    half = size // 2
    result, opposite = [], []
    for e in range(held[0].shape[1]):
        last = [held[half + 1][0, e], held[half - 1][1, e]]
        if opposite:
            last = tie(last, *opposite, rows)
        opposite = [turn(last[0], size, 1), turn(last[1], size, -1)]
        result.append(held[:half] + opposite + held[half + 1 :])
    return result


def ring_add_kernel(ahead, first, behind, second, *refs):
    out_a, out_b = refs[-2:]
    if len(first.shape) == len(ahead.shape):
        out_a[...] = (ahead[...].astype(f32) + first[...].astype(f32)).astype(bf16)
        out_b[...] = (behind[...].astype(f32) + second[...].astype(f32)).astype(bf16)
    else:
        out_a[0] = (ahead[0].astype(f32) + first[...].astype(f32)).astype(bf16)
        out_a[1] = ahead[1]
        out_b[0] = behind[0]
        out_b[1] = (behind[1].astype(f32) + second[...].astype(f32)).astype(bf16)


def ring_add(ahead, first, behind, second, after):
    return pl.pallas_call(
        ring_add_kernel,
        out_shape=[sds(ahead.shape, bf16)] * 2,
        in_specs=[WHOLE] * 4 + [ANY] * len(after),
        out_specs=[WHOLE] * 2,
        compiler_params=params(16),
        cost_estimate=cost(0),
        name="ring_add",
    )(ahead, first, behind, second, *after)


def ring_sum(grads, size, formed):
    half = size // 2
    full = grads[:half] + [None] + grads[half + 2 :]
    sums = grads[half : half + 2]
    for hop in range(half, 0, -1):
        moving = [turn(sums[0], size, 1), turn(sums[1], size, -1)]
        if hop > 1:
            others = (yield moving) or []
            sums = ring_add(full[hop - 1], moving[0], full[size - hop + 1], moving[1], others)
            formed.extend(sums)
    yield [full[0]] + moving


def add(left, right):
    return (left.astype(f32) + right.astype(f32)).astype(bf16)


def shards(
    tokens,
    routes,
    cotangent,
    attn_weights,
    attn_first,
    attn_second,
    router_weights,
    router_first,
    router_second,
    norm_params,
    norm_first,
    norm_second,
    expert_weights,
    expert_first,
    expert_second,
    *,
    group,
    ring,
):
    tok_count, width = tokens.shape
    experts = router_weights.shape[1]
    local = expert_weights.shape[0]
    capacity = min(tok_count, (tok_count * 8 // (3 * experts) + 7) // 8 * 8)
    stride = -(-(capacity + 8) // 16) * 16
    images = tok_count // SEQ
    me = lax.axis_index("shard").astype(jnp.int32).reshape(1)

    packed, low = pack(attn_weights, router_weights.T, norm_params, expert_weights)
    gathering = ring_gather(low, ring)
    hop = next(gathering)
    pieces = spread_far(packed, group)
    x, cot, pos = stage(me, tokens, cotangent, routes, packed, images, local, group, stride)

    second = next(gathering)
    cots = spread_far(cot, group)
    pieces = spread_near(tie(pieces, pos), group)
    c, *saved = front(me, x, cot, pieces, experts, hop)
    c = tie([c], *second)[0]

    cs = spread_far(c, group)
    gathering.send([c])
    cots = tie(cots, c)
    cot = cots[0]
    cot_slots, places = gather_grads(me, spread_near(cots, group), local, stride)
    cs = spread_near(tie(cs, places), group)
    held = list(gathering)[-1]
    rows, outs = gather_rows(places, cot_slots, cs)
    shards = ring_opposite(held, ring, rows)

    back, made, summing, formed = [], [], [], []
    after, latest = [], []

    def send_back(blocks):
        return [v if k == 0 else swap(v, "shard", group, k) for k, v in enumerate(blocks)]

    def start_sum(grads):
        formed.append([])
        summing.append(ring_sum(list(grads), ring, formed[-1]))
        latest.append(next(summing[-1]))

    def next_hop(at, others):
        latest[at] = summing[at].send(others)

    for e in range(local - 1):
        out = run_whole(e, rows, outs, shards[e], group)
        back += send_back(out[:group])
        made += out[group : 2 * group]
        start_sum(out[2 * group :])
        after = [out[2 * group]]
    early = list(back)
    out = run_first(local - 1, rows, outs, shards[-1], group, after)
    back += send_back(out[:group])
    kept = out[group:]
    for at in range(len(summing)):
        next_hop(at, [out[0]])
    after = early + [value for own in formed for value in own[-2:]]
    out = run_last(local - 1, rows, outs, kept, shards[-1], after, group)
    grads = out[group:]
    made = [v for at in range(0, len(made), group) for v in send_back(made[at : at + group])]
    for at in range(len(summing)):
        next_hop(at, [grads[0]])
    start_sum(grads)
    after = [grads[0]] + [value for own in formed for value in own[-2:]]

    grad, carried = None, None
    for start in range(0, images, GROUP):
        closing = start + GROUP >= images
        grad, *carried = home(
            me, pos, cot, x, saved, pieces, back, after, carried, start, closing, experts
        )
        if start == 0:
            gate = carried[1]
            carried.append(grad)
            for at in range(local):
                next_hop(at, [gate])
            after = [part for own in formed for part in own[-2:]] + made
            made = made + send_back(tie(out[:group], gate))
    keep, send = carried
    send = tie([send], *made, *latest[-1][-2:])[0]

    total = add(keep, swap(send, "shard", group, 1))
    next_hop(-1, [total])
    total = tie([total], *formed[-1][-2:])[0]
    bit = 2
    while bit < group:
        count = total.shape[0] // 2
        pairs = total.reshape(count, 2, *total.shape[1:])
        total = add(pairs[:, 0], swap(pairs[:, 1], "shard", group, bit))
        bit *= 2
    total = total[0]

    total = tie([total], *latest[-1][-2:])[0]
    side = lax.axis_index("rep") % 2
    count = total.shape[0] // 2
    own = lax.dynamic_slice_in_dim(total, side * count, count)
    other = lax.dynamic_slice_in_dim(total, (1 - side) * count, count)
    total = add(own, swap(other, "rep", ring, 1))
    bit = 2
    while bit < ring:
        total = add(total, swap(total, "rep", ring, bit))
        if bit == 2:
            next_hop(-1, [total])
            output = finish(pos, saved, made, [total])
        bit *= 2
    total = tie([total], *latest[-1][-2:])[0]
    for at in range(local):
        for latest[at] in summing[at]:
            pass
    halves = [total, swap(total, "rep", ring, 1)]
    dense = dense_update(
        side.astype(jnp.int32).reshape(1),
        halves,
        (attn_weights, attn_first, attn_second),
        (router_weights.T, router_first.T, router_second.T),
        (norm_params, norm_first, norm_second),
    )
    dense = [value.T if 4 <= i < 8 else value for i, value in enumerate(dense)]
    updated = expert_update(latest, expert_weights, expert_first, expert_second)

    def unpadded(rows):
        return rows[:, :SEQ].reshape(tok_count, width)

    return (unpadded(output), unpadded(grad), *dense, *updated)


def solution(mesh):
    rows = P(("shard", "rep"), None)
    attn = P(None, "shard", None)
    router = P("shard", None)
    norm = P(None, "shard")
    expert = P("shard", None, "rep", None)
    return jax.shard_map(
        functools.partial(shards, group=mesh.shape["shard"], ring=mesh.shape["rep"]),
        mesh=mesh,
        in_specs=(rows,) * 3 + (attn,) * 3 + (router,) * 3 + (norm,) * 3 + (expert,) * 3,
        out_specs=(rows,) * 2 + (attn,) * 4 + (router,) * 4 + (norm,) * 4 + (expert,) * 4,
        check_vma=False,
    )
```

```python
import functools

import jax
import jax.numpy as jnp
from jax import lax
from jax.experimental import pallas as pl
from jax.experimental.pallas import tpu as pltpu
from jax.sharding import PartitionSpec as P

HEADS = 6
HEAD_DIM = 64
SEQ = 197
PAD = 208
STEP = 10
GROUP = 2
CHUNK = 272
STEP_HIDDEN = 256

beta_one = 0.9
beta_two = 0.999
adam_floor = 1e-08
decay_rate = 0.1
rate_matrix = 0.05
rate_vector = 0.3
norm_floor = 1e-06

bf16 = jnp.bfloat16
f32 = jnp.float32
VMEM = pltpu.VMEM
ANY = pl.BlockSpec(memory_space=pl.ANY)
FAR = pl.BlockSpec(memory_space=pltpu.HBM)
WHOLE = pl.BlockSpec(memory_space=pltpu.VMEM)
SCALAR = pl.BlockSpec(memory_space=pltpu.SMEM)


def params(mebibytes):
    return pltpu.CompilerParams(vmem_limit_bytes=mebibytes << 20)


def sds(shape, dtype):
    return jax.ShapeDtypeStruct(shape, dtype)


def cost(time_us):
    return pl.CostEstimate(
        flops=time_us * 1_150_000_000, bytes_accessed=time_us * 1_000_000, transcendentals=0
    )


def nn(left, right):
    return lax.dot_general(left, right, (((1,), (0,)), ((), ())), preferred_element_type=f32)


def nt(left, right):
    return lax.dot_general(left, right, (((1,), (1,)), ((), ())), preferred_element_type=f32)


def iota(shape, dim):
    return lax.broadcasted_iota(jnp.int32, shape, dim)


def normalize(values):
    centred = values - jnp.mean(values, axis=-1, keepdims=True)
    inverse = lax.rsqrt(jnp.mean(centred * centred, axis=-1, keepdims=True) + norm_floor)
    return centred * inverse, inverse


def norm_back(grad_rows, normed, inverse, gain):
    scaled = grad_rows * gain
    inner = (
        scaled
        - jnp.mean(scaled, axis=-1, keepdims=True)
        - normed * jnp.mean(scaled * normed, axis=-1, keepdims=True)
    )
    return inner * inverse


def eight_rows(values):
    rows, cols = values.shape
    return jnp.sum(values.reshape(rows // 8, 8, cols), axis=0)


def adamw(weight, first, second, grad, rate, decay):
    first_new = beta_one * first + (1.0 - beta_one) * grad
    second_new = beta_two * second + (1.0 - beta_two) * grad * grad
    first_hat = first_new * (1.0 / (1.0 - beta_one**STEP))
    second_hat = second_new * (1.0 / (1.0 - beta_two**STEP))
    return (
        first_new,
        second_new,
        weight - rate * (first_hat / (jnp.sqrt(second_hat) + adam_floor) + decay * weight),
    )


def pack_kernel(attn, router_t, norm, expert, packed, low):
    for e in range(expert.shape[0]):
        for m in range(2):
            low[m, e] = expert[e, m].astype(bf16)
    width = attn.shape[2]
    for index in range(4):
        packed[:, index * width : (index + 1) * width] = attn[index].astype(bf16)
    count, rows = router_t.shape
    filler = jnp.zeros((128 - count - 4, rows), f32)
    block = jnp.concatenate([router_t[...], norm[...], filler], axis=0)
    packed[:, 4 * width :] = block.T.astype(bf16)


def pack(attn, router_t, norm, expert):
    _, rows, width = attn.shape
    local, _, hidden, _ = expert.shape
    return pl.pallas_call(
        pack_kernel,
        out_shape=[sds((rows, 4 * width + 128), bf16), sds((2, local, hidden, width), bf16)],
        in_specs=[WHOLE] * 4,
        out_specs=[WHOLE] * 2,
        compiler_params=params(60),
        cost_estimate=cost(2),
        name="pack",
    )(attn, router_t, norm, expert)


def stage_kernel(local, group, stride, me_ref, tok_ref, cot_ref, routes_ref, _, *refs):
    x_ref, sent_ref, pos_ref, wide_ref, route_ref = refs
    images, _, width = x_ref.shape
    count = tok_ref.shape[0]
    rows = images * PAD

    def cut(image):
        tail = jnp.zeros((PAD - SEQ, width), f32)
        return jnp.concatenate([wide_ref[image * SEQ : (image + 1) * SEQ, :], tail], axis=0)

    wide_ref[:count, :] = tok_ref[...].astype(f32)
    for image in range(images):
        x_ref[image] = cut(image).astype(bf16)

    route_ref[:count, :] = routes_ref[...].astype(f32)
    gap = jnp.full((PAD - SEQ, 2), -1.0, f32)
    parts = []
    for image in range(images):
        parts += [route_ref[image * SEQ : (image + 1) * SEQ, :], gap]
    routes = jnp.concatenate(parts, axis=0)
    one, two = routes[:, 0:1], routes[:, 1:2]
    lane = iota((rows, 128), 1).astype(f32)
    pick_one, pick_two = lane == one, lane == two
    mask = jnp.where(pick_one | pick_two, 1.0, 0.0).astype(bf16)
    lower = jnp.where(iota((rows, rows), 0) >= iota((rows, rows), 1), 1.0, 0.0).astype(bf16)
    seen = nn(lower, mask)
    ranks = [
        jnp.sum(jnp.where(pick, seen, 0.0), axis=1, keepdims=True) - 1.0
        for pick in (pick_one, pick_two)
    ]
    places = []
    for route, rank in zip((one, two), ranks):
        owner = jnp.floor(route * (1.0 / local))
        inner = route - owner * local
        other = jnp.bitwise_xor(owner.astype(jnp.int32), me_ref[0]).astype(f32)
        places.append(
            jnp.where(route < 0.0, -1.0, (inner * group + other) * stride + rank)
        )
    table = jnp.where(lane == 0.0, places[0], jnp.where(lane == 1.0, places[1], 0.0))
    table = jnp.where(lane == 2.0, one, jnp.where(lane == 3.0, two, table))
    pos_ref[...] = table.reshape(images, PAD, 128)
    for at, rank in enumerate(ranks):
        high = jnp.floor(rank * (1.0 / 16.0))
        table = jnp.where(lane == 4.0 + 2 * at, high, table)
        table = jnp.where(lane == 5.0 + 2 * at, rank - 16.0 * high, table)
    wide_ref[:count, :] = cot_ref[...].astype(f32)
    for image in range(images):
        turned = table[image * PAD : (image + 1) * PAD].T[:8]
        turned = jnp.where(iota((8, PAD), 0) < 2, 0.0, turned)
        meta = jnp.concatenate([turned, jnp.zeros((8, width - PAD), f32)], axis=1)
        body = cut(image)[: PAD - 8]
        sent_ref[image] = jnp.concatenate([body, meta], axis=0).astype(bf16)


def stage(me, tokens, cotangent, routes, after, images, local, group, stride):
    count, width = tokens.shape
    padded = -(-count // 8) * 8
    return pl.pallas_call(
        functools.partial(stage_kernel, local, group, stride),
        out_shape=[sds((images, PAD, width), bf16)] * 2 + [sds((images, PAD, 128), f32)],
        in_specs=[SCALAR, WHOLE, WHOLE, WHOLE, ANY],
        out_specs=[WHOLE] * 3,
        scratch_shapes=[VMEM((padded, width), f32), VMEM((padded, 2), f32)],
        compiler_params=params(24),
        cost_estimate=cost(5),
        name="stage",
    )(me, tokens, cotangent, routes, after)


def load_weights(me, pieces, weights, turned):
    rows = pieces[0].shape[0]
    for index, piece in enumerate(pieces):
        start = pl.multiple_of(jnp.bitwise_xor(me, index) * rows, 16)
        weights[pl.ds(start, rows), :] = piece[...]
    width = weights.shape[0]
    turned[...] = weights[:, 4 * width :].astype(f32).T


def front_kernel(experts, group, *refs):
    me_ref, x_ref, meta_ref = refs[:3]
    pieces = refs[3 : 3 + group]
    sent_ref, mid_ref, qkv_ref, probs_ref, turned_ref, gate_ref, weights, table = refs[-8:]
    width = weights.shape[0]

    @pl.when(pl.program_id(0) == 0)
    def _():
        load_weights(me_ref[0], pieces, weights, table)

    inputs = x_ref[0].astype(f32)
    normed, _ = normalize(inputs)
    gains = table[experts : experts + 4]
    rows_in = (normed * gains[0:1] + gains[1:2]).astype(bf16)
    qkv = nn(rows_in, weights[:, : 3 * width]).astype(bf16)
    qkv_ref[0] = qkv
    half = iota((PAD, 128), 1) < HEAD_DIM
    real = iota((PAD, PAD), 0) < SEQ
    scale = HEAD_DIM ** (-0.5)
    joined = []
    for pair in range(HEADS // 2):
        at = pair * 128
        query = qkv[:, at : at + 128]
        keys = qkv[:, width + at : width + at + 128]
        values = qkv[:, 2 * width + at : 2 * width + at + 128].astype(f32).T.astype(bf16)
        parts = []
        for head in range(2):
            own = jnp.where(half if head == 0 else ~half, keys, jnp.zeros_like(keys))
            scores = jnp.where(real, nt(own, query) * scale, -1e30)
            expd = jnp.exp(scores - jnp.max(scores, axis=0, keepdims=True))
            probs = (expd * (1.0 / jnp.sum(expd, axis=0, keepdims=True))).astype(bf16)
            probs_ref[0, 2 * pair + head] = probs
            parts.append(nn(values[head * HEAD_DIM : (head + 1) * HEAD_DIM], probs))
        both = jnp.concatenate(parts, axis=0)
        turned_ref[0, at : at + 128, :] = both.astype(bf16)
        joined.append(both.T.astype(bf16))
    attended = jnp.concatenate(joined, axis=1)
    middle = inputs + nn(attended, weights[:, 3 * width : 4 * width])
    mid_ref[0] = middle
    normed_two, _ = normalize(middle)
    expert_in = (normed_two * gains[2:3] + gains[3:4]).astype(bf16)
    logits = nt(table[:16].astype(bf16), expert_in)
    meta = meta_ref[0][PAD - 16 :].astype(f32)[8:, :PAD]
    row = iota((16, PAD), 0).astype(f32)
    picked = [
        jnp.sum(jnp.where(row == meta[2 + j : 3 + j], logits, 0.0), axis=0, keepdims=True)
        for j in range(2)
    ]
    top = jnp.maximum(picked[0], picked[1])
    exps = [jnp.exp(value - top) for value in picked]
    total = exps[0] + exps[1]
    row8 = iota((8, PAD), 0)
    gates = jnp.where(row8 == 0, exps[0] / total, jnp.where(row8 == 1, exps[1] / total, 0.0))
    gate_ref[0] = jnp.concatenate([gates, jnp.zeros((120, PAD), f32)], axis=0).T
    gap = picked[0] - picked[1]
    high = gap.astype(bf16).astype(f32)
    meta = jnp.where(row8 == 0, high, jnp.where(row8 == 1, gap - high, 0.0))
    meta = jnp.concatenate([meta, jnp.zeros((8, width - PAD), f32)], axis=1)
    sent_ref[0] = jnp.concatenate([expert_in.astype(f32)[: PAD - 8], meta], axis=0).astype(bf16)


def front(me, x, cot, pieces, experts, after):
    width = x.shape[2]
    count = x.shape[0]
    group = len(pieces)
    columns = pieces[0].shape[1]

    def take(*tail):
        return pl.BlockSpec((1,) + tail, lambda i: (i,) + (0,) * len(tail))

    give = take

    return pl.pallas_call(
        functools.partial(front_kernel, experts, group),
        grid=(count,),
        out_shape=[
            sds((count, PAD, width), bf16),
            sds((count, PAD, width), f32),
            sds((count, PAD, 3 * width), bf16),
            sds((count, HEADS, PAD, PAD), bf16),
            sds((count, width, PAD), bf16),
            sds((count, PAD, 128), f32),
        ],
        in_specs=[SCALAR, take(PAD, width), take(PAD, width)]
        + [WHOLE] * group
        + [ANY] * len(after),
        out_specs=[
            give(PAD, width),
            give(PAD, width),
            give(PAD, 3 * width),
            give(HEADS, PAD, PAD),
            give(width, PAD),
            give(PAD, 128),
        ],
        scratch_shapes=[
            VMEM((width, columns), bf16),
            VMEM((128, width), f32),
        ],
        compiler_params=params(28),
        cost_estimate=cost(3 * count),
        name="front",
    )(me, x, cot, *pieces, *after)


def gather_grads_kernel(local, stride, *refs):
    refs = list(refs)
    me_ref, *grads = refs[:-2]
    out_ref, place_ref = refs[-2:]
    group = len(grads)
    images, _, width = grads[0].shape
    first = me_ref[0] * local
    slot = iota((stride, PAD), 0).astype(f32)
    row8 = iota((8, PAD), 0)
    for k in range(group):
        sums = jnp.zeros((local * stride, width), f32)
        for image in range(images):
            block = grads[k][image]
            meta = block[PAD - 16 :].astype(f32)[8:, :PAD]
            ranks = [16.0 * meta[4 + 2 * j : 5 + 2 * j] + meta[5 + 2 * j : 6 + 2 * j] for j in range(2)]
            picks = []
            table = jnp.zeros((8, PAD), f32)
            for e in range(local):
                expert = (first + e).astype(f32)
                is_one, is_two = meta[2:3] == expert, meta[3:4] == expert
                place = jnp.where(is_one, ranks[0], jnp.where(is_two, ranks[1], -1.0))
                picks.append(jnp.where(slot == place, 1.0, 0.0).astype(bf16))
                table = jnp.where(row8 == e, place, table)
                table = jnp.where(row8 == 4 + e, jnp.where(is_one, 1.0, 0.0), table)
            place_ref[k, image] = jnp.concatenate([table, jnp.zeros((8, 256 - PAD), f32)], axis=1)
            sums += nn(jnp.concatenate(picks, axis=0), block)
        for e in range(local):
            out_ref[e, k * stride : (k + 1) * stride, :] = sums[
                e * stride : (e + 1) * stride
            ].astype(bf16)


def gather_grads(me, grads, local, stride):
    group = len(grads)
    images, _, width = grads[0].shape
    return pl.pallas_call(
        functools.partial(gather_grads_kernel, local, stride),
        out_shape=[
            sds((local, group * stride, width), bf16),
            sds((group, images, 8, 256), f32),
        ],
        in_specs=[SCALAR] + [WHOLE] * group,
        out_specs=[WHOLE] * 2,
        compiler_params=params(22),
        cost_estimate=cost(6),
        name="gather_grads",
    )(me, *grads)


def gather_rows_kernel(local, stride, *refs):
    refs = list(refs)
    place_ref, grad_ref, *tokens = refs[:-2]
    rows_ref, outs_ref = refs[-2:]
    group = len(tokens)
    images, _, width = tokens[0].shape
    slot = iota((stride, PAD), 0).astype(f32)
    for k in range(group):
        sums = jnp.zeros((local * stride, width), f32)
        gate_sum = jnp.zeros((local * stride, PAD), f32)
        for image in range(images):
            block = tokens[k][image]
            meta = block[PAD - 16 :].astype(f32)[8:, :PAD]
            gap = meta[0:1] + meta[1:2]
            top = jnp.maximum(gap, 0.0)
            left, right = jnp.exp(gap - top), jnp.exp(-top)
            inverse = 1.0 / (left + right)
            table = place_ref[k, image][:, :PAD]
            picks, weighted = [], []
            for e in range(local):
                match = slot == table[e : e + 1]
                gate = jnp.where(table[4 + e : 5 + e] > 0.0, left, right) * inverse
                picks.append(jnp.where(match, 1.0, 0.0).astype(bf16))
                weighted.append(jnp.where(match, gate, 0.0))
            sums += nn(jnp.concatenate(picks, axis=0), block)
            gate_sum += jnp.concatenate(weighted, axis=0)
        gate = jnp.sum(gate_sum, axis=1, keepdims=True)
        part = slice(k * stride, (k + 1) * stride)
        for e in range(local):
            mine = slice(e * stride, (e + 1) * stride)
            rows_ref[e, part, :] = sums[mine].astype(bf16)
            outs_ref[e, part, :] = (grad_ref[e, part, :].astype(f32) * gate[mine]).astype(bf16)


def gather_rows(places, grads, tokens):
    local, slots, width = grads.shape
    group = len(tokens)
    images = tokens[0].shape[0]
    return pl.pallas_call(
        functools.partial(gather_rows_kernel, local, slots // group),
        out_shape=[sds((local, slots, width), bf16)] * 2,
        in_specs=[WHOLE] * (2 + group),
        out_specs=[WHOLE] * 2,
        compiler_params=params(22),
        cost_estimate=cost(6),
        name="gather_rows",
    )(places, grads, *tokens)


def shard_views(shards):
    half = (len(shards) - 1) // 2
    views = [[ref.at[0], ref.at[1]] for ref in shards[:half]]
    views.append([shards[half], shards[half + 1]])
    return views + [[ref.at[0], ref.at[1]] for ref in shards[half + 2 :]]


def assemble(shards, index, mats, first):
    hidden = mats.shape[1] // len(shards)
    for r, shard in enumerate(shards):
        for m in range(first, 2):
            whole = len(shard[m].shape) == 2
            mats[m - first, r * hidden : (r + 1) * hidden, :] = (
                shard[m][...] if whole else shard[m][index]
            )


def expert_back(index, rows, outs, mats, moment, act_s, down_s, back_out, finished):
    steps, slots, step = act_s.shape
    stride = slots // len(back_out)
    width = mats.shape[2]
    k0 = 0.7978845608028654
    k1 = 0.044715
    for i in range(steps):
        for k in range(len(back_out)):
            part = slice(k * stride, (k + 1) * stride)
            partial = None
            for at in range(0, step, 256):
                own = slice(i * step + at, i * step + at + 256)
                pre = nt(rows[index, part, :], mats[0, own, :])
                back = nt(outs[index, part, :], mats[1, own, :])
                square = pre * pre
                tanh = jnp.tanh(pre * (k0 + (k0 * k1) * square))
                half = 0.5 + 0.5 * tanh
                act = pre * half
                slope = half + (2.0 * act) * (1.0 - half) * (k0 + (3.0 * k0 * k1) * square)
                both = act * back
                both = both[:, :128] + both[:, 128:]
                act_s[i, part, at : at + 256] = act.astype(bf16)
                down_s[i, part, at : at + 256] = (back * slope).astype(bf16)
                partial = both if partial is None else partial + both
            if i == 0:
                moment[part, :] = partial
            else:
                moment[part, :] += partial
        finished(i)

    wide = -(-slots // 128) * 128
    row8 = iota((8, slots), 0)
    inside = iota((8, width), 1) < stride - 8
    sums = jnp.sum(moment[...].T, axis=0, keepdims=True)
    high = sums.astype(bf16).astype(f32)
    table = jnp.where(row8 == 0, high, jnp.where(row8 == 1, sums - high, 0.0))
    if wide > slots:
        table = jnp.concatenate([table, jnp.zeros((8, wide - slots), f32)], axis=1)
    for k, out in enumerate(back_out):
        part = slice(k * stride, (k + 1) * stride)
        gone = sum(
            nn(down_s[i, part, :], mats[0, i * step : (i + 1) * step, :]) for i in range(steps)
        )
        here = table if k == 0 else pltpu.roll(table, wide - k * stride, 1)
        here = jnp.where(inside, here[:, :width], 0.0)
        out[...] = jnp.concatenate([gone[: stride - 8], here], axis=0).astype(bf16)


def expert_ends(index, rows, outs, second, act, down, grads, made_out, grad_out, sem, before):
    steps, slots, step = act.shape
    stride = slots // len(made_out)
    hidden = steps * step // len(grad_out)
    copies = [
        [
            pltpu.make_async_copy(
                grads.at[m, pl.ds(r * hidden, hidden)], grad_out[r][m], sem.at[r, m]
            )
            for m in range(2)
        ]
        for r in range(len(grad_out))
    ]
    rows_t = rows[index].astype(f32).T.astype(bf16)
    outs_t = outs[index].astype(f32).T.astype(bf16)
    sent = 0
    for i in range(steps):
        at = i * step
        before(i)
        grads[0, at : at + step, :] = nn(rows_t, down[i]).T.astype(bf16)
        grads[1, at : at + step, :] = nn(outs_t, act[i]).T.astype(bf16)
        while (sent + 1) * hidden <= at + step:
            for copy in copies[sent]:
                copy.start()
            sent += 1
    for k, out in enumerate(made_out):
        part = slice(k * stride, (k + 1) * stride)
        made = sum(
            nn(act[i, part, :], second[i * step : (i + 1) * step, :]) for i in range(steps)
        )
        out[...] = made.astype(bf16)
    for pair in copies:
        for copy in pair:
            copy.wait()


def expert_all_kernel(index, group, count, *refs):
    refs = list(refs)
    rows, outs = refs[:2]
    shards, refs = shard_views(refs[2 : 2 + count]), refs[2 + count :]
    back_out, made_out, refs = refs[:group], refs[group : 2 * group], refs[2 * group :]
    grad_out, refs = shard_views(refs[:count]), refs[count:]
    mats, moment, act_s, down_s, grads, sem = refs
    assemble(shards, index, mats, 0)
    expert_back(index, rows, outs, mats, moment, act_s, down_s, back_out, lambda i: None)
    expert_ends(
        index, rows, outs, mats.at[1], act_s, down_s, grads, made_out, grad_out, sem, lambda i: None
    )


def expert_back_kernel(index, group, count, *refs):
    refs = list(refs)
    rows, outs = refs[:2]
    shards, refs = shard_views(refs[2 : 2 + count]), refs[2 + count :]
    back_out, act_s, down_s, mats, moment = (refs[-4 - group : -4], *refs[-4:])
    assemble(shards, index, mats, 0)
    expert_back(index, rows, outs, mats, moment, act_s, down_s, back_out, lambda i: None)


def expert_ends_kernel(index, group, count, *refs):
    refs = list(refs)
    rows, outs, act, down = refs[:4]
    shards, refs = shard_views(refs[4 : 4 + count]), refs[4 + count :]
    second, grads, sem = refs[-3:]
    grad_out = shard_views(refs[-3 - count : -3])
    made_out = refs[-3 - count - group : -3 - count]
    assemble(shards, index, second, 1)
    expert_ends(
        index, rows, outs, second.at[0], act, down, grads, made_out, grad_out, sem, lambda i: None
    )


def expert_shapes(rows, shards, group):
    _, slots, width = rows.shape
    hidden = shards[0].shape[2]
    total = (len(shards) - 1) * hidden
    step = 512 if total % 512 == 0 else 256
    half = (len(shards) - 1) // 2
    grads = [sds(((2, hidden, width)), bf16)] * half + [sds((hidden, width), bf16)] * 2
    grads += [sds(((2, hidden, width)), bf16)] * (half - 1)
    grads = [pltpu.HBM(value.shape, bf16) for value in grads]
    return slots // group, total, (total // step, slots, step), grads


def run_whole(index, rows, outs, shards, group):
    stride, total, kept, grads = expert_shapes(rows, shards, group)
    _, slots, width = rows.shape
    count = len(shards)
    return pl.pallas_call(
        functools.partial(expert_all_kernel, index, group, count),
        out_shape=[sds((stride, width), bf16)] * (2 * group) + grads,
        in_specs=[WHOLE] * (2 + count),
        out_specs=[WHOLE] * (2 * group) + [ANY] * count,
        scratch_shapes=[
            VMEM((2, total, width), bf16),
            VMEM((slots, 128), f32),
            VMEM(kept, bf16),
            VMEM(kept, bf16),
            VMEM((2, total, width), bf16),
            pltpu.SemaphoreType.DMA((count - 1, 2)),
        ],
        compiler_params=params(32),
        cost_estimate=cost(14),
        name="expert_all",
    )(rows, outs, *shards)


def run_first(index, rows, outs, shards, group, after):
    stride, total, kept, _ = expert_shapes(rows, shards, group)
    _, slots, width = rows.shape
    count = len(shards)
    return pl.pallas_call(
        functools.partial(expert_back_kernel, index, group, count),
        out_shape=[sds((stride, width), bf16)] * group + [sds(kept, bf16)] * 2,
        in_specs=[WHOLE] * (2 + count) + [ANY] * len(after),
        out_specs=[WHOLE] * (group + 2),
        scratch_shapes=[VMEM((2, total, width), bf16), VMEM((slots, 128), f32)],
        compiler_params=params(24),
        cost_estimate=cost(9),
        name="expert_first",
    )(rows, outs, *shards, *after)


def run_last(index, rows, outs, kept, shards, after, group):
    stride, total, shape, grads = expert_shapes(rows, shards, group)
    width = rows.shape[2]
    count = len(shards)
    return pl.pallas_call(
        functools.partial(expert_ends_kernel, index, group, count),
        out_shape=[sds((stride, width), bf16)] * group + grads,
        in_specs=[WHOLE] * (4 + count) + [ANY] * len(after),
        out_specs=[WHOLE] * group + [ANY] * count,
        scratch_shapes=[
            VMEM((1, total, width), bf16),
            VMEM((2, total, width), bf16),
            pltpu.SemaphoreType.DMA((count - 1, 2)),
        ],
        compiler_params=params(24),
        cost_estimate=cost(8),
        name="expert_last",
    )(rows, outs, *kept, *shards, *after)


def load_slots(blocks, buffer):
    stride = blocks[0].shape[0]
    for i, block in enumerate(blocks):
        buffer[i * stride : (i + 1) * stride, :] = block[...]


def home_kernel(experts, group, blocks, extra, opening, closing, *refs):
    refs = list(refs)
    me_ref, pos_ref, gate_ref, x_ref, cot_ref, mid_ref, qkv_ref, probs_ref, turned_ref = refs[:9]
    refs = refs[9:]
    pieces, refs = refs[:group], refs[group:]
    slots, refs = refs[:blocks], refs[blocks:]
    refs = refs[extra:]
    if not opening:
        carried, refs = refs[:3], refs[4:]
    grad_ref, refs = refs[0], refs[1:]
    if closing:
        keep_ref, send_ref = refs[:2]
        refs = refs[2:]
    else:
        carry, refs = refs[:3], refs[3:]
    weights, table, buffer, moments = refs[:4]
    sums = refs[4:] if closing else carry
    grads, router_acc, norm_acc = sums
    width = weights.shape[0]
    stride = slots[0].shape[0]
    wide = buffer.shape[0]
    step = pl.program_id(0)

    @pl.when(step == 0)
    def _():
        load_slots(slots, buffer)
        load_weights(me_ref[0], pieces, weights, table)
        for i, ref in enumerate(sums):
            ref[...] = jnp.zeros_like(ref) if opening else carried[i][...]
        total = jnp.zeros((8, wide), f32)
        for i in range(blocks):
            tail = buffer[(i + 1) * stride - 16 : (i + 1) * stride, :].astype(f32)[8:]
            tail = jnp.concatenate([tail, jnp.zeros((8, wide - width), f32)], axis=1)
            total += tail if i == 0 else pltpu.roll(tail, i * stride, 1)
        moments[...] = total

    real = iota((PAD, 1), 0) < SEQ
    gains = table[experts : experts + 4]
    pos = pos_ref[0]
    gates = gate_ref[0]
    lane = iota((PAD, wide), 1).astype(f32)
    match_one = lane == pos[:, 0:1]
    match_two = lane == pos[:, 1:2]
    pick = jnp.where(match_one | match_two, 1.0, 0.0).astype(bf16)
    moment = moments[0:1] + moments[1:2]
    moment_one = jnp.sum(jnp.where(match_one, moment, 0.0), axis=1, keepdims=True)
    moment_two = jnp.sum(jnp.where(match_two, moment, 0.0), axis=1, keepdims=True)
    dz = gates[:, 1:2] * moment_one - gates[:, 0:1] * moment_two
    lane = iota((PAD, 128), 1).astype(f32)
    dl = jnp.where(lane == pos[:, 2:3], dz, jnp.where(lane == pos[:, 3:4], -dz, 0.0))
    middle = mid_ref[0]
    normed, inverse = normalize(middle)
    expert_in = (normed * gains[2:3] + gains[3:4]).astype(bf16)
    dc = nn(pick, buffer[...]) + nn(dl.astype(bf16), table[...].astype(bf16))
    router_acc[...] += nn(dl.T.astype(bf16), expert_in)
    norm_acc[2] += eight_rows(dc * normed)
    norm_acc[3] += eight_rows(dc)
    dx1 = jnp.where(real, cot_ref[0].astype(f32), 0.0) + norm_back(dc, normed, inverse, gains[2:3])
    low = dx1.astype(bf16)
    turned = turned_ref[0]
    grads[:, 3 * width :] += nn(turned, low)
    out_proj = weights[:, 3 * width : 4 * width]
    d_out = nt(low, out_proj).astype(bf16)
    d_out_t = nt(out_proj, low).astype(bf16)
    shared = d_out_t.astype(f32) * turned.astype(f32)

    qkv = qkv_ref[0]
    scale = HEAD_DIM ** (-0.5)
    half = iota((PAD, 128), 1) < HEAD_DIM
    dq, dk, dv = [], [], []
    for pair in range(HEADS // 2):
        at = pair * 128
        query = qkv[:, at : at + 128]
        keys = qkv[:, width + at : width + at + 128]
        values = qkv[:, 2 * width + at : 2 * width + at + 128]
        keys_t = keys.astype(f32).T.astype(bf16)
        do = d_out[:, at : at + 128]
        do_t = d_out_t[at : at + 128]
        zero = jnp.zeros_like(query)
        dq_t = []
        dk_sum = jnp.zeros((PAD, 128), f32)
        dv_sum = jnp.zeros((PAD, 128), f32)
        pair_values = [jnp.where(mask, values, zero) for mask in (half, ~half)]
        dps = nn(jnp.concatenate(pair_values, axis=0), do_t)
        for head in range(2):
            mask = half if head == 0 else ~half
            low_at = at + head * HEAD_DIM
            probs = probs_ref[0, 2 * pair + head]
            dp = dps[head * PAD : (head + 1) * PAD]
            center = jnp.sum(shared[low_at : low_at + HEAD_DIM], axis=0, keepdims=True)
            ds = (probs.astype(f32) * (dp - center)).astype(bf16)
            dk_sum += nn(ds, jnp.where(mask, query, zero))
            dv_sum += nn(probs, jnp.where(mask, do, zero))
            dq_t.append(nn(keys_t[head * HEAD_DIM : (head + 1) * HEAD_DIM], ds))
        dq.append((jnp.concatenate(dq_t, axis=0).T * scale).astype(bf16))
        dk.append((dk_sum * scale).astype(bf16))
        dv.append(dv_sum.astype(bf16))
    dqkv = jnp.concatenate(dq + dk + dv, axis=1)
    inputs = x_ref[0].astype(f32)
    normed_one, inverse_one = normalize(inputs)
    rows_in = normed_one * gains[0:1] + gains[1:2]
    grads[:, : 3 * width] += nn(rows_in.T.astype(bf16), dqkv)
    da = nt(dqkv, weights[:, : 3 * width])
    norm_acc[0] += eight_rows(da * normed_one)
    norm_acc[1] += eight_rows(da)
    grad_ref[0] = dx1 + norm_back(da, normed_one, inverse_one, gains[0:1])

    @pl.when(step == pl.num_programs(0) - 1)
    def _():
        if not closing:
            return
        rows = pieces[0].shape[0]
        row = iota((128, width), 0)
        misc = router_acc[...]
        for i in range(4):
            misc = jnp.where(
                row == experts + i, jnp.sum(norm_acc[i], axis=0, keepdims=True), misc
            )
        table[...] = misc
        extra = table[...].T
        weights[:, : 4 * width] = grads[...].astype(bf16)
        weights[:, 4 * width :] = extra.astype(bf16)
        for k in range(group):
            start = pl.multiple_of(jnp.bitwise_xor(me_ref[0], k) * rows, 16)
            target = keep_ref if k % 2 == 0 else send_ref
            target[k // 2] = weights[pl.ds(start, rows), :]


def home(me, pos, cot, x, saved, pieces, slots, after, carried, start, closing, experts):
    mid, qkv, probs, turned, gates = saved
    group, blocks = len(pieces), len(slots)
    count = GROUP
    width = x.shape[2]
    rows, columns = pieces[0].shape
    stride = slots[0].shape[0]
    wide = blocks * stride

    def take(*tail):
        return pl.BlockSpec((1,) + tail, lambda i: (i + start,) + (0,) * len(tail))

    sums = [sds((width, 4 * width), f32), sds((128, width), f32), sds((4, 8, width), f32)]
    if closing:
        last = [sds((group // 2, rows, columns), bf16)] * 2
    else:
        last = sums
    return pl.pallas_call(
        functools.partial(
            home_kernel, experts, group, blocks, len(after), carried is None, closing
        ),
        grid=(count,),
        out_shape=[sds(x.shape[:2] + (width,), f32)] + last,
        in_specs=[
            SCALAR,
            take(PAD, 128),
            take(PAD, 128),
            take(PAD, width),
            take(PAD, width),
            take(PAD, width),
            take(PAD, 3 * width),
            take(HEADS, PAD, PAD),
            take(width, PAD),
        ]
        + [WHOLE] * (group + blocks)
        + [ANY] * len(after)
        + ([] if carried is None else [WHOLE] * 3 + [ANY]),
        out_specs=[take(PAD, width)] + [WHOLE] * len(last),
        input_output_aliases={} if carried is None else {12 + group + blocks + len(after): 0},
        scratch_shapes=[
            VMEM((width, columns), bf16),
            VMEM((128, width), f32),
            VMEM((wide, width), bf16),
            VMEM((8, wide), f32),
        ]
        + ([VMEM(value.shape, f32) for value in sums] if closing else []),
        compiler_params=params(32),
        cost_estimate=cost(6 * count),
        name="home",
    )(me, pos, gates, x, cot, mid, qkv, probs, turned, *pieces, *slots, *after, *(carried or ()))


def finish_kernel(blocks, *refs):
    pos_ref, gate_ref, mid_ref = refs[:3]
    slots = refs[3 : 3 + blocks]
    out_ref, buffer = refs[-2:]

    @pl.when(pl.program_id(0) == 0)
    def _():
        load_slots(slots, buffer)

    pos, gates = pos_ref[0], gate_ref[0]
    lane = iota((PAD, buffer.shape[0]), 1).astype(f32)
    total = mid_ref[0]
    for j in range(2):
        pick = jnp.where(lane == pos[:, j : j + 1], 1.0, 0.0).astype(bf16)
        total += gates[:, j : j + 1] * nn(pick, buffer[...])
    out_ref[0] = total.astype(bf16)


def finish(pos, saved, slots, after):
    mid, gates = saved[0], saved[4]
    count, _, width = mid.shape
    blocks = len(slots)
    stride = slots[0].shape[0]

    def take(*tail):
        return pl.BlockSpec((1,) + tail, lambda i: (i,) + (0,) * len(tail))

    return pl.pallas_call(
        functools.partial(finish_kernel, blocks),
        grid=(count,),
        out_shape=sds((count, PAD, width), bf16),
        in_specs=[
            take(PAD, 128),
            take(PAD, 128),
            take(PAD, width),
        ]
        + [WHOLE] * blocks
        + [ANY] * len(after),
        out_specs=take(PAD, width),
        scratch_shapes=[VMEM((blocks * stride, width), bf16)],
        compiler_params=params(24),
        cost_estimate=cost(2 * count),
        name="finish",
    )(pos, gates, mid, *slots, *after)


def dense_kernel(side_ref, own_ref, other_ref, *refs):
    attn, router, norm = refs[:3], refs[3:6], refs[6:9]
    attn_out, router_out, norm_out, sum_ref = refs[9:13], refs[13:17], refs[17:21], refs[21]
    count = own_ref.shape[0]
    for half, ref in enumerate((own_ref, other_ref)):
        at = pl.multiple_of(jnp.bitwise_xor(side_ref[0], half) * count, 8)
        sum_ref[pl.ds(at, count), :] = ref[...].astype(f32)
    width = attn[0].shape[2]
    count = router[0].shape[0]
    for index in range(4):
        grad = sum_ref[:, index * width : (index + 1) * width]
        new = adamw(*(ref[index] for ref in attn), grad, rate_matrix, decay_rate)
        for ref, value in zip(attn_out, (grad,) + new):
            ref[index] = value
    extra = sum_ref[:, 4 * width :].T
    grad = extra[:count]
    new = adamw(*(ref[...] for ref in router), grad, rate_matrix, decay_rate)
    for ref, value in zip(router_out, (grad,) + new):
        ref[...] = value
    grad = extra[count : count + 4]
    new = adamw(*(ref[...] for ref in norm), grad, rate_vector, 0.0)
    for ref, value in zip(norm_out, (grad,) + new):
        ref[...] = value


def dense_update(side, halves, attn, router, norm):
    shapes = [sds(group[0].shape, f32) for group in (attn, router, norm) for _ in range(4)]
    return pl.pallas_call(
        dense_kernel,
        out_shape=shapes,
        in_specs=[SCALAR] + [WHOLE] * 11,
        out_specs=[WHOLE] * 12,
        scratch_shapes=[VMEM((2 * halves[0].shape[0], halves[0].shape[1]), f32)],
        compiler_params=params(16),
        cost_estimate=cost(3),
        name="dense_update",
    )(side, *halves, *attn, *router, *norm)


def expert_update_kernel(parts, *refs):
    state, sources, outs = refs[:3], refs[3:-4], refs[-4:]
    for e in range(state[0].shape[0]):
        grad = sum(ref[0].astype(f32) for ref in sources[e * parts : (e + 1) * parts])
        new = adamw(*(ref[e, 0] for ref in state), grad, rate_matrix, decay_rate)
        for ref, value in zip(outs, (grad,) + new):
            ref[e, 0] = value


def expert_update(parts, weight, first, second):
    local, _, hidden, width = weight.shape
    block = pl.BlockSpec((local, 1, hidden, width), lambda m: (0, m, 0, 0))
    part = pl.BlockSpec((1, hidden, width), lambda m: (m, 0, 0))
    flat = [value for own in parts for value in own]
    return pl.pallas_call(
        functools.partial(expert_update_kernel, len(parts[0])),
        grid=(2,),
        out_shape=[sds(weight.shape, f32)] * 4,
        in_specs=[block] * 3 + [part] * len(flat),
        out_specs=[block] * 4,
        compiler_params=params(60),
        cost_estimate=cost(4),
        name="expert_update",
    )(weight, first, second, *flat)


def swap(value, axis, size, bit):
    return lax.ppermute(value, axis, [(i, i ^ bit) for i in range(size)])


def ring_list(size):
    half = size // 2
    return [2 * i for i in range(half)] + [2 * i + 1 for i in reversed(range(half))]


def turn(value, size, by):
    order = ring_list(size)
    pairs = [(order[i], order[(i + by) % size]) for i in range(size)]
    return lax.ppermute(value, "rep", pairs)


def relay_kernel(*refs):
    pass


def tie(values, *others):
    values = list(values)
    return pl.pallas_call(
        relay_kernel,
        out_shape=[sds(value.shape, value.dtype) for value in values],
        in_specs=[ANY] * (len(values) + len(others)),
        out_specs=[ANY] * len(values),
        input_output_aliases={i: i for i in range(len(values))},
        compiler_params=params(1),
        cost_estimate=cost(0),
        name="relay",
    )(*values, *others)


def spread_far(value, size):
    held = {0: value}
    bit = size // 2
    while bit > 1:
        for k in list(held):
            held[k ^ bit] = swap(held[k], "shard", size, bit)
        bit //= 2
    return [held[k] for k in range(0, size, 2)]


def spread_near(values, size):
    both = [(value, swap(value, "shard", size, 1)) for value in values]
    return [value for pair in both for value in pair]


def ring_gather(value, size):
    half = size // 2
    held = [None] * size
    held[0] = value
    others = []
    ahead = behind = value
    for hop in range(1, half):
        if others:
            ahead, behind = tie([ahead, behind], *others)
            held[size - hop + 1], held[hop - 1] = ahead, behind
        ahead, behind = turn(ahead, size, 1), turn(behind, size, -1)
        held[size - hop], held[hop] = ahead, behind
        others = (yield [ahead, behind]) or []
    yield held


def ring_opposite(held, size, rows):
    half = size // 2
    result, opposite = [], []
    for e in range(held[0].shape[1]):
        last = [held[half + 1][0, e], held[half - 1][1, e]]
        opposite = [turn(last[0], size, 1), turn(last[1], size, -1)]
        result.append(held[:half] + opposite + held[half + 1 :])
    return result


def ring_add_kernel(ahead, first, behind, second, *refs):
    out_a, out_b = refs[-2:]
    if len(first.shape) == len(ahead.shape):
        out_a[...] = (ahead[...].astype(f32) + first[...].astype(f32)).astype(bf16)
        out_b[...] = (behind[...].astype(f32) + second[...].astype(f32)).astype(bf16)
    else:
        out_a[0] = (ahead[0].astype(f32) + first[...].astype(f32)).astype(bf16)
        out_a[1] = ahead[1]
        out_b[0] = behind[0]
        out_b[1] = (behind[1].astype(f32) + second[...].astype(f32)).astype(bf16)


def ring_add(ahead, first, behind, second, after):
    return pl.pallas_call(
        ring_add_kernel,
        out_shape=[sds(ahead.shape, bf16)] * 2,
        in_specs=[WHOLE] * 4 + [ANY] * len(after),
        out_specs=[WHOLE] * 2,
        compiler_params=params(16),
        cost_estimate=cost(0),
        name="ring_add",
    )(ahead, first, behind, second, *after)


def ring_sum(grads, size, formed):
    half = size // 2
    full = grads[:half] + [None] + grads[half + 2 :]
    sums = grads[half : half + 2]
    for hop in range(half, 0, -1):
        moving = [turn(sums[0], size, 1), turn(sums[1], size, -1)]
        if hop > 1:
            others = (yield moving) or []
            sums = ring_add(full[hop - 1], moving[0], full[size - hop + 1], moving[1], others)
            formed.extend(sums)
    yield [full[0]] + moving


def add(left, right):
    return (left.astype(f32) + right.astype(f32)).astype(bf16)


def shards(
    tokens,
    routes,
    cotangent,
    attn_weights,
    attn_first,
    attn_second,
    router_weights,
    router_first,
    router_second,
    norm_params,
    norm_first,
    norm_second,
    expert_weights,
    expert_first,
    expert_second,
    *,
    group,
    ring,
):
    tok_count, width = tokens.shape
    experts = router_weights.shape[1]
    local = expert_weights.shape[0]
    capacity = min(tok_count, (tok_count * 8 // (3 * experts) + 7) // 8 * 8)
    stride = -(-(capacity + 8) // 16) * 16
    images = tok_count // SEQ
    me = lax.axis_index("shard").astype(jnp.int32).reshape(1)

    packed, low = pack(attn_weights, router_weights.T, norm_params, expert_weights)
    gathering = ring_gather(low, ring)
    hop = next(gathering)
    pieces = spread_far(packed, group)
    x, cot, pos = stage(me, tokens, cotangent, routes, packed, images, local, group, stride)

    second = next(gathering)
    cots = spread_far(cot, group)
    pieces = spread_near(tie(pieces, pos), group)
    c, *saved = front(me, x, cot, pieces, experts, hop)
    c = tie([c], *second)[0]

    cs = spread_far(c, group)
    gathering.send([c])
    cots = tie(cots, c)
    cot = cots[0]
    cot_slots, places = gather_grads(me, spread_near(cots, group), local, stride)
    cs = spread_near(tie(cs, places), group)
    held = list(gathering)[-1]
    rows, outs = gather_rows(places, cot_slots, cs)
    shards = ring_opposite(held, ring, rows)

    back, made, summing, formed = [], [], [], []
    after, latest = [], []

    def send_back(blocks):
        return [v if k == 0 else swap(v, "shard", group, k) for k, v in enumerate(blocks)]

    def start_sum(grads):
        formed.append([])
        summing.append(ring_sum(list(grads), ring, formed[-1]))
        latest.append(next(summing[-1]))

    def next_hop(at, others):
        latest[at] = summing[at].send(others)

    for e in range(local - 1):
        out = run_whole(e, rows, outs, shards[e], group)
        back += send_back(out[:group])
        made += out[group : 2 * group]
        start_sum(out[2 * group :])
        after = [out[2 * group]]
    early = list(back)
    out = run_first(local - 1, rows, outs, shards[-1], group, after)
    back += send_back(out[:group])
    kept = out[group:]
    for at in range(len(summing)):
        next_hop(at, [out[0]])
    after = early + [value for own in formed for value in own[-2:]]
    out = run_last(local - 1, rows, outs, kept, shards[-1], after, group)
    grads = out[group:]
    made = [v for at in range(0, len(made), group) for v in send_back(made[at : at + group])]
    for at in range(len(summing)):
        next_hop(at, [grads[0]])
    start_sum(grads)
    after = [grads[0]] + [value for own in formed for value in own[-2:]]

    grad, carried = None, None
    for start in range(0, images, GROUP):
        closing = start + GROUP >= images
        grad, *carried = home(
            me, pos, cot, x, saved, pieces, back, after, carried, start, closing, experts
        )
        if start == 0:
            gate = carried[1]
            carried.append(grad)
            for at in range(local):
                next_hop(at, [gate])
            after = [part for own in formed for part in own[-2:]] + made
            made = made + send_back(tie(out[:group], gate))
    keep, send = carried
    send = tie([send], *made, *latest[-1][-2:])[0]

    total = add(keep, swap(send, "shard", group, 1))
    next_hop(-1, [total])
    total = tie([total], *formed[-1][-2:])[0]
    bit = 2
    while bit < group:
        count = total.shape[0] // 2
        pairs = total.reshape(count, 2, *total.shape[1:])
        total = add(pairs[:, 0], swap(pairs[:, 1], "shard", group, bit))
        bit *= 2
    total = total[0]

    total = tie([total], *latest[-1][-2:])[0]
    side = lax.axis_index("rep") % 2
    count = total.shape[0] // 2
    own = lax.dynamic_slice_in_dim(total, side * count, count)
    other = lax.dynamic_slice_in_dim(total, (1 - side) * count, count)
    total = add(own, swap(other, "rep", ring, 1))
    bit = 2
    while bit < ring:
        total = add(total, swap(total, "rep", ring, bit))
        if bit == 2:
            next_hop(-1, [total])
            output = finish(pos, saved, made, [total])
        bit *= 2
    total = tie([total], *latest[-1][-2:])[0]
    for at in range(local):
        for latest[at] in summing[at]:
            pass
    halves = [total, swap(total, "rep", ring, 1)]
    dense = dense_update(
        side.astype(jnp.int32).reshape(1),
        halves,
        (attn_weights, attn_first, attn_second),
        (router_weights.T, router_first.T, router_second.T),
        (norm_params, norm_first, norm_second),
    )
    dense = [value.T if 4 <= i < 8 else value for i, value in enumerate(dense)]
    updated = expert_update(latest, expert_weights, expert_first, expert_second)

    def unpadded(rows):
        return rows[:, :SEQ].reshape(tok_count, width)

    return (unpadded(output), unpadded(grad), *dense, *updated)


def solution(mesh):
    rows = P(("shard", "rep"), None)
    attn = P(None, "shard", None)
    router = P("shard", None)
    norm = P(None, "shard")
    expert = P("shard", None, "rep", None)
    return jax.shard_map(
        functools.partial(shards, group=mesh.shape["shard"], ring=mesh.shape["rep"]),
        mesh=mesh,
        in_specs=(rows,) * 3 + (attn,) * 3 + (router,) * 3 + (norm,) * 3 + (expert,) * 3,
        out_specs=(rows,) * 2 + (attn,) * 4 + (router,) * 4 + (norm,) * 4 + (expert,) * 4,
        check_vma=False,
    )
```

```python
import functools

import jax
import jax.numpy as jnp
from jax import lax
from jax.experimental import pallas as pl
from jax.experimental.pallas import tpu as pltpu
from jax.sharding import PartitionSpec as P

HEADS = 6
HEAD_DIM = 64
SEQ = 197
PAD = 208
STEP = 10
GROUP = 2
CHUNK = 272
STEP_HIDDEN = 256

beta_one = 0.9
beta_two = 0.999
adam_floor = 1e-08
decay_rate = 0.1
rate_matrix = 0.05
rate_vector = 0.3
norm_floor = 1e-06

bf16 = jnp.bfloat16
f32 = jnp.float32
VMEM = pltpu.VMEM
ANY = pl.BlockSpec(memory_space=pl.ANY)
FAR = pl.BlockSpec(memory_space=pltpu.HBM)
WHOLE = pl.BlockSpec(memory_space=pltpu.VMEM)
SCALAR = pl.BlockSpec(memory_space=pltpu.SMEM)


def params(mebibytes):
    return pltpu.CompilerParams(vmem_limit_bytes=mebibytes << 20)


def sds(shape, dtype):
    return jax.ShapeDtypeStruct(shape, dtype)


def cost(time_us):
    return pl.CostEstimate(
        flops=time_us * 1_150_000_000, bytes_accessed=time_us * 1_000_000, transcendentals=0
    )


def nn(left, right):
    return lax.dot_general(left, right, (((1,), (0,)), ((), ())), preferred_element_type=f32)


def nt(left, right):
    return lax.dot_general(left, right, (((1,), (1,)), ((), ())), preferred_element_type=f32)


def iota(shape, dim):
    return lax.broadcasted_iota(jnp.int32, shape, dim)


def normalize(values):
    centred = values - jnp.mean(values, axis=-1, keepdims=True)
    inverse = lax.rsqrt(jnp.mean(centred * centred, axis=-1, keepdims=True) + norm_floor)
    return centred * inverse, inverse


def norm_back(grad_rows, normed, inverse, gain):
    scaled = grad_rows * gain
    inner = (
        scaled
        - jnp.mean(scaled, axis=-1, keepdims=True)
        - normed * jnp.mean(scaled * normed, axis=-1, keepdims=True)
    )
    return inner * inverse


def eight_rows(values):
    rows, cols = values.shape
    return jnp.sum(values.reshape(rows // 8, 8, cols), axis=0)


def adamw(weight, first, second, grad, rate, decay):
    first_new = beta_one * first + (1.0 - beta_one) * grad
    second_new = beta_two * second + (1.0 - beta_two) * grad * grad
    first_hat = first_new * (1.0 / (1.0 - beta_one**STEP))
    second_hat = second_new * (1.0 / (1.0 - beta_two**STEP))
    return (
        first_new,
        second_new,
        weight - rate * (first_hat / (jnp.sqrt(second_hat) + adam_floor) + decay * weight),
    )


def pack_kernel(attn, router_t, norm, expert, packed, low):
    for e in range(expert.shape[0]):
        for m in range(2):
            low[m, e] = expert[e, m].astype(bf16)
    width = attn.shape[2]
    for index in range(4):
        packed[:, index * width : (index + 1) * width] = attn[index].astype(bf16)
    count, rows = router_t.shape
    filler = jnp.zeros((128 - count - 4, rows), f32)
    block = jnp.concatenate([router_t[...], norm[...], filler], axis=0)
    packed[:, 4 * width :] = block.T.astype(bf16)


def pack(attn, router_t, norm, expert):
    _, rows, width = attn.shape
    local, _, hidden, _ = expert.shape
    return pl.pallas_call(
        pack_kernel,
        out_shape=[sds((rows, 4 * width + 128), bf16), sds((2, local, hidden, width), bf16)],
        in_specs=[WHOLE] * 4,
        out_specs=[WHOLE] * 2,
        compiler_params=params(60),
        cost_estimate=cost(2),
        name="pack",
    )(attn, router_t, norm, expert)


def stage_kernel(local, group, stride, me_ref, tok_ref, cot_ref, routes_ref, _, *refs):
    x_ref, sent_ref, pos_ref, wide_ref, route_ref = refs
    images, _, width = x_ref.shape
    count = tok_ref.shape[0]
    rows = images * PAD

    def cut(image):
        tail = jnp.zeros((PAD - SEQ, width), f32)
        return jnp.concatenate([wide_ref[image * SEQ : (image + 1) * SEQ, :], tail], axis=0)

    wide_ref[:count, :] = tok_ref[...].astype(f32)
    for image in range(images):
        x_ref[image] = cut(image).astype(bf16)

    route_ref[:count, :] = routes_ref[...].astype(f32)
    gap = jnp.full((PAD - SEQ, 2), -1.0, f32)
    parts = []
    for image in range(images):
        parts += [route_ref[image * SEQ : (image + 1) * SEQ, :], gap]
    routes = jnp.concatenate(parts, axis=0)
    one, two = routes[:, 0:1], routes[:, 1:2]
    lane = iota((rows, 128), 1).astype(f32)
    pick_one, pick_two = lane == one, lane == two
    mask = jnp.where(pick_one | pick_two, 1.0, 0.0).astype(bf16)
    lower = jnp.where(iota((rows, rows), 0) >= iota((rows, rows), 1), 1.0, 0.0).astype(bf16)
    seen = nn(lower, mask)
    ranks = [
        jnp.sum(jnp.where(pick, seen, 0.0), axis=1, keepdims=True) - 1.0
        for pick in (pick_one, pick_two)
    ]
    places = []
    for route, rank in zip((one, two), ranks):
        owner = jnp.floor(route * (1.0 / local))
        inner = route - owner * local
        other = jnp.bitwise_xor(owner.astype(jnp.int32), me_ref[0]).astype(f32)
        places.append(
            jnp.where(route < 0.0, -1.0, (inner * group + other) * stride + rank)
        )
    table = jnp.where(lane == 0.0, places[0], jnp.where(lane == 1.0, places[1], 0.0))
    table = jnp.where(lane == 2.0, one, jnp.where(lane == 3.0, two, table))
    pos_ref[...] = table.reshape(images, PAD, 128)
    for at, rank in enumerate(ranks):
        high = jnp.floor(rank * (1.0 / 16.0))
        table = jnp.where(lane == 4.0 + 2 * at, high, table)
        table = jnp.where(lane == 5.0 + 2 * at, rank - 16.0 * high, table)
    wide_ref[:count, :] = cot_ref[...].astype(f32)
    for image in range(images):
        turned = table[image * PAD : (image + 1) * PAD].T[:8]
        turned = jnp.where(iota((8, PAD), 0) < 2, 0.0, turned)
        meta = jnp.concatenate([turned, jnp.zeros((8, width - PAD), f32)], axis=1)
        body = cut(image)[: PAD - 8]
        sent_ref[image] = jnp.concatenate([body, meta], axis=0).astype(bf16)


def stage(me, tokens, cotangent, routes, after, images, local, group, stride):
    count, width = tokens.shape
    padded = -(-count // 8) * 8
    return pl.pallas_call(
        functools.partial(stage_kernel, local, group, stride),
        out_shape=[sds((images, PAD, width), bf16)] * 2 + [sds((images, PAD, 128), f32)],
        in_specs=[SCALAR, WHOLE, WHOLE, WHOLE, ANY],
        out_specs=[WHOLE] * 3,
        scratch_shapes=[VMEM((padded, width), f32), VMEM((padded, 2), f32)],
        compiler_params=params(24),
        cost_estimate=cost(5),
        name="stage",
    )(me, tokens, cotangent, routes, after)


def load_weights(me, pieces, weights, turned):
    rows = pieces[0].shape[0]
    for index, piece in enumerate(pieces):
        start = pl.multiple_of(jnp.bitwise_xor(me, index) * rows, 16)
        weights[pl.ds(start, rows), :] = piece[...]
    width = weights.shape[0]
    turned[...] = weights[:, 4 * width :].astype(f32).T


def front_kernel(experts, group, *refs):
    me_ref, x_ref, meta_ref = refs[:3]
    pieces = refs[3 : 3 + group]
    sent_ref, mid_ref, qkv_ref, probs_ref, turned_ref, gate_ref, weights, table = refs[-8:]
    width = weights.shape[0]

    @pl.when(pl.program_id(0) == 0)
    def _():
        load_weights(me_ref[0], pieces, weights, table)

    inputs = x_ref[0].astype(f32)
    normed, _ = normalize(inputs)
    gains = table[experts : experts + 4]
    rows_in = (normed * gains[0:1] + gains[1:2]).astype(bf16)
    qkv = nn(rows_in, weights[:, : 3 * width]).astype(bf16)
    qkv_ref[0] = qkv
    half = iota((PAD, 128), 1) < HEAD_DIM
    real = iota((PAD, PAD), 0) < SEQ
    scale = HEAD_DIM ** (-0.5)
    joined = []
    for pair in range(HEADS // 2):
        at = pair * 128
        query = qkv[:, at : at + 128]
        keys = qkv[:, width + at : width + at + 128]
        values = qkv[:, 2 * width + at : 2 * width + at + 128].astype(f32).T.astype(bf16)
        parts = []
        for head in range(2):
            own = jnp.where(half if head == 0 else ~half, keys, jnp.zeros_like(keys))
            scores = jnp.where(real, nt(own, query) * scale, -1e30)
            expd = jnp.exp(scores - jnp.max(scores, axis=0, keepdims=True))
            probs = (expd * (1.0 / jnp.sum(expd, axis=0, keepdims=True))).astype(bf16)
            probs_ref[0, 2 * pair + head] = probs
            parts.append(nn(values[head * HEAD_DIM : (head + 1) * HEAD_DIM], probs))
        both = jnp.concatenate(parts, axis=0)
        turned_ref[0, at : at + 128, :] = both.astype(bf16)
        joined.append(both.T.astype(bf16))
    attended = jnp.concatenate(joined, axis=1)
    middle = inputs + nn(attended, weights[:, 3 * width : 4 * width])
    mid_ref[0] = middle
    normed_two, _ = normalize(middle)
    expert_in = (normed_two * gains[2:3] + gains[3:4]).astype(bf16)
    logits = nt(table[:16].astype(bf16), expert_in)
    meta = meta_ref[0][PAD - 16 :].astype(f32)[8:, :PAD]
    row = iota((16, PAD), 0).astype(f32)
    picked = [
        jnp.sum(jnp.where(row == meta[2 + j : 3 + j], logits, 0.0), axis=0, keepdims=True)
        for j in range(2)
    ]
    top = jnp.maximum(picked[0], picked[1])
    exps = [jnp.exp(value - top) for value in picked]
    total = exps[0] + exps[1]
    row8 = iota((8, PAD), 0)
    gates = jnp.where(row8 == 0, exps[0] / total, jnp.where(row8 == 1, exps[1] / total, 0.0))
    gate_ref[0] = jnp.concatenate([gates, jnp.zeros((120, PAD), f32)], axis=0).T
    gap = picked[0] - picked[1]
    high = gap.astype(bf16).astype(f32)
    meta = jnp.where(row8 == 0, high, jnp.where(row8 == 1, gap - high, 0.0))
    meta = jnp.concatenate([meta, jnp.zeros((8, width - PAD), f32)], axis=1)
    sent_ref[0] = jnp.concatenate([expert_in.astype(f32)[: PAD - 8], meta], axis=0).astype(bf16)


def front(me, x, cot, pieces, experts, after):
    width = x.shape[2]
    count = x.shape[0]
    group = len(pieces)
    columns = pieces[0].shape[1]

    def take(*tail):
        return pl.BlockSpec((1,) + tail, lambda i: (i,) + (0,) * len(tail))

    give = take

    return pl.pallas_call(
        functools.partial(front_kernel, experts, group),
        grid=(count,),
        out_shape=[
            sds((count, PAD, width), bf16),
            sds((count, PAD, width), f32),
            sds((count, PAD, 3 * width), bf16),
            sds((count, HEADS, PAD, PAD), bf16),
            sds((count, width, PAD), bf16),
            sds((count, PAD, 128), f32),
        ],
        in_specs=[SCALAR, take(PAD, width), take(PAD, width)]
        + [WHOLE] * group
        + [ANY] * len(after),
        out_specs=[
            give(PAD, width),
            give(PAD, width),
            give(PAD, 3 * width),
            give(HEADS, PAD, PAD),
            give(width, PAD),
            give(PAD, 128),
        ],
        scratch_shapes=[
            VMEM((width, columns), bf16),
            VMEM((128, width), f32),
        ],
        compiler_params=params(28),
        cost_estimate=cost(3 * count),
        name="front",
    )(me, x, cot, *pieces, *after)


def gather_grads_kernel(local, stride, *refs):
    refs = list(refs)
    me_ref, *grads = refs[:-2]
    out_ref, place_ref = refs[-2:]
    group = len(grads)
    images, _, width = grads[0].shape
    first = me_ref[0] * local
    slot = iota((stride, PAD), 0).astype(f32)
    row8 = iota((8, PAD), 0)
    for k in range(group):
        sums = jnp.zeros((local * stride, width), f32)
        for image in range(images):
            block = grads[k][image]
            meta = block[PAD - 16 :].astype(f32)[8:, :PAD]
            ranks = [16.0 * meta[4 + 2 * j : 5 + 2 * j] + meta[5 + 2 * j : 6 + 2 * j] for j in range(2)]
            picks = []
            table = jnp.zeros((8, PAD), f32)
            for e in range(local):
                expert = (first + e).astype(f32)
                is_one, is_two = meta[2:3] == expert, meta[3:4] == expert
                place = jnp.where(is_one, ranks[0], jnp.where(is_two, ranks[1], -1.0))
                picks.append(jnp.where(slot == place, 1.0, 0.0).astype(bf16))
                table = jnp.where(row8 == e, place, table)
                table = jnp.where(row8 == 4 + e, jnp.where(is_one, 1.0, 0.0), table)
            place_ref[k, image] = jnp.concatenate([table, jnp.zeros((8, 256 - PAD), f32)], axis=1)
            sums += nn(jnp.concatenate(picks, axis=0), block)
        for e in range(local):
            out_ref[e, k * stride : (k + 1) * stride, :] = sums[
                e * stride : (e + 1) * stride
            ].astype(bf16)


def gather_grads(me, grads, local, stride):
    group = len(grads)
    images, _, width = grads[0].shape
    return pl.pallas_call(
        functools.partial(gather_grads_kernel, local, stride),
        out_shape=[
            sds((local, group * stride, width), bf16),
            sds((group, images, 8, 256), f32),
        ],
        in_specs=[SCALAR] + [WHOLE] * group,
        out_specs=[WHOLE] * 2,
        compiler_params=params(22),
        cost_estimate=cost(6),
        name="gather_grads",
    )(me, *grads)


def gather_rows_kernel(local, stride, *refs):
    refs = list(refs)
    place_ref, grad_ref, *tokens = refs[:-2]
    rows_ref, outs_ref = refs[-2:]
    group = len(tokens)
    images, _, width = tokens[0].shape
    slot = iota((stride, PAD), 0).astype(f32)
    for k in range(group):
        sums = jnp.zeros((local * stride, width), f32)
        gate_sum = jnp.zeros((local * stride, PAD), f32)
        for image in range(images):
            block = tokens[k][image]
            meta = block[PAD - 16 :].astype(f32)[8:, :PAD]
            gap = meta[0:1] + meta[1:2]
            top = jnp.maximum(gap, 0.0)
            left, right = jnp.exp(gap - top), jnp.exp(-top)
            inverse = 1.0 / (left + right)
            table = place_ref[k, image][:, :PAD]
            picks, weighted = [], []
            for e in range(local):
                match = slot == table[e : e + 1]
                gate = jnp.where(table[4 + e : 5 + e] > 0.0, left, right) * inverse
                picks.append(jnp.where(match, 1.0, 0.0).astype(bf16))
                weighted.append(jnp.where(match, gate, 0.0))
            sums += nn(jnp.concatenate(picks, axis=0), block)
            gate_sum += jnp.concatenate(weighted, axis=0)
        gate = jnp.sum(gate_sum, axis=1, keepdims=True)
        part = slice(k * stride, (k + 1) * stride)
        for e in range(local):
            mine = slice(e * stride, (e + 1) * stride)
            rows_ref[e, part, :] = sums[mine].astype(bf16)
            outs_ref[e, part, :] = (grad_ref[e, part, :].astype(f32) * gate[mine]).astype(bf16)


def gather_rows(places, grads, tokens):
    local, slots, width = grads.shape
    group = len(tokens)
    images = tokens[0].shape[0]
    return pl.pallas_call(
        functools.partial(gather_rows_kernel, local, slots // group),
        out_shape=[sds((local, slots, width), bf16)] * 2,
        in_specs=[WHOLE] * (2 + group),
        out_specs=[WHOLE] * 2,
        compiler_params=params(22),
        cost_estimate=cost(6),
        name="gather_rows",
    )(places, grads, *tokens)


def shard_views(shards):
    half = (len(shards) - 1) // 2
    views = [[ref.at[0], ref.at[1]] for ref in shards[:half]]
    views.append([shards[half], shards[half + 1]])
    return views + [[ref.at[0], ref.at[1]] for ref in shards[half + 2 :]]


def assemble(shards, index, mats, first):
    hidden = mats.shape[1] // len(shards)
    for r, shard in enumerate(shards):
        for m in range(first, 2):
            whole = len(shard[m].shape) == 2
            mats[m - first, r * hidden : (r + 1) * hidden, :] = (
                shard[m][...] if whole else shard[m][index]
            )


def expert_back(index, rows, outs, mats, moment, act_s, down_s, back_out, finished):
    steps, slots, step = act_s.shape
    stride = slots // len(back_out)
    width = mats.shape[2]
    k0 = 0.7978845608028654
    k1 = 0.044715
    for i in range(steps):
        for k in range(len(back_out)):
            part = slice(k * stride, (k + 1) * stride)
            partial = None
            for at in range(0, step, 256):
                own = slice(i * step + at, i * step + at + 256)
                pre = nt(rows[index, part, :], mats[0, own, :])
                back = nt(outs[index, part, :], mats[1, own, :])
                square = pre * pre
                tanh = jnp.tanh(pre * (k0 + (k0 * k1) * square))
                half = 0.5 + 0.5 * tanh
                act = pre * half
                slope = half + (2.0 * act) * (1.0 - half) * (k0 + (3.0 * k0 * k1) * square)
                both = act * back
                both = both[:, :128] + both[:, 128:]
                act_s[i, part, at : at + 256] = act.astype(bf16)
                down_s[i, part, at : at + 256] = (back * slope).astype(bf16)
                partial = both if partial is None else partial + both
            if i == 0:
                moment[part, :] = partial
            else:
                moment[part, :] += partial
        finished(i)

    wide = -(-slots // 128) * 128
    row8 = iota((8, slots), 0)
    inside = iota((8, width), 1) < stride - 8
    sums = jnp.sum(moment[...].T, axis=0, keepdims=True)
    high = sums.astype(bf16).astype(f32)
    table = jnp.where(row8 == 0, high, jnp.where(row8 == 1, sums - high, 0.0))
    if wide > slots:
        table = jnp.concatenate([table, jnp.zeros((8, wide - slots), f32)], axis=1)
    for k, out in enumerate(back_out):
        part = slice(k * stride, (k + 1) * stride)
        gone = sum(
            nn(down_s[i, part, :], mats[0, i * step : (i + 1) * step, :]) for i in range(steps)
        )
        here = table if k == 0 else pltpu.roll(table, wide - k * stride, 1)
        here = jnp.where(inside, here[:, :width], 0.0)
        out[...] = jnp.concatenate([gone[: stride - 8], here], axis=0).astype(bf16)


def expert_ends(index, rows, outs, second, act, down, grads, made_out, grad_out, sem, before):
    steps, slots, step = act.shape
    stride = slots // len(made_out)
    hidden = steps * step // len(grad_out)
    copies = [
        [
            pltpu.make_async_copy(
                grads.at[m, pl.ds(r * hidden, hidden)], grad_out[r][m], sem.at[r, m]
            )
            for m in range(2)
        ]
        for r in range(len(grad_out))
    ]
    rows_t = rows[index].astype(f32).T.astype(bf16)
    outs_t = outs[index].astype(f32).T.astype(bf16)
    sent = 0
    for i in range(steps):
        at = i * step
        before(i)
        grads[0, at : at + step, :] = nn(rows_t, down[i]).T.astype(bf16)
        grads[1, at : at + step, :] = nn(outs_t, act[i]).T.astype(bf16)
        while (sent + 1) * hidden <= at + step:
            for copy in copies[sent]:
                copy.start()
            sent += 1
    for k, out in enumerate(made_out):
        part = slice(k * stride, (k + 1) * stride)
        made = sum(
            nn(act[i, part, :], second[i * step : (i + 1) * step, :]) for i in range(steps)
        )
        out[...] = made.astype(bf16)
    for pair in copies:
        for copy in pair:
            copy.wait()


def expert_all_kernel(index, group, count, *refs):
    refs = list(refs)
    rows, outs = refs[:2]
    shards, refs = shard_views(refs[2 : 2 + count]), refs[2 + count :]
    back_out, made_out, refs = refs[:group], refs[group : 2 * group], refs[2 * group :]
    grad_out, refs = shard_views(refs[:count]), refs[count:]
    mats, moment, act_s, down_s, grads, sem = refs
    assemble(shards, index, mats, 0)
    expert_back(index, rows, outs, mats, moment, act_s, down_s, back_out, lambda i: None)
    expert_ends(
        index, rows, outs, mats.at[1], act_s, down_s, grads, made_out, grad_out, sem, lambda i: None
    )


def expert_back_kernel(index, group, count, *refs):
    refs = list(refs)
    rows, outs = refs[:2]
    shards, refs = shard_views(refs[2 : 2 + count]), refs[2 + count :]
    back_out, act_s, down_s, mats, moment = (refs[-4 - group : -4], *refs[-4:])
    assemble(shards, index, mats, 0)
    expert_back(index, rows, outs, mats, moment, act_s, down_s, back_out, lambda i: None)


def expert_ends_kernel(index, group, count, *refs):
    refs = list(refs)
    rows, outs, act, down = refs[:4]
    shards, refs = shard_views(refs[4 : 4 + count]), refs[4 + count :]
    second, grads, sem = refs[-3:]
    grad_out = shard_views(refs[-3 - count : -3])
    made_out = refs[-3 - count - group : -3 - count]
    assemble(shards, index, second, 1)
    expert_ends(
        index, rows, outs, second.at[0], act, down, grads, made_out, grad_out, sem, lambda i: None
    )


def expert_shapes(rows, shards, group):
    _, slots, width = rows.shape
    hidden = shards[0].shape[2]
    total = (len(shards) - 1) * hidden
    step = 512 if total % 512 == 0 else 256
    half = (len(shards) - 1) // 2
    grads = [sds(((2, hidden, width)), bf16)] * half + [sds((hidden, width), bf16)] * 2
    grads += [sds(((2, hidden, width)), bf16)] * (half - 1)
    grads = [pltpu.HBM(value.shape, bf16) for value in grads]
    return slots // group, total, (total // step, slots, step), grads


def run_whole(index, rows, outs, shards, group):
    stride, total, kept, grads = expert_shapes(rows, shards, group)
    _, slots, width = rows.shape
    count = len(shards)
    return pl.pallas_call(
        functools.partial(expert_all_kernel, index, group, count),
        out_shape=[sds((stride, width), bf16)] * (2 * group) + grads,
        in_specs=[WHOLE] * (2 + count),
        out_specs=[WHOLE] * (2 * group) + [ANY] * count,
        scratch_shapes=[
            VMEM((2, total, width), bf16),
            VMEM((slots, 128), f32),
            VMEM(kept, bf16),
            VMEM(kept, bf16),
            VMEM((2, total, width), bf16),
            pltpu.SemaphoreType.DMA((count - 1, 2)),
        ],
        compiler_params=params(32),
        cost_estimate=cost(14),
        name="expert_all",
    )(rows, outs, *shards)


def run_first(index, rows, outs, shards, group, after):
    stride, total, kept, _ = expert_shapes(rows, shards, group)
    _, slots, width = rows.shape
    count = len(shards)
    return pl.pallas_call(
        functools.partial(expert_back_kernel, index, group, count),
        out_shape=[sds((stride, width), bf16)] * group + [sds(kept, bf16)] * 2,
        in_specs=[WHOLE] * (2 + count) + [ANY] * len(after),
        out_specs=[WHOLE] * (group + 2),
        scratch_shapes=[VMEM((2, total, width), bf16), VMEM((slots, 128), f32)],
        compiler_params=params(24),
        cost_estimate=cost(9),
        name="expert_first",
    )(rows, outs, *shards, *after)


def run_last(index, rows, outs, kept, shards, after, group):
    stride, total, shape, grads = expert_shapes(rows, shards, group)
    width = rows.shape[2]
    count = len(shards)
    return pl.pallas_call(
        functools.partial(expert_ends_kernel, index, group, count),
        out_shape=[sds((stride, width), bf16)] * group + grads,
        in_specs=[WHOLE] * (4 + count) + [ANY] * len(after),
        out_specs=[WHOLE] * group + [ANY] * count,
        scratch_shapes=[
            VMEM((1, total, width), bf16),
            VMEM((2, total, width), bf16),
            pltpu.SemaphoreType.DMA((count - 1, 2)),
        ],
        compiler_params=params(24),
        cost_estimate=cost(8),
        name="expert_last",
    )(rows, outs, *kept, *shards, *after)


def load_slots(blocks, buffer):
    stride = blocks[0].shape[0]
    for i, block in enumerate(blocks):
        buffer[i * stride : (i + 1) * stride, :] = block[...]


def home_kernel(experts, group, blocks, extra, opening, closing, *refs):
    refs = list(refs)
    me_ref, pos_ref, gate_ref, x_ref, cot_ref, mid_ref, qkv_ref, probs_ref, turned_ref = refs[:9]
    refs = refs[9:]
    pieces, refs = refs[:group], refs[group:]
    slots, refs = refs[:blocks], refs[blocks:]
    refs = refs[extra:]
    if not opening:
        carried, refs = refs[:3], refs[4:]
    grad_ref, refs = refs[0], refs[1:]
    if closing:
        keep_ref, send_ref = refs[:2]
        refs = refs[2:]
    else:
        carry, refs = refs[:3], refs[3:]
    weights, table, buffer, moments = refs[:4]
    sums = refs[4:] if closing else carry
    grads, router_acc, norm_acc = sums
    width = weights.shape[0]
    stride = slots[0].shape[0]
    wide = buffer.shape[0]
    step = pl.program_id(0)

    @pl.when(step == 0)
    def _():
        load_slots(slots, buffer)
        load_weights(me_ref[0], pieces, weights, table)
        for i, ref in enumerate(sums):
            ref[...] = jnp.zeros_like(ref) if opening else carried[i][...]
        total = jnp.zeros((8, wide), f32)
        for i in range(blocks):
            tail = buffer[(i + 1) * stride - 16 : (i + 1) * stride, :].astype(f32)[8:]
            tail = jnp.concatenate([tail, jnp.zeros((8, wide - width), f32)], axis=1)
            total += tail if i == 0 else pltpu.roll(tail, i * stride, 1)
        moments[...] = total

    real = iota((PAD, 1), 0) < SEQ
    gains = table[experts : experts + 4]
    pos = pos_ref[0]
    gates = gate_ref[0]
    lane = iota((PAD, wide), 1).astype(f32)
    match_one = lane == pos[:, 0:1]
    match_two = lane == pos[:, 1:2]
    pick = jnp.where(match_one | match_two, 1.0, 0.0).astype(bf16)
    moment = moments[0:1] + moments[1:2]
    share = jnp.where(match_one, gates[:, 1:2], jnp.where(match_two, -gates[:, 0:1], 0.0))
    dz = jnp.sum(share * moment, axis=1, keepdims=True)
    lane = iota((PAD, 128), 1).astype(f32)
    dl = jnp.where(lane == pos[:, 2:3], dz, jnp.where(lane == pos[:, 3:4], -dz, 0.0))
    middle = mid_ref[0]
    normed, inverse = normalize(middle)
    expert_in = (normed * gains[2:3] + gains[3:4]).astype(bf16)
    dc = nn(pick, buffer[...]) + nn(dl.astype(bf16), table[...].astype(bf16))
    router_acc[...] += nn(dl.T.astype(bf16), expert_in)
    norm_acc[2] += eight_rows(dc * normed)
    norm_acc[3] += eight_rows(dc)
    dx1 = jnp.where(real, cot_ref[0].astype(f32), 0.0) + norm_back(dc, normed, inverse, gains[2:3])
    low = dx1.astype(bf16)
    turned = turned_ref[0]
    grads[:, 3 * width :] += nn(turned, low)
    out_proj = weights[:, 3 * width : 4 * width]
    d_out = nt(low, out_proj).astype(bf16)
    d_out_t = nt(out_proj, low).astype(bf16)
    shared = d_out_t.astype(f32) * turned.astype(f32)

    qkv = qkv_ref[0]
    scale = HEAD_DIM ** (-0.5)
    half = iota((PAD, 128), 1) < HEAD_DIM
    dq, dk, dv = [], [], []
    for pair in range(HEADS // 2):
        at = pair * 128
        query = qkv[:, at : at + 128]
        keys = qkv[:, width + at : width + at + 128]
        values = qkv[:, 2 * width + at : 2 * width + at + 128]
        keys_t = keys.astype(f32).T.astype(bf16)
        do = d_out[:, at : at + 128]
        do_t = d_out_t[at : at + 128]
        zero = jnp.zeros_like(query)
        dq_t = []
        dk_sum = jnp.zeros((PAD, 128), f32)
        dv_sum = jnp.zeros((PAD, 128), f32)
        pair_values = [jnp.where(mask, values, zero) for mask in (half, ~half)]
        dps = nn(jnp.concatenate(pair_values, axis=0), do_t)
        for head in range(2):
            mask = half if head == 0 else ~half
            low_at = at + head * HEAD_DIM
            probs = probs_ref[0, 2 * pair + head]
            dp = dps[head * PAD : (head + 1) * PAD]
            center = jnp.sum(shared[low_at : low_at + HEAD_DIM], axis=0, keepdims=True)
            ds = (probs.astype(f32) * (dp - center)).astype(bf16)
            dk_sum += nn(ds, jnp.where(mask, query, zero))
            dv_sum += nn(probs, jnp.where(mask, do, zero))
            dq_t.append(nn(keys_t[head * HEAD_DIM : (head + 1) * HEAD_DIM], ds))
        dq.append((jnp.concatenate(dq_t, axis=0).T * scale).astype(bf16))
        dk.append((dk_sum * scale).astype(bf16))
        dv.append(dv_sum.astype(bf16))
    dqkv = jnp.concatenate(dq + dk + dv, axis=1)
    inputs = x_ref[0].astype(f32)
    normed_one, inverse_one = normalize(inputs)
    rows_in = normed_one * gains[0:1] + gains[1:2]
    grads[:, : 3 * width] += nn(rows_in.T.astype(bf16), dqkv)
    da = nt(dqkv, weights[:, : 3 * width])
    norm_acc[0] += eight_rows(da * normed_one)
    norm_acc[1] += eight_rows(da)
    grad_ref[0] = dx1 + norm_back(da, normed_one, inverse_one, gains[0:1])

    @pl.when(step == pl.num_programs(0) - 1)
    def _():
        if not closing:
            return
        rows = pieces[0].shape[0]
        row = iota((128, width), 0)
        misc = router_acc[...]
        for i in range(4):
            misc = jnp.where(
                row == experts + i, jnp.sum(norm_acc[i], axis=0, keepdims=True), misc
            )
        table[...] = misc
        extra = table[...].T
        weights[:, : 4 * width] = grads[...].astype(bf16)
        weights[:, 4 * width :] = extra.astype(bf16)
        for k in range(group):
            start = pl.multiple_of(jnp.bitwise_xor(me_ref[0], k) * rows, 16)
            target = keep_ref if k % 2 == 0 else send_ref
            target[k // 2] = weights[pl.ds(start, rows), :]


def home(me, pos, cot, x, saved, pieces, slots, after, carried, start, closing, experts):
    mid, qkv, probs, turned, gates = saved
    group, blocks = len(pieces), len(slots)
    count = GROUP
    width = x.shape[2]
    rows, columns = pieces[0].shape
    stride = slots[0].shape[0]
    wide = blocks * stride

    def take(*tail):
        return pl.BlockSpec((1,) + tail, lambda i: (i + start,) + (0,) * len(tail))

    sums = [sds((width, 4 * width), f32), sds((128, width), f32), sds((4, 8, width), f32)]
    if closing:
        last = [sds((group // 2, rows, columns), bf16)] * 2
    else:
        last = sums
    return pl.pallas_call(
        functools.partial(
            home_kernel, experts, group, blocks, len(after), carried is None, closing
        ),
        grid=(count,),
        out_shape=[sds(x.shape[:2] + (width,), f32)] + last,
        in_specs=[
            SCALAR,
            take(PAD, 128),
            take(PAD, 128),
            take(PAD, width),
            take(PAD, width),
            take(PAD, width),
            take(PAD, 3 * width),
            take(HEADS, PAD, PAD),
            take(width, PAD),
        ]
        + [WHOLE] * (group + blocks)
        + [ANY] * len(after)
        + ([] if carried is None else [WHOLE] * 3 + [ANY]),
        out_specs=[take(PAD, width)] + [WHOLE] * len(last),
        input_output_aliases={} if carried is None else {12 + group + blocks + len(after): 0},
        scratch_shapes=[
            VMEM((width, columns), bf16),
            VMEM((128, width), f32),
            VMEM((wide, width), bf16),
            VMEM((8, wide), f32),
        ]
        + ([VMEM(value.shape, f32) for value in sums] if closing else []),
        compiler_params=params(32),
        cost_estimate=cost(6 * count),
        name="home",
    )(me, pos, gates, x, cot, mid, qkv, probs, turned, *pieces, *slots, *after, *(carried or ()))


def finish_kernel(blocks, *refs):
    pos_ref, gate_ref, mid_ref = refs[:3]
    slots = refs[3 : 3 + blocks]
    out_ref, buffer = refs[-2:]

    @pl.when(pl.program_id(0) == 0)
    def _():
        load_slots(slots, buffer)

    pos, gates = pos_ref[0], gate_ref[0]
    lane = iota((PAD, buffer.shape[0]), 1).astype(f32)
    total = mid_ref[0]
    for j in range(2):
        pick = jnp.where(lane == pos[:, j : j + 1], 1.0, 0.0).astype(bf16)
        total += gates[:, j : j + 1] * nn(pick, buffer[...])
    out_ref[0] = total.astype(bf16)


def finish(pos, saved, slots, after):
    mid, gates = saved[0], saved[4]
    count, _, width = mid.shape
    blocks = len(slots)
    stride = slots[0].shape[0]

    def take(*tail):
        return pl.BlockSpec((1,) + tail, lambda i: (i,) + (0,) * len(tail))

    return pl.pallas_call(
        functools.partial(finish_kernel, blocks),
        grid=(count,),
        out_shape=sds((count, PAD, width), bf16),
        in_specs=[
            take(PAD, 128),
            take(PAD, 128),
            take(PAD, width),
        ]
        + [WHOLE] * blocks
        + [ANY] * len(after),
        out_specs=take(PAD, width),
        scratch_shapes=[VMEM((blocks * stride, width), bf16)],
        compiler_params=params(24),
        cost_estimate=cost(2 * count),
        name="finish",
    )(pos, gates, mid, *slots, *after)


def dense_kernel(side_ref, own_ref, other_ref, *refs):
    attn, router, norm = refs[:3], refs[3:6], refs[6:9]
    attn_out, router_out, norm_out, sum_ref = refs[9:13], refs[13:17], refs[17:21], refs[21]
    count = own_ref.shape[0]
    for half, ref in enumerate((own_ref, other_ref)):
        at = pl.multiple_of(jnp.bitwise_xor(side_ref[0], half) * count, 8)
        sum_ref[pl.ds(at, count), :] = ref[...].astype(f32)
    width = attn[0].shape[2]
    count = router[0].shape[0]
    for index in range(4):
        grad = sum_ref[:, index * width : (index + 1) * width]
        new = adamw(*(ref[index] for ref in attn), grad, rate_matrix, decay_rate)
        for ref, value in zip(attn_out, (grad,) + new):
            ref[index] = value
    extra = sum_ref[:, 4 * width :].T
    grad = extra[:count]
    new = adamw(*(ref[...] for ref in router), grad, rate_matrix, decay_rate)
    for ref, value in zip(router_out, (grad,) + new):
        ref[...] = value
    grad = extra[count : count + 4]
    new = adamw(*(ref[...] for ref in norm), grad, rate_vector, 0.0)
    for ref, value in zip(norm_out, (grad,) + new):
        ref[...] = value


def dense_update(side, halves, attn, router, norm):
    shapes = [sds(group[0].shape, f32) for group in (attn, router, norm) for _ in range(4)]
    return pl.pallas_call(
        dense_kernel,
        out_shape=shapes,
        in_specs=[SCALAR] + [WHOLE] * 11,
        out_specs=[WHOLE] * 12,
        scratch_shapes=[VMEM((2 * halves[0].shape[0], halves[0].shape[1]), f32)],
        compiler_params=params(16),
        cost_estimate=cost(3),
        name="dense_update",
    )(side, *halves, *attn, *router, *norm)


def expert_update_kernel(parts, *refs):
    state, sources, outs = refs[:3], refs[3:-4], refs[-4:]
    for e in range(state[0].shape[0]):
        grad = sum(ref[0].astype(f32) for ref in sources[e * parts : (e + 1) * parts])
        new = adamw(*(ref[e, 0] for ref in state), grad, rate_matrix, decay_rate)
        for ref, value in zip(outs, (grad,) + new):
            ref[e, 0] = value


def expert_update(parts, weight, first, second):
    local, _, hidden, width = weight.shape
    block = pl.BlockSpec((local, 1, hidden, width), lambda m: (0, m, 0, 0))
    part = pl.BlockSpec((1, hidden, width), lambda m: (m, 0, 0))
    flat = [value for own in parts for value in own]
    return pl.pallas_call(
        functools.partial(expert_update_kernel, len(parts[0])),
        grid=(2,),
        out_shape=[sds(weight.shape, f32)] * 4,
        in_specs=[block] * 3 + [part] * len(flat),
        out_specs=[block] * 4,
        compiler_params=params(60),
        cost_estimate=cost(4),
        name="expert_update",
    )(weight, first, second, *flat)


def swap(value, axis, size, bit):
    return lax.ppermute(value, axis, [(i, i ^ bit) for i in range(size)])


def ring_list(size):
    half = size // 2
    return [2 * i for i in range(half)] + [2 * i + 1 for i in reversed(range(half))]


def turn(value, size, by):
    order = ring_list(size)
    pairs = [(order[i], order[(i + by) % size]) for i in range(size)]
    return lax.ppermute(value, "rep", pairs)


def relay_kernel(*refs):
    pass


def tie(values, *others):
    values = list(values)
    return pl.pallas_call(
        relay_kernel,
        out_shape=[sds(value.shape, value.dtype) for value in values],
        in_specs=[ANY] * (len(values) + len(others)),
        out_specs=[ANY] * len(values),
        input_output_aliases={i: i for i in range(len(values))},
        compiler_params=params(1),
        cost_estimate=cost(0),
        name="relay",
    )(*values, *others)


def spread_far(value, size):
    held = {0: value}
    bit = size // 2
    while bit > 1:
        for k in list(held):
            held[k ^ bit] = swap(held[k], "shard", size, bit)
        bit //= 2
    return [held[k] for k in range(0, size, 2)]


def spread_near(values, size):
    both = [(value, swap(value, "shard", size, 1)) for value in values]
    return [value for pair in both for value in pair]


def ring_gather(value, size):
    half = size // 2
    held = [None] * size
    held[0] = value
    others = []
    ahead = behind = value
    for hop in range(1, half):
        if others:
            ahead, behind = tie([ahead, behind], *others)
            held[size - hop + 1], held[hop - 1] = ahead, behind
        ahead, behind = turn(ahead, size, 1), turn(behind, size, -1)
        held[size - hop], held[hop] = ahead, behind
        others = (yield [ahead, behind]) or []
    yield held


def ring_opposite(held, size, rows):
    half = size // 2
    result, opposite = [], []
    for e in range(held[0].shape[1]):
        last = [held[half + 1][0, e], held[half - 1][1, e]]
        opposite = [turn(last[0], size, 1), turn(last[1], size, -1)]
        result.append(held[:half] + opposite + held[half + 1 :])
    return result


def ring_add_kernel(ahead, first, behind, second, *refs):
    out_a, out_b = refs[-2:]
    if len(first.shape) == len(ahead.shape):
        out_a[...] = (ahead[...].astype(f32) + first[...].astype(f32)).astype(bf16)
        out_b[...] = (behind[...].astype(f32) + second[...].astype(f32)).astype(bf16)
    else:
        out_a[0] = (ahead[0].astype(f32) + first[...].astype(f32)).astype(bf16)
        out_a[1] = ahead[1]
        out_b[0] = behind[0]
        out_b[1] = (behind[1].astype(f32) + second[...].astype(f32)).astype(bf16)


def ring_add(ahead, first, behind, second, after):
    return pl.pallas_call(
        ring_add_kernel,
        out_shape=[sds(ahead.shape, bf16)] * 2,
        in_specs=[WHOLE] * 4 + [ANY] * len(after),
        out_specs=[WHOLE] * 2,
        compiler_params=params(16),
        cost_estimate=cost(0),
        name="ring_add",
    )(ahead, first, behind, second, *after)


def ring_sum(grads, size, formed):
    half = size // 2
    full = grads[:half] + [None] + grads[half + 2 :]
    sums = grads[half : half + 2]
    for hop in range(half, 0, -1):
        moving = [turn(sums[0], size, 1), turn(sums[1], size, -1)]
        if hop > 1:
            others = (yield moving) or []
            sums = ring_add(full[hop - 1], moving[0], full[size - hop + 1], moving[1], others)
            formed.extend(sums)
    yield [full[0]] + moving


def add(left, right):
    return (left.astype(f32) + right.astype(f32)).astype(bf16)


def shards(
    tokens,
    routes,
    cotangent,
    attn_weights,
    attn_first,
    attn_second,
    router_weights,
    router_first,
    router_second,
    norm_params,
    norm_first,
    norm_second,
    expert_weights,
    expert_first,
    expert_second,
    *,
    group,
    ring,
):
    tok_count, width = tokens.shape
    experts = router_weights.shape[1]
    local = expert_weights.shape[0]
    capacity = min(tok_count, (tok_count * 8 // (3 * experts) + 7) // 8 * 8)
    stride = -(-(capacity + 8) // 16) * 16
    images = tok_count // SEQ
    me = lax.axis_index("shard").astype(jnp.int32).reshape(1)

    packed, low = pack(attn_weights, router_weights.T, norm_params, expert_weights)
    gathering = ring_gather(low, ring)
    hop = next(gathering)
    pieces = spread_far(packed, group)
    x, cot, pos = stage(me, tokens, cotangent, routes, packed, images, local, group, stride)

    second = next(gathering)
    cots = spread_far(cot, group)
    pieces = spread_near(tie(pieces, pos), group)
    c, *saved = front(me, x, cot, pieces, experts, hop)
    c = tie([c], *second)[0]

    cs = spread_far(c, group)
    gathering.send([c])
    cots = tie(cots, c)
    cot = cots[0]
    cot_slots, places = gather_grads(me, spread_near(cots, group), local, stride)
    cs = spread_near(tie(cs, places), group)
    held = list(gathering)[-1]
    rows, outs = gather_rows(places, cot_slots, cs)
    shards = ring_opposite(held, ring, rows)

    back, made, summing, formed = [], [], [], []
    after, latest = [], []

    def send_back(blocks):
        return [v if k == 0 else swap(v, "shard", group, k) for k, v in enumerate(blocks)]

    def start_sum(grads):
        formed.append([])
        summing.append(ring_sum(list(grads), ring, formed[-1]))
        latest.append(next(summing[-1]))

    def next_hop(at, others):
        latest[at] = summing[at].send(others)

    for e in range(local - 1):
        out = run_whole(e, rows, outs, shards[e], group)
        back += send_back(out[:group])
        made += out[group : 2 * group]
        start_sum(out[2 * group :])
        after = [out[2 * group]]
    early = list(back)
    out = run_first(local - 1, rows, outs, shards[-1], group, after)
    back += send_back(out[:group])
    kept = out[group:]
    for at in range(len(summing)):
        next_hop(at, [out[0]])
    after = early + [value for own in formed for value in own[-2:]]
    out = run_last(local - 1, rows, outs, kept, shards[-1], after, group)
    grads = out[group:]
    made = [v for at in range(0, len(made), group) for v in send_back(made[at : at + group])]
    for at in range(len(summing)):
        next_hop(at, [grads[0]])
    start_sum(grads)
    after = [grads[0]] + [value for own in formed for value in own[-2:]]

    grad, carried = None, None
    for start in range(0, images, GROUP):
        closing = start + GROUP >= images
        grad, *carried = home(
            me, pos, cot, x, saved, pieces, back, after, carried, start, closing, experts
        )
        if start == 0:
            gate = carried[1]
            carried.append(grad)
            for at in range(local):
                next_hop(at, [gate])
            after = [part for own in formed for part in own[-2:]] + made
            made = made + send_back(tie(out[:group], gate))
    keep, send = carried
    send = tie([send], *made, *latest[-1][-2:])[0]

    total = add(keep, swap(send, "shard", group, 1))
    next_hop(-1, [total])
    total = tie([total], *formed[-1][-2:])[0]
    bit = 2
    while bit < group:
        count = total.shape[0] // 2
        pairs = total.reshape(count, 2, *total.shape[1:])
        total = add(pairs[:, 0], swap(pairs[:, 1], "shard", group, bit))
        bit *= 2
    total = total[0]

    total = tie([total], *latest[-1][-2:])[0]
    side = lax.axis_index("rep") % 2
    count = total.shape[0] // 2
    own = lax.dynamic_slice_in_dim(total, side * count, count)
    other = lax.dynamic_slice_in_dim(total, (1 - side) * count, count)
    total = add(own, swap(other, "rep", ring, 1))
    bit = 2
    while bit < ring:
        total = add(total, swap(total, "rep", ring, bit))
        if bit == 2:
            next_hop(-1, [total])
            output = finish(pos, saved, made, [total])
        bit *= 2
    total = tie([total], *latest[-1][-2:])[0]
    for at in range(local):
        for latest[at] in summing[at]:
            pass
    halves = [total, swap(total, "rep", ring, 1)]
    dense = dense_update(
        side.astype(jnp.int32).reshape(1),
        halves,
        (attn_weights, attn_first, attn_second),
        (router_weights.T, router_first.T, router_second.T),
        (norm_params, norm_first, norm_second),
    )
    dense = [value.T if 4 <= i < 8 else value for i, value in enumerate(dense)]
    updated = expert_update(latest, expert_weights, expert_first, expert_second)

    def unpadded(rows):
        return rows[:, :SEQ].reshape(tok_count, width)

    return (unpadded(output), unpadded(grad), *dense, *updated)


def solution(mesh):
    rows = P(("shard", "rep"), None)
    attn = P(None, "shard", None)
    router = P("shard", None)
    norm = P(None, "shard")
    expert = P("shard", None, "rep", None)
    return jax.shard_map(
        functools.partial(shards, group=mesh.shape["shard"], ring=mesh.shape["rep"]),
        mesh=mesh,
        in_specs=(rows,) * 3 + (attn,) * 3 + (router,) * 3 + (norm,) * 3 + (expert,) * 3,
        out_specs=(rows,) * 2 + (attn,) * 4 + (router,) * 4 + (norm,) * 4 + (expert,) * 4,
        check_vma=False,
    )
```
